32 devices in a mesh: dp: 4 (over x, core), seq: 8 (over z, y).
Axes of the slice: x: 2, y: 2, z: 4, core: 2. Of those that a mesh axis runs over, the one named last changes fastest.
Arguments:
- patches: bfloat16 [50176, 768], P(('dp', 'seq')), may hold values from -6 to 6
- keep_index: int32 [1024, 49], P('dp'), may hold values from 0 to 195, as said below
- ln1_gain: float32 [768], replicated, may hold values from 0.25 to 1.75
- ln1_shift: float32 [768], replicated, may hold values from -1.75 to 1.75
- w_qkv: bfloat16 [768, 2304], replicated, may hold values from -0.21875 to 0.21875
- q_bias: float32 [768], replicated, may hold values from -3 to 3
- v_bias: float32 [768], replicated, may hold values from -3 to 3
- w_out: bfloat16 [768, 768], replicated, may hold values from -0.875 to 0.875
- out_bias: float32 [768], replicated, may hold values from -1.75 to 1.75
- ln2_gain: float32 [768], replicated, may hold values from 0.25 to 1.75
- ln2_shift: float32 [768], replicated, may hold values from -1.75 to 1.75
- w_fc1: bfloat16 [768, 3072], replicated, may hold values from -0.21875 to 0.21875
- fc1_bias: float32 [3072], replicated, may hold values from -3 to 3
- w_fc2: bfloat16 [3072, 768], replicated, may hold values from -0.109375 to 0.109375
- fc2_bias: float32 [768], replicated, may hold values from -1.75 to 1.75
- w_embed: bfloat16 [768, 512], replicated, may hold values from -0.21875 to 0.21875
- embed_bias: float32 [512], replicated, may hold values from -1.75 to 1.75
- mask_token: float32 [512], replicated, may hold values from -6 to 6
- decoder_grad: bfloat16 [200704, 512], P(('dp', 'seq')), may hold values from -6 to 6
Outputs:
- decoder_input: bfloat16 [200704, 512], P(('dp', 'seq'))
- patches_grad: bfloat16 [50176, 768], P(('dp', 'seq'))
- ln1_gain_grad: float32 [768], P('seq')
- ln1_shift_grad: float32 [768], P('seq')
- w_qkv_grad: float32 [768, 2304], P('seq')
- q_bias_grad: float32 [768], P('seq')
- v_bias_grad: float32 [768], P('seq')
- w_out_grad: float32 [768, 768], P('seq')
- out_bias_grad: float32 [768], P('seq')
- ln2_gain_grad: float32 [768], P('seq')
- ln2_shift_grad: float32 [768], P('seq')
- w_fc1_grad: float32 [768, 3072], P('seq')
- fc1_bias_grad: float32 [3072], P('seq')
- w_fc2_grad: float32 [3072, 768], P('seq')
- fc2_bias_grad: float32 [768], P('seq')
- w_embed_grad: float32 [768, 512], P('seq')
- embed_bias_grad: float32 [512], P('seq')
- mask_token_grad: float32 [512], P('seq')
The draws below stay inside these ranges and needn't reach their ends.
Inputs may be any that keep to these rules, and one draw needn't show every extreme that they name: `keep_index`: each image's 49 kept positions are distinct and ascending. In a group, decoder device s holds rows s * 32 * 196 up to (s + 1) * 32 * 196 of the group's (position * 256 + image) rows. Of one image, at most 12 kept positions fall on one decoder device and at least one on each; in each group one decoder device gets exactly 12 from every image of the group.
All inputs are finite; a program needn't handle non-finite values.
Results may differ from the reference program's by a relative error of at most 0.019.
Values may be sent and summed in bfloat16 or wider, within the bound.
A program may use at most 256 MiB of HBM per device.

```python
import jax
import jax.numpy as jnp
from jax import lax

D = 768
HEADS = 12
HEAD = 64
FF = 3072
DEC = 512
PATCHES = 196
KEEP = 49
IMG_DEV = 32
SLOTS = 12
IMG_GRP = 256
IMAGES = 1024
VISIBLE = 50176
DEC_ROWS = 200704


def draw_keep_index(key, part):
    key = jax.random.fold_in(key, 11)
    seq_count = IMG_GRP // IMG_DEV
    focus_key, coarse_key, fine_key = jax.random.split(key, 3)
    group_count = IMAGES // IMG_GRP
    focus_dev = jax.random.randint(focus_key, (group_count,), 0, seq_count).astype(jnp.int32)
    image_ids = jnp.arange(IMAGES, dtype=jnp.int32)
    local_ids = image_ids % IMG_GRP
    places = jnp.arange(PATCHES, dtype=jnp.int32)
    owner_ids = (places[None, :] * IMG_GRP + local_ids[:, None]) // (IMG_DEV * PATCHES)
    coarse = jax.random.randint(coarse_key, (IMAGES, (PATCHES + 6) // 7), 0, 8).astype(jnp.int32)
    coarse_full = jnp.repeat(coarse, 7, axis=1)[:, :PATCHES]
    fine_part = jax.vmap(lambda sub_key: jax.random.permutation(sub_key, PATCHES))(jax.random.split(fine_key, IMAGES)).astype(jnp.int32)
    pos_score = coarse_full * 256 + fine_part
    same_owner = owner_ids[:, :, None] == owner_ids[:, None, :]
    higher = pos_score[:, None, :] > pos_score[:, :, None]
    inner_rank = jnp.sum((same_owner & higher).astype(jnp.int32), axis=2)
    eligible = inner_rank < SLOTS
    group_focus = focus_dev[image_ids // IMG_GRP]
    extra_pts = jnp.where(eligible & (owner_ids == group_focus[:, None]), 1 << 20, 0) + jnp.where(inner_rank == 0, 1 << 16, 0)
    priority = jnp.where(eligible, pos_score + extra_pts, -1 - places[None, :])
    outrank = jnp.sum((priority[:, None, :] > priority[:, :, None]).astype(jnp.int32), axis=2)
    chosen = outrank < KEEP
    order_idx = jnp.cumsum(chosen.astype(jnp.int32), axis=1) - 1
    slot_pos = jnp.where(chosen, order_idx, KEEP)
    result = jnp.zeros((IMAGES, KEEP), jnp.int32).at[image_ids[:, None], slot_pos].set(jnp.broadcast_to(places[None, :], (IMAGES, PATCHES)), mode='drop')
    return result


def spiked(entries, key, source, target, parts, factor):
    def block_of(axis_at):
        return (jnp.arange(entries.shape[axis_at]) // (entries.shape[axis_at] // parts)).reshape((-1,) + (1,) * (entries.ndim - 1 - axis_at))

    one_side = jax.random.permutation(key, parts)[block_of(target)]
    second = (block_of(target) + parts // 2) % parts
    return jnp.where((block_of(source) == one_side) | (block_of(source) == second), factor * entries, entries)


def block_scale(stream_key, extent, pieces, least, largest):
    factor_of = 1.0
    for dim, shards_of in pieces:
        heights = jax.random.uniform(jax.random.fold_in(jax.random.fold_in(stream_key, 6), dim), (shards_of,), jnp.float32, least / len(pieces), largest / len(pieces))
        factor_of = factor_of * jnp.repeat(jnp.exp(heights), extent[dim] // shards_of).reshape((-1,) + (1,) * (len(extent) - 1 - dim))
    return factor_of


def scatter_about(stream_key, dims, deviation, bound, cuts=(), kind=jnp.bfloat16):
    drawn = deviation * jax.random.normal(stream_key, dims, jnp.float32)
    if cuts:
        drawn = drawn * block_scale(stream_key, dims, cuts, -0.22, 0.18)
    return jnp.clip(drawn, -bound, bound).astype(kind)


def noise_with(rng, dims, spread, bound, shards, heavy, kind=jnp.bfloat16):
    entries = spread * jax.random.normal(rng, dims, jnp.float32)
    if shards:
        entries = entries * block_scale(rng, dims, shards, -0.22, 0.18)
    return jnp.clip(spiked(entries, jax.random.fold_in(rng, 3), *heavy), -bound, bound).astype(kind)


def setup_inputs(seed: int = 0) -> dict:
    seeds = jax.random.split(jax.random.key(seed), 20)
    patches = scatter_about(seeds[0], (VISIBLE, D), 1.0, 6.0, ((0, 32),))
    keep_index = draw_keep_index(jax.random.fold_in(seeds[19], 71), 0)
    ln1_gain = jnp.clip(1.0 + 0.15 * jax.random.normal(seeds[2], (D,), jnp.float32), 0.25, 1.75)
    ln1_shift = scatter_about(seeds[3], (D,), 0.3, 1.75, (), jnp.float32)
    w_qkv = scatter_about(seeds[4], (D, 3 * D), D ** -0.5, 0.21875)
    q_bias = scatter_about(seeds[5], (D,), 0.5, 3.0, (), jnp.float32)
    v_bias = scatter_about(seeds[6], (D,), 0.5, 3.0, (), jnp.float32)
    w_out = scatter_about(seeds[7], (D, D), (D // 16) ** -0.5, 0.875)
    out_bias = scatter_about(seeds[8], (D,), 0.3, 1.75, (), jnp.float32)
    ln2_gain = jnp.clip(1.0 + 0.15 * jax.random.normal(seeds[9], (D,), jnp.float32), 0.25, 1.75)
    ln2_shift = scatter_about(seeds[10], (D,), 0.3, 1.75, (), jnp.float32)
    w_fc1 = scatter_about(seeds[11], (D, FF), D ** -0.5, 0.21875)
    fc1_bias = scatter_about(seeds[12], (FF,), 0.5, 3.0, (), jnp.float32)
    w_fc2 = scatter_about(seeds[13], (FF, D), FF ** -0.5, 0.109375)
    fc2_bias = scatter_about(seeds[14], (D,), 0.3, 1.75, (), jnp.float32)
    w_embed = scatter_about(seeds[15], (D, DEC), D ** -0.5, 0.21875)
    embed_bias = scatter_about(seeds[16], (DEC,), 0.3, 1.75, (), jnp.float32)
    mask_token = scatter_about(seeds[17], (DEC,), 1.0, 6.0, (), jnp.float32)
    decoder_grad = noise_with(seeds[18], (DEC_ROWS, DEC), 1.0, 6.0, ((0, 32),), (0, 1, 32, 2.75))
    return {"patches": patches, "keep_index": keep_index, "ln1_gain": ln1_gain, "ln1_shift": ln1_shift, "w_qkv": w_qkv, "q_bias": q_bias, "v_bias": v_bias, "w_out": w_out, "out_bias": out_bias, "ln2_gain": ln2_gain, "ln2_shift": ln2_shift, "w_fc1": w_fc1, "fc1_bias": fc1_bias, "w_fc2": w_fc2, "fc2_bias": fc2_bias, "w_embed": w_embed, "embed_bias": embed_bias, "mask_token": mask_token, "decoder_grad": decoder_grad}


@jax.custom_vjp
def low(v):
    return lax.optimization_barrier(v.astype(jnp.bfloat16)).astype(jnp.float32)

@jax.custom_vjp
def low_back(v):
    return v

def low_keep(v):
    return (low(v), None)

def low_pass(kept, grad):
    return (grad,)

def back_keep(v):
    return (v, None)

def back_low(kept, grad):
    return (low(grad),)
low.defvjp(low_keep, low_pass)
low_back.defvjp(back_keep, back_low)
EPSILON = 1e-06
HIGHEST = lax.Precision.HIGHEST

def matmul_hi(left, right):
    return jnp.dot(left, right, precision=HIGHEST, preferred_element_type=jnp.float32)

def layer_norm(values, gain_vec, shift_vec):
    row_mean = lax.optimization_barrier(jnp.mean(values, axis=-1, keepdims=True))
    centered = values - row_mean
    row_var = lax.optimization_barrier(jnp.mean(centered * centered, axis=-1, keepdims=True))
    return centered * lax.rsqrt(row_var + EPSILON) * gain_vec + shift_vec

def gelu_exact(values):
    return jax.nn.gelu(values, approximate=False)

def encode(tok_rows, layer_params):
    ln1_gain, ln1_shift, w_qkv, q_bias, v_bias, w_out, out_bias, ln2_gain, ln2_shift, w_fc1, fc1_bias, w_fc2, fc2_bias, w_embed, embed_bias = layer_params
    images_in = tok_rows.shape[0] // KEEP
    first_in = low(layer_norm(tok_rows, ln1_gain, ln1_shift))
    qkv_bias = jnp.concatenate([q_bias, jnp.zeros_like(q_bias), v_bias])
    qkv_rows = low_back(low(matmul_hi(first_in, w_qkv) + qkv_bias))
    qkv_heads = qkv_rows.reshape(images_in, KEEP, 3, HEADS, HEAD)
    scale_qk = HEAD ** (-0.5)
    scores = low_back(jnp.einsum('bqhd,bkhd->bhqk', qkv_heads[:, :, 0], qkv_heads[:, :, 1], precision=HIGHEST) * scale_qk)
    attn_probs = low(jax.nn.softmax(scores, axis=-1))
    attended = jnp.einsum('bhqk,bkhd->bqhd', attn_probs, qkv_heads[:, :, 2], precision=HIGHEST)
    attended = low_back(low(attended.reshape(images_in * KEEP, HEADS * HEAD)))
    hidden = tok_rows + low_back(matmul_hi(attended, w_out) + out_bias)
    second = low(layer_norm(hidden, ln2_gain, ln2_shift))
    inner_pre = low_back(matmul_hi(second, w_fc1) + fc1_bias)
    active = low(gelu_exact(inner_pre))
    block_out = hidden + low_back(matmul_hi(active, w_fc2) + fc2_bias)
    embedded = matmul_hi(low(block_out), w_embed) + embed_bias
    return low_back(low(embedded))

def reference(patches, keep_index, ln1_gain, ln1_shift, w_qkv, q_bias, v_bias, w_out, out_bias, ln2_gain, ln2_shift, w_fc1, fc1_bias, w_fc2, fc2_bias, w_embed, embed_bias, mask_token, decoder_grad):
    image_ids = jnp.arange(IMAGES, dtype=jnp.int32)[:, None]
    targets = ((image_ids // IMG_GRP * PATCHES + keep_index) * IMG_GRP + image_ids % IMG_GRP).reshape(-1).astype(jnp.int32)
    block_imgs = 4 * IMG_DEV

    def forward(tok_rows, *params):
        layer_params = params[:-1]

        def run_block(block_rows):
            return encode(block_rows, layer_params)
        blocks = tok_rows.reshape(IMAGES // block_imgs, block_imgs * KEEP, D)
        embedded = lax.map(jax.checkpoint(run_block), blocks).reshape(IMAGES * KEEP, DEC)
        filled = jnp.broadcast_to(params[-1], (DEC_ROWS, DEC))
        return filled.at[targets].set(embedded)
    floats = [arg.astype(jnp.float32) for arg in (ln1_gain, ln1_shift, w_qkv, q_bias, v_bias, w_out, out_bias, ln2_gain, ln2_shift, w_fc1, fc1_bias, w_fc2, fc2_bias, w_embed, embed_bias, mask_token)]
    decoded, pull_back = jax.vjp(forward, patches.astype(jnp.float32), *floats)
    gradients = pull_back(decoder_grad.astype(jnp.float32))
    return (decoded.astype(jnp.bfloat16), gradients[0].astype(jnp.bfloat16), gradients[1], gradients[2], gradients[3], gradients[4], gradients[5], gradients[6], gradients[7], gradients[8], gradients[9], gradients[10], gradients[11], gradients[12], gradients[13], gradients[14], gradients[15], gradients[16])
```

```python
import functools
import math

import jax
import jax.numpy as jnp
from jax import lax
from jax.experimental import pallas as pl
from jax.experimental.pallas import tpu as pltpu
from jax.sharding import PartitionSpec as P

D = 768
HEADS = 12
HEAD = 64
FF = 3072
DEC = 512
PATCHES = 196
KEEP = 49
IMG = 32
HALF = 16
ROWS = IMG * KEEP
HROWS = HALF * KEEP
PADK = 64
UNITS = 3
EPSILON = 1e-06
BF = jnp.bfloat16
F32 = jnp.float32
MIB = 1 << 20

NN = (((1,), (0,)), ((), ()))
NT = (((1,), (1,)), ((), ()))
TN = (((0,), (0,)), ((), ()))


def dot(left, right, dims=NN):
    return lax.dot_general(left, right, dims, preferred_element_type=F32)


def params(mib=60):
    return pltpu.CompilerParams(vmem_limit_bytes=mib * MIB)


def whole(shape):
    return pl.BlockSpec(shape, lambda *_: (0,) * len(shape), pipeline_mode=pl.Buffered(1))


def norm(values):
    centered = values - jnp.mean(values, axis=-1, keepdims=True)
    inv = lax.rsqrt(jnp.mean(centered * centered, axis=-1, keepdims=True) + EPSILON)
    return centered * inv, inv


def norm_back(unit, inv, grad, gain):
    f = grad * gain
    return inv * (
        f
        - jnp.mean(f, axis=-1, keepdims=True)
        - unit * jnp.mean(f * unit, axis=-1, keepdims=True)
    )


def col_sum(values):
    return jnp.sum(values, axis=0, keepdims=True)


def gelu_pair(v):
    z = jnp.abs(v) * (1 / math.sqrt(2.0))
    t = 1.0 / (1.0 + 0.3275911 * z)
    e = jnp.exp(-z * z)
    poly = t * (
        0.5 * 0.254829592
        + t
        * (
            0.5 * -0.284496736
            + t * (0.5 * 1.421413741 + t * (0.5 * -1.453152027 + t * (0.5 * 1.061405429)))
        )
    )
    tail = poly * e
    cdf = jnp.where(v >= 0, 1.0 - tail, tail)
    return v * cdf, cdf + v * (e * (1 / math.sqrt(2 * math.pi)))


def one_hot(rows, code):
    at = lax.broadcasted_iota(jnp.int32, (rows, code.shape[1]), 0)
    return jnp.where(at == code, 1.0, 0.0).astype(BF)


def owner_blocks(seq_count):
    dev_blocks = PATCHES
    most = -(-dev_blocks // seq_count)
    return dev_blocks, most, -(-most // 4) * 4


def first_block(seq_count, t):
    return lax.rem(
        t + seq_count - lax.rem(lax.axis_index("seq") * PATCHES, seq_count), seq_count
    )


def pick_kernel(seq_count, slots, code_ref, dec_ref, out_ref, sum_ref):
    t = pl.program_id(0)
    dev_blocks, most, padded = owner_blocks(seq_count)
    start = first_block(seq_count, t)
    pieces = []
    for m in range(most):
        at = start + m * seq_count
        clamped = jnp.minimum(at, dev_blocks - 1)
        pieces.append(dec_ref[pl.ds(pl.multiple_of(clamped * IMG, IMG), IMG), :])
    if padded > most:
        pieces.append(jnp.zeros(((padded - most) * IMG, DEC), BF))
    picked = dot(one_hot(slots * IMG + 16, code_ref[0]), jnp.concatenate(pieces, axis=0))
    out_ref[...] = picked[: slots * IMG].astype(BF).reshape(slots, IMG, DEC)

    @pl.when(t == 0)
    def _():
        sum_ref[...] = jnp.zeros_like(sum_ref)

    sum_ref[...] += picked[slots * IMG : slots * IMG + 8]


def pick(seq_count, slots, code, dec_grad):
    return pl.pallas_call(
        functools.partial(pick_kernel, seq_count, slots),
        grid=(seq_count,),
        in_specs=[
            pl.BlockSpec((1, 1, code.shape[2]), lambda t: (t, 0, 0)),
            whole(dec_grad.shape),
        ],
        out_specs=[
            pl.BlockSpec((slots, IMG, DEC), lambda t: (t, 0, 0)),
            pl.BlockSpec((8, DEC), lambda t: (0, 0)),
        ],
        out_shape=[
            jax.ShapeDtypeStruct((seq_count * slots, IMG, DEC), BF),
            jax.ShapeDtypeStruct((8, DEC), F32),
        ],
        compiler_params=params(),
        name="pick",
    )(code, dec_grad)


def place_kernel(seq_count, slots, code_ref, arrived_ref, mask_ref, out_ref):
    t = pl.program_id(0)
    dev_blocks, most, padded = owner_blocks(seq_count)
    start = first_block(seq_count, t)
    fill = jnp.where(
        lax.broadcasted_iota(jnp.int32, (16, DEC), 0) == 0, mask_ref[...], 0.0
    ).astype(BF)
    source = jnp.concatenate([arrived_ref[...].reshape(slots * IMG, DEC), fill], axis=0)
    spread = dot(one_hot(slots * IMG + 16, code_ref[0]), source, TN).astype(BF)
    for m in range(most):
        at = start + m * seq_count
        piece = spread[m * IMG : (m + 1) * IMG]
        if (m + 1) * seq_count <= dev_blocks:
            out_ref[pl.ds(pl.multiple_of(at * IMG, IMG), IMG), :] = piece
        else:

            @pl.when(at < dev_blocks)
            def _():
                out_ref[pl.ds(pl.multiple_of(at * IMG, IMG), IMG), :] = piece


def place(seq_count, slots, code, arrived, mask_token):
    return pl.pallas_call(
        functools.partial(place_kernel, seq_count, slots),
        grid=(seq_count,),
        in_specs=[
            pl.BlockSpec((1, 1, code.shape[2]), lambda t: (t, 0, 0)),
            pl.BlockSpec((slots, IMG, DEC), lambda t: (t, 0, 0)),
            whole((1, DEC)),
        ],
        out_specs=whole((PATCHES * IMG, DEC)),
        out_shape=jax.ShapeDtypeStruct((PATCHES * IMG, DEC), BF),
        compiler_params=params(),
        name="place",
    )(code, arrived, mask_token)


def pack_kernel(code_ref, rows_ref, out_ref):
    count = out_ref.shape[0]
    picked = dot(one_hot(count * HALF, code_ref[0]), rows_ref[...])
    out_ref[...] = picked.astype(BF).reshape(count, HALF, DEC)


def pack(code, rows, count):
    return pl.pallas_call(
        pack_kernel,
        grid=(2,),
        in_specs=[
            pl.BlockSpec((1, 1, HROWS), lambda g: (g, 0, 0)),
            pl.BlockSpec((HROWS, DEC), lambda g: (g, 0)),
        ],
        out_specs=pl.BlockSpec((count, HALF, DEC), lambda g: (0, g, 0)),
        out_shape=jax.ShapeDtypeStruct((count, IMG, DEC), BF),
        compiler_params=params(),
        name="pack",
    )(code, rows)


def unpack_kernel(code_ref, slots_ref, out_ref):
    count = slots_ref.shape[0]
    source = slots_ref[...].reshape(count * HALF, DEC)
    out_ref[...] = dot(one_hot(count * HALF, code_ref[0]), source, TN).astype(BF)


def unpack(code, slots):
    count = slots.shape[0]
    return pl.pallas_call(
        unpack_kernel,
        grid=(2,),
        in_specs=[
            pl.BlockSpec((1, 1, HROWS), lambda g: (g, 0, 0)),
            pl.BlockSpec((count, HALF, DEC), lambda g: (0, g, 0)),
        ],
        out_specs=pl.BlockSpec((HROWS, DEC), lambda g: (g, 0)),
        out_shape=jax.ShapeDtypeStruct((ROWS, DEC), BF),
        compiler_params=params(),
        name="unpack",
    )(code, slots)


UNIT = 4 * HEAD


def block_diag(rows):
    lane_head = lax.broadcasted_iota(jnp.int32, rows.shape, 1) // HEAD
    zero = jnp.zeros_like(rows)
    return jnp.concatenate([jnp.where(lane_head == h, rows, zero) for h in range(4)], axis=0)


def fold_heads(left, right):
    low = lax.broadcasted_iota(jnp.int32, (PADK, 2 * HEAD), 1) < HEAD
    return jnp.concatenate(
        [
            jnp.where(low, left[:PADK], left[PADK:]),
            jnp.where(low, right[:PADK], right[PADK:]),
        ],
        axis=1,
    )


def soft_cols(key, query_diag):
    scores = dot(key, query_diag, NT)
    valid = lax.broadcasted_iota(jnp.int32, scores.shape, 0) < KEEP
    scores = jnp.where(valid, scores, -1e30)
    e = jnp.exp(scores - jnp.max(scores, axis=0, keepdims=True))
    return e * (1.0 / jnp.sum(e, axis=0, keepdims=True))


def each_image(image, *refs):
    def group(g, carry):
        base = pl.multiple_of(g * 8 * KEEP, 8)
        views = [ref.at[pl.ds(base, 8 * KEEP + 16)] for ref in refs]
        for near in range(8):
            image(g * 8 + near, near, *views)
        return carry

    lax.fori_loop(0, HALF // 8, group, 0)


def attn_fwd_kernel(
    x_ref, gain_ref, shift_ref, wqkv_ref, bias_ref, wout_ref, obias_ref,
    qkvp_ref, att_ref, hidden_ref, qs, ats,
):
    x = x_ref[...].astype(F32)
    unit, _ = norm(x)
    first = (unit * gain_ref[...] + shift_ref[...]).astype(BF)
    for c in range(3):
        cols = slice(c * D, (c + 1) * D)
        qs[:HROWS, cols] = (
            (dot(first, wqkv_ref[:, cols]) + bias_ref[:, cols]).astype(BF).astype(F32)
        )
    qs[HROWS:, :] = jnp.zeros((16, 3 * D), F32)

    def image(i, near, qs, ats):
        r0 = near * KEEP
        for u in range(UNITS):
            part = []
            for c in range(3):
                cols = slice(c * D + u * UNIT, c * D + (u + 1) * UNIT)
                rows = qs[r0 : r0 + PADK, cols].astype(BF)
                qkvp_ref[i, :, cols] = rows
                part.append(rows)
            q, k, v = part
            probs = soft_cols(k, block_diag(q * BF(0.125))).astype(BF)
            out = fold_heads(
                dot(probs[:, :128], v[:, :128], TN), dot(probs[:, 128:], v[:, 128:], TN)
            )
            ats[r0 : r0 + 56, u * UNIT : (u + 1) * UNIT] = out[:56]

    each_image(image, qs, ats)
    att = ats[:HROWS, :].astype(BF)
    att_ref[...] = att
    hidden_ref[...] = x_ref[...].astype(F32) + (dot(att, wout_ref[...]) + obias_ref[...])


def attn_fwd(x, gain, shift, wqkv, bias, wout, obias):
    return pl.pallas_call(
        attn_fwd_kernel,
        grid=(2,),
        in_specs=[
            pl.BlockSpec((HROWS, D), lambda g: (g, 0)),
            whole((1, D)),
            whole((1, D)),
            whole((D, 3 * D)),
            whole((1, 3 * D)),
            whole((D, D)),
            whole((1, D)),
        ],
        out_specs=[
            pl.BlockSpec((HALF, PADK, 3 * D), lambda g: (g, 0, 0)),
            pl.BlockSpec((HROWS, D), lambda g: (g, 0)),
            pl.BlockSpec((HROWS, D), lambda g: (g, 0)),
        ],
        out_shape=[
            jax.ShapeDtypeStruct((IMG, PADK, 3 * D), BF),
            jax.ShapeDtypeStruct((ROWS, D), BF),
            jax.ShapeDtypeStruct((ROWS, D), F32),
        ],
        scratch_shapes=[pltpu.VMEM((HROWS + 16, 3 * D), F32), pltpu.VMEM((HROWS + 16, D), F32)],
        compiler_params=params(),
        name="attn_fwd",
    )(x, gain, shift, wqkv, bias, wout, obias)


def attn_bwd_kernel(
    hgrad_ref, att_ref, qkvp_ref, x_ref, gain_ref, shift_ref, wout_ref, wqkv_ref,
    pgrad_ref, wqkvg_ref, woutg_ref, obias_ref, qkvb_ref, lng_ref, lns_ref,
    ags, dqs, wqacc, woacc,
):
    g = pl.program_id(0)

    @pl.when(g == 0)
    def _():
        wqacc[...] = jnp.zeros_like(wqacc)
        woacc[...] = jnp.zeros_like(woacc)
        for ref in (obias_ref, qkvb_ref, lng_ref, lns_ref):
            ref[...] = jnp.zeros_like(ref)

    branch = hgrad_ref[...].astype(BF)
    obias_ref[...] += col_sum(branch.astype(F32))
    woacc[...] += dot(att_ref[...], branch, TN)
    ags[:HROWS, :] = dot(branch, wout_ref[...], NT)
    ags[HROWS:, :] = jnp.zeros((16, D), F32)

    def image(i, near, ags, dqs):
        r0 = near * KEEP
        valid = lax.broadcasted_iota(jnp.int32, (PADK, UNIT), 0) < KEEP
        for u in range(UNITS):
            q, k, v = (
                qkvp_ref[i, :, c * D + u * UNIT : c * D + (u + 1) * UNIT] for c in range(3)
            )
            q_diag = block_diag(q * BF(0.125))
            probs = soft_cols(k, q_diag)
            probs_in = probs.astype(BF)
            agrad = jnp.where(
                valid, ags[r0 : r0 + PADK, u * UNIT : (u + 1) * UNIT], 0.0
            ).astype(BF)
            a_diag = block_diag(agrad)
            pgrad = dot(v, a_diag, NT)
            vgrad = dot(probs_in, a_diag)
            inner = jnp.sum(probs * pgrad, axis=0, keepdims=True)
            sgrad = (probs * (pgrad - inner)).astype(BF)
            kgrad = dot(sgrad, q_diag)
            qgrad = 0.125 * fold_heads(
                dot(sgrad[:, :128], k[:, :128], TN), dot(sgrad[:, 128:], k[:, 128:], TN)
            )
            for c, grad in enumerate((qgrad, kgrad, vgrad)):
                dqs[r0 : r0 + 56, c * D + u * UNIT : c * D + (u + 1) * UNIT] = grad[:56]

    each_image(image, ags, dqs)
    unit, inv = norm(x_ref[...].astype(F32))
    first = (unit * gain_ref[...] + shift_ref[...]).astype(BF)
    fgrad = None
    for c in range(3):
        cols = slice(c * D, (c + 1) * D)
        grad = dqs[:HROWS, cols].astype(BF)
        qkvb_ref[:, cols] += col_sum(grad.astype(F32))
        wqacc[:, cols] += dot(first, grad, TN)
        term = dot(grad, wqkv_ref[:, cols], NT)
        fgrad = term if fgrad is None else fgrad + term
    lng_ref[...] += col_sum(fgrad * unit)
    lns_ref[...] += col_sum(fgrad)
    pgrad_ref[...] = (hgrad_ref[...] + norm_back(unit, inv, fgrad, gain_ref[...])).astype(BF)

    @pl.when(g == 1)
    def _():
        wqkvg_ref[...] = wqacc[...].astype(BF)
        woutg_ref[...] = woacc[...].astype(BF)


def attn_bwd(hgrad, att, qkvp, x, gain, shift, wout, wqkv):
    rows = pl.BlockSpec((HROWS, D), lambda g: (g, 0))
    return pl.pallas_call(
        attn_bwd_kernel,
        grid=(2,),
        in_specs=[
            rows,
            rows,
            pl.BlockSpec((HALF, PADK, 3 * D), lambda g: (g, 0, 0)),
            rows,
            whole((1, D)),
            whole((1, D)),
            whole((D, D)),
            whole((D, 3 * D)),
        ],
        out_specs=[
            rows,
            whole((D, 3 * D)),
            whole((D, D)),
            whole((1, D)),
            whole((1, 3 * D)),
            whole((1, D)),
            whole((1, D)),
        ],
        out_shape=[
            jax.ShapeDtypeStruct((ROWS, D), BF),
            jax.ShapeDtypeStruct((D, 3 * D), BF),
            jax.ShapeDtypeStruct((D, D), BF),
            jax.ShapeDtypeStruct((1, D), F32),
            jax.ShapeDtypeStruct((1, 3 * D), F32),
            jax.ShapeDtypeStruct((1, D), F32),
            jax.ShapeDtypeStruct((1, D), F32),
        ],
        scratch_shapes=[
            pltpu.VMEM((HROWS + 16, D), F32),
            pltpu.VMEM((HROWS + 16, 3 * D), F32),
            pltpu.VMEM((D, 3 * D), F32),
            pltpu.VMEM((D, D), F32),
        ],
        compiler_params=params(),
        name="attn_bwd",
    )(hgrad, att, qkvp, x, gain, shift, wout, wqkv)


FTILE = 512
FSTEPS = FF // FTILE


def mlp_fwd_kernel(
    hidden_ref, gain_ref, shift_ref, w1_ref, b1_ref, w2_ref, b2_ref, we_ref, be_ref,
    act_ref, slope_ref, block_ref, emb_ref, second, acc,
):
    f = pl.program_id(0)

    @pl.when(f == 0)
    def _():
        unit, _ = norm(hidden_ref[...])
        second[...] = (unit * gain_ref[...] + shift_ref[...]).astype(BF)
        acc[...] = hidden_ref[...] + b2_ref[...]

    for h in range(2):
        rows = slice(h * HROWS, (h + 1) * HROWS)
        active, slope = gelu_pair(dot(second[rows, :], w1_ref[...]) + b1_ref[...])
        active = active.astype(BF)
        act_ref[rows, :] = active
        slope_ref[rows, :] = slope.astype(BF)
        acc[rows, :] += dot(active, w2_ref[...])

    @pl.when(f == FSTEPS - 1)
    def _():
        block_in = acc[...].astype(BF)
        block_ref[...] = block_in
        emb_ref[...] = (dot(block_in, we_ref[...]) + be_ref[...]).astype(BF)


def mlp_fwd(hidden, gain, shift, w1, b1, w2, b2, we, be):
    tile = pl.BlockSpec((ROWS, FTILE), lambda f: (0, f))
    return pl.pallas_call(
        mlp_fwd_kernel,
        grid=(FSTEPS,),
        in_specs=[
            whole((ROWS, D)),
            whole((1, D)),
            whole((1, D)),
            pl.BlockSpec((D, FTILE), lambda f: (0, f)),
            pl.BlockSpec((1, FTILE), lambda f: (0, f)),
            pl.BlockSpec((FTILE, D), lambda f: (f, 0)),
            whole((1, D)),
            whole((D, DEC)),
            whole((1, DEC)),
        ],
        out_specs=[tile, tile, whole((ROWS, D)), whole((ROWS, DEC))],
        out_shape=[
            jax.ShapeDtypeStruct((ROWS, FF), BF),
            jax.ShapeDtypeStruct((ROWS, FF), BF),
            jax.ShapeDtypeStruct((ROWS, D), BF),
            jax.ShapeDtypeStruct((ROWS, DEC), BF),
        ],
        scratch_shapes=[pltpu.VMEM((ROWS, D), BF), pltpu.VMEM((ROWS, D), F32)],
        compiler_params=params(),
        name="mlp_fwd",
    )(hidden, gain, shift, w1, b1, w2, b2, we, be)


def mlp_bwd_kernel(
    egrad_ref, block_ref, hidden_ref, gain_ref, shift_ref, we_ref, act_ref, slope_ref, w2_ref, w1_ref,
    hgrad_ref, weg_ref, ebias_ref, w2g_ref, b2_ref, w1g_ref, b1_ref, lng_ref, lns_ref,
    two, second, acc,
):
    f = pl.program_id(0)

    @pl.when(f == 0)
    def _():
        egrad = egrad_ref[...]
        weg_ref[...] = dot(block_ref[...], egrad, TN).astype(BF)
        ebias_ref[...] = col_sum(egrad.astype(F32))
        out_grad = dot(egrad, we_ref[...], NT)
        hgrad_ref[...] = out_grad
        two_grad = out_grad.astype(BF)
        two[...] = two_grad
        b2_ref[...] = col_sum(two_grad.astype(F32))
        unit, _ = norm(hidden_ref[...])
        second[...] = (unit * gain_ref[...] + shift_ref[...]).astype(BF)
        acc[...] = jnp.zeros_like(acc)

    w2g_ref[...] = dot(act_ref[...], two[...], TN).astype(BF)
    inner = (dot(two[...], w2_ref[...], NT) * slope_ref[...].astype(F32)).astype(BF)
    b1_ref[...] = col_sum(inner.astype(F32))
    w1g_ref[...] = dot(second[...], inner, TN).astype(BF)
    acc[...] += dot(inner, w1_ref[...], NT)

    @pl.when(f == FSTEPS - 1)
    def _():
        unit, inv = norm(hidden_ref[...])
        grad = acc[...]
        lng_ref[...] = col_sum(grad * unit)
        lns_ref[...] = col_sum(grad)
        hgrad_ref[...] += norm_back(unit, inv, grad, gain_ref[...])


def mlp_bwd(egrad, block_in, hidden, gain, shift, we, act, slope, w2, w1):
    tile = pl.BlockSpec((ROWS, FTILE), lambda f: (0, f))
    return pl.pallas_call(
        mlp_bwd_kernel,
        grid=(FSTEPS,),
        in_specs=[
            whole((ROWS, DEC)),
            whole((ROWS, D)),
            whole((ROWS, D)),
            whole((1, D)),
            whole((1, D)),
            whole((D, DEC)),
            tile,
            tile,
            pl.BlockSpec((FTILE, D), lambda f: (f, 0)),
            pl.BlockSpec((D, FTILE), lambda f: (0, f)),
        ],
        out_specs=[
            whole((ROWS, D)),
            whole((D, DEC)),
            whole((1, DEC)),
            pl.BlockSpec((FTILE, D), lambda f: (f, 0)),
            whole((1, D)),
            pl.BlockSpec((D, FTILE), lambda f: (0, f)),
            pl.BlockSpec((1, FTILE), lambda f: (0, f)),
            whole((1, D)),
            whole((1, D)),
        ],
        out_shape=[
            jax.ShapeDtypeStruct((ROWS, D), F32),
            jax.ShapeDtypeStruct((D, DEC), BF),
            jax.ShapeDtypeStruct((1, DEC), F32),
            jax.ShapeDtypeStruct((FF, D), BF),
            jax.ShapeDtypeStruct((1, D), F32),
            jax.ShapeDtypeStruct((D, FF), BF),
            jax.ShapeDtypeStruct((1, FF), F32),
            jax.ShapeDtypeStruct((1, D), F32),
            jax.ShapeDtypeStruct((1, D), F32),
        ],
        scratch_shapes=[
            pltpu.VMEM((ROWS, D), BF),
            pltpu.VMEM((ROWS, D), BF),
            pltpu.VMEM((ROWS, D), F32),
        ],
        compiler_params=params(),
        name="mlp_bwd",
    )(egrad, block_in, hidden, gain, shift, we, act, slope, w2, w1)


def decoder_codes(keep_index, slots):
    seq_count = lax.axis_size("seq")
    dev_blocks, _, padded = owner_blocks(seq_count)
    t = jnp.arange(seq_count, dtype=jnp.int32)
    start = first_block(seq_count, t)
    lowest = (lax.axis_index("seq") * PATCHES + start) // seq_count
    m = jnp.arange(padded, dtype=jnp.int32)
    valid = (start[:, None] + m[None, :] * seq_count) < dev_blocks
    place_at = (lowest[:, None] + m[None, :])[None, :, :, None]
    kept = keep_index.T.reshape(KEEP, seq_count, 1, IMG)
    hit = jnp.sum((kept == place_at).astype(jnp.int32), axis=0)
    below = (kept < place_at) & (kept >= lowest[None, :, None, None])
    rank = jnp.sum(below.astype(jnp.int32), axis=0)
    image = jnp.arange(IMG, dtype=jnp.int32)
    code = jnp.where(hit > 0, rank * IMG + image, slots * IMG)
    code = jnp.where(valid[:, :, None], code, -1)
    return code.reshape(seq_count, 1, padded * IMG)


def image_codes(keep_index, slots):
    seq_count = lax.axis_size("seq")
    group_imgs = keep_index.shape[0]
    at = lax.axis_index("seq") * IMG
    own = lax.dynamic_slice_in_dim(keep_index, at, IMG, 0)
    image = jnp.arange(IMG, dtype=jnp.int32)[:, None]
    owner = (own * group_imgs + at + image) // (IMG * PATCHES)
    lower = jnp.sum((owner[:, None, :] < owner[:, :, None]).astype(jnp.int32), axis=2)
    rank = jnp.arange(KEEP, dtype=jnp.int32)[None, :] - lower
    code = (owner * slots + rank) * HALF + image % HALF
    return code.reshape(2, 1, HROWS)


def local(
    patches,
    keep_index,
    ln1_gain,
    ln1_shift,
    w_qkv,
    q_bias,
    v_bias,
    w_out,
    out_bias,
    ln2_gain,
    ln2_shift,
    w_fc1,
    fc1_bias,
    w_fc2,
    fc2_bias,
    w_embed,
    embed_bias,
    mask_token,
    decoder_grad,
):
    seq_count = lax.axis_size("seq")
    slots = 2 * KEEP // seq_count
    row = lambda v: v.reshape(1, -1)
    dec_code = decoder_codes(keep_index, slots)
    img_code = image_codes(keep_index, slots)
    grad_slots, mask_rows = pick(seq_count, slots, dec_code, decoder_grad)
    returned = lax.all_to_all(grad_slots, "seq", split_axis=0, concat_axis=0, tiled=True)

    qkv_bias = jnp.concatenate([q_bias, jnp.zeros_like(q_bias), v_bias])
    qkvp, attended, hidden = attn_fwd(
        patches, row(ln1_gain), row(ln1_shift), w_qkv, row(qkv_bias), w_out, row(out_bias)
    )
    active, slope, block_in, embedded = mlp_fwd(
        hidden, row(ln2_gain), row(ln2_shift), w_fc1, row(fc1_bias), w_fc2, row(fc2_bias),
        w_embed, row(embed_bias),
    )
    send = pack(img_code, embedded, seq_count * slots)
    arrived = lax.all_to_all(send, "seq", split_axis=0, concat_axis=0, tiled=True)

    embed_grad = unpack(img_code, returned)
    hgrad, weg, ebias, w2g, b2, w1g, b1, ln2g, ln2s = mlp_bwd(
        embed_grad, block_in, hidden, row(ln2_gain), row(ln2_shift), w_embed, active, slope,
        w_fc2, w_fc1,
    )
    patches_grad, wqkvg, woutg, obias, qkvb, ln1g, ln1s = attn_bwd(
        hgrad, attended, qkvp, patches, row(ln1_gain), row(ln1_shift), w_out, w_qkv
    )
    decoder_input = place(seq_count, slots, dec_code, arrived, row(mask_token))

    shares = [
        lax.psum(lax.psum_scatter(v, "seq", scatter_dimension=0, tiled=True), "dp").astype(F32)
        for v in (weg, w2g, w1g, woutg, wqkvg)
    ]
    vectors = [
        ln1g, ln1s, qkvb[:, :D], qkvb[:, 2 * D :], obias, ln2g, ln2s, b1, b2, ebias, mask_rows[:1],
    ]
    packed = jnp.concatenate([v.reshape(seq_count, -1) for v in vectors], axis=1).astype(BF)
    small = lax.psum(
        lax.psum_scatter(packed, "seq", scatter_dimension=0, tiled=True), "dp"
    ).astype(F32).reshape(-1)
    parts, at = [], 0
    for v in vectors:
        size = v.shape[1] // seq_count
        parts.append(small[at : at + size])
        at += size
    ln1g, ln1s, qb, vb, obias, ln2g, ln2s, b1, b2, ebias, mask_grad = parts
    weg, w2g, w1g, woutg, wqkvg = shares
    return (
        decoder_input,
        patches_grad,
        ln1g,
        ln1s,
        wqkvg,
        qb,
        vb,
        woutg,
        obias,
        ln2g,
        ln2s,
        w1g,
        b1,
        w2g,
        b2,
        weg,
        ebias,
        mask_grad,
    )


def solution(mesh):
    rows = P(("dp", "seq"), None)
    placed = (rows, P("dp", None)) + (P(),) * 16 + (rows,)
    vec, mat = P("seq"), P("seq", None)
    return jax.shard_map(
        local,
        mesh=mesh,
        in_specs=placed,
        out_specs=(
            rows, rows, vec, vec, mat, vec, vec, mat, vec, vec, vec, mat, vec, mat, vec, mat, vec, vec,
        ),
        check_vma=False,
    )
```

```python
import functools
import math

import jax
import jax.numpy as jnp
from jax import lax
from jax.experimental import pallas as pl
from jax.experimental.pallas import tpu as pltpu
from jax.sharding import PartitionSpec as P

D = 768
HEADS = 12
HEAD = 64
FF = 3072
DEC = 512
PATCHES = 196
KEEP = 49
IMG = 32
HALF = 16
ROWS = IMG * KEEP
HROWS = HALF * KEEP
PADK = 64
UNITS = 3
EPSILON = 1e-06
BF = jnp.bfloat16
F32 = jnp.float32
MIB = 1 << 20

NN = (((1,), (0,)), ((), ()))
NT = (((1,), (1,)), ((), ()))
TN = (((0,), (0,)), ((), ()))


def dot(left, right, dims=NN):
    return lax.dot_general(left, right, dims, preferred_element_type=F32)


def params(mib=60):
    return pltpu.CompilerParams(vmem_limit_bytes=mib * MIB)


def whole(shape):
    return pl.BlockSpec(shape, lambda *_: (0,) * len(shape), pipeline_mode=pl.Buffered(1))


def norm(values):
    centered = values - jnp.mean(values, axis=-1, keepdims=True)
    inv = lax.rsqrt(jnp.mean(centered * centered, axis=-1, keepdims=True) + EPSILON)
    return centered * inv, inv


def norm_back(unit, inv, grad, gain):
    f = grad * gain
    return inv * (
        f
        - jnp.mean(f, axis=-1, keepdims=True)
        - unit * jnp.mean(f * unit, axis=-1, keepdims=True)
    )


def col_sum(values):
    return jnp.sum(values, axis=0, keepdims=True)


def gelu_pair(v):
    z = jnp.abs(v) * (1 / math.sqrt(2.0))
    t = 1.0 / (1.0 + 0.3275911 * z)
    e = jnp.exp(-z * z)
    poly = t * (
        0.5 * 0.254829592
        + t
        * (
            0.5 * -0.284496736
            + t * (0.5 * 1.421413741 + t * (0.5 * -1.453152027 + t * (0.5 * 1.061405429)))
        )
    )
    tail = poly * e
    cdf = jnp.where(v >= 0, 1.0 - tail, tail)
    return v * cdf, cdf + v * (e * (1 / math.sqrt(2 * math.pi)))


def one_hot(rows, code):
    at = lax.broadcasted_iota(jnp.int32, (rows, code.shape[1]), 0)
    return jnp.where(at == code, 1.0, 0.0).astype(BF)


def owner_blocks(seq_count):
    dev_blocks = PATCHES
    most = -(-dev_blocks // seq_count)
    return dev_blocks, most, -(-most // 4) * 4


def first_block(seq_count, t):
    return lax.rem(
        t + seq_count - lax.rem(lax.axis_index("seq") * PATCHES, seq_count), seq_count
    )


def pick_kernel(seq_count, slots, code_ref, dec_ref, out_ref, sum_ref):
    t = pl.program_id(0)
    dev_blocks, most, padded = owner_blocks(seq_count)
    start = first_block(seq_count, t)
    pieces = []
    for m in range(most):
        at = start + m * seq_count
        clamped = jnp.minimum(at, dev_blocks - 1)
        pieces.append(dec_ref[pl.ds(pl.multiple_of(clamped * IMG, IMG), IMG), :])
    if padded > most:
        pieces.append(jnp.zeros(((padded - most) * IMG, DEC), BF))
    picked = dot(one_hot(slots * IMG + 16, code_ref[0]), jnp.concatenate(pieces, axis=0))
    out_ref[...] = picked[: slots * IMG].astype(BF).reshape(slots, IMG, DEC)

    @pl.when(t == 0)
    def _():
        sum_ref[...] = jnp.zeros_like(sum_ref)

    sum_ref[...] += picked[slots * IMG : slots * IMG + 8]


def pick(seq_count, slots, code, dec_grad):
    return pl.pallas_call(
        functools.partial(pick_kernel, seq_count, slots),
        grid=(seq_count,),
        in_specs=[
            pl.BlockSpec((1, 1, code.shape[2]), lambda t: (t, 0, 0)),
            whole(dec_grad.shape),
        ],
        out_specs=[
            pl.BlockSpec((slots, IMG, DEC), lambda t: (t, 0, 0)),
            pl.BlockSpec((8, DEC), lambda t: (0, 0)),
        ],
        out_shape=[
            jax.ShapeDtypeStruct((seq_count * slots, IMG, DEC), BF),
            jax.ShapeDtypeStruct((8, DEC), F32),
        ],
        compiler_params=params(),
        name="pick",
    )(code, dec_grad)


def place_kernel(seq_count, slots, code_ref, arrived_ref, mask_ref, out_ref):
    t = pl.program_id(0)
    dev_blocks, most, padded = owner_blocks(seq_count)
    start = first_block(seq_count, t)
    fill = jnp.where(
        lax.broadcasted_iota(jnp.int32, (16, DEC), 0) == 0, mask_ref[...], 0.0
    ).astype(BF)
    source = jnp.concatenate([arrived_ref[...].reshape(slots * IMG, DEC), fill], axis=0)
    spread = dot(one_hot(slots * IMG + 16, code_ref[0]), source, TN).astype(BF)
    for m in range(most):
        at = start + m * seq_count
        piece = spread[m * IMG : (m + 1) * IMG]
        if (m + 1) * seq_count <= dev_blocks:
            out_ref[pl.ds(pl.multiple_of(at * IMG, IMG), IMG), :] = piece
        else:

            @pl.when(at < dev_blocks)
            def _():
                out_ref[pl.ds(pl.multiple_of(at * IMG, IMG), IMG), :] = piece


def place(seq_count, slots, code, arrived, mask_token):
    return pl.pallas_call(
        functools.partial(place_kernel, seq_count, slots),
        grid=(seq_count,),
        in_specs=[
            pl.BlockSpec((1, 1, code.shape[2]), lambda t: (t, 0, 0)),
            pl.BlockSpec((slots, IMG, DEC), lambda t: (t, 0, 0)),
            whole((1, DEC)),
        ],
        out_specs=whole((PATCHES * IMG, DEC)),
        out_shape=jax.ShapeDtypeStruct((PATCHES * IMG, DEC), BF),
        compiler_params=params(),
        name="place",
    )(code, arrived, mask_token)


def pack_kernel(code_ref, rows_ref, out_ref):
    count = out_ref.shape[0]
    picked = dot(one_hot(count * HALF, code_ref[0]), rows_ref[...])
    out_ref[...] = picked.astype(BF).reshape(count, HALF, DEC)


def pack(code, rows, count):
    return pl.pallas_call(
        pack_kernel,
        grid=(2,),
        in_specs=[
            pl.BlockSpec((1, 1, HROWS), lambda g: (g, 0, 0)),
            pl.BlockSpec((HROWS, DEC), lambda g: (g, 0)),
        ],
        out_specs=pl.BlockSpec((count, HALF, DEC), lambda g: (0, g, 0)),
        out_shape=jax.ShapeDtypeStruct((count, IMG, DEC), BF),
        compiler_params=params(),
        name="pack",
    )(code, rows)


def unpack_kernel(code_ref, slots_ref, out_ref):
    count = slots_ref.shape[0]
    source = slots_ref[...].reshape(count * HALF, DEC)
    out_ref[...] = dot(one_hot(count * HALF, code_ref[0]), source, TN).astype(BF)


def unpack(code, slots):
    count = slots.shape[0]
    return pl.pallas_call(
        unpack_kernel,
        grid=(2,),
        in_specs=[
            pl.BlockSpec((1, 1, HROWS), lambda g: (g, 0, 0)),
            pl.BlockSpec((count, HALF, DEC), lambda g: (0, g, 0)),
        ],
        out_specs=pl.BlockSpec((HROWS, DEC), lambda g: (g, 0)),
        out_shape=jax.ShapeDtypeStruct((ROWS, DEC), BF),
        compiler_params=params(),
        name="unpack",
    )(code, slots)


UNIT = 4 * HEAD


def block_diag(rows):
    lane_head = lax.broadcasted_iota(jnp.int32, rows.shape, 1) // HEAD
    zero = jnp.zeros_like(rows)
    return jnp.concatenate([jnp.where(lane_head == h, rows, zero) for h in range(4)], axis=0)


def fold_heads(left, right):
    low = lax.broadcasted_iota(jnp.int32, (PADK, 2 * HEAD), 1) < HEAD
    return jnp.concatenate(
        [
            jnp.where(low, left[:PADK], left[PADK:]),
            jnp.where(low, right[:PADK], right[PADK:]),
        ],
        axis=1,
    )


def soft_cols(key, query_diag):
    scores = dot(key, query_diag, NT)
    valid = lax.broadcasted_iota(jnp.int32, scores.shape, 0) < KEEP
    scores = jnp.where(valid, scores, -1e30)
    e = jnp.exp(scores - jnp.max(scores, axis=0, keepdims=True))
    return e * (1.0 / jnp.sum(e, axis=0, keepdims=True))


def each_image(image, *refs):
    def group(g, carry):
        base = pl.multiple_of(g * 8 * KEEP, 8)
        views = [ref.at[pl.ds(base, 8 * KEEP + 16)] for ref in refs]
        for near in range(8):
            image(g * 8 + near, near, *views)
        return carry

    lax.fori_loop(0, HALF // 8, group, 0)


def attn_fwd_kernel(
    x_ref, gain_ref, shift_ref, wqkv_ref, bias_ref, wout_ref, obias_ref,
    qkvp_ref, att_ref, hidden_ref, qs, ats,
):
    x = x_ref[...].astype(F32)
    unit, _ = norm(x)
    first = (unit * gain_ref[...] + shift_ref[...]).astype(BF)
    for c in range(3):
        cols = slice(c * D, (c + 1) * D)
        qs[:HROWS, cols] = (
            (dot(first, wqkv_ref[:, cols]) + bias_ref[:, cols]).astype(BF).astype(F32)
        )
    qs[HROWS:, :] = jnp.zeros((16, 3 * D), F32)

    def image(i, near, qs, ats):
        r0 = near * KEEP
        for u in range(UNITS):
            part = []
            for c in range(3):
                cols = slice(c * D + u * UNIT, c * D + (u + 1) * UNIT)
                rows = qs[r0 : r0 + PADK, cols].astype(BF)
                qkvp_ref[i, :, cols] = rows
                part.append(rows)
            q, k, v = part
            probs = soft_cols(k, block_diag(q * BF(0.125))).astype(BF)
            out = fold_heads(
                dot(probs[:, :128], v[:, :128], TN), dot(probs[:, 128:], v[:, 128:], TN)
            )
            ats[r0 : r0 + 56, u * UNIT : (u + 1) * UNIT] = out[:56]

    each_image(image, qs, ats)
    att = ats[:HROWS, :].astype(BF)
    att_ref[...] = att
    hidden_ref[...] = x_ref[...].astype(F32) + (dot(att, wout_ref[...]) + obias_ref[...])


def attn_fwd(x, gain, shift, wqkv, bias, wout, obias):
    return pl.pallas_call(
        attn_fwd_kernel,
        grid=(2,),
        in_specs=[
            pl.BlockSpec((HROWS, D), lambda g: (g, 0)),
            whole((1, D)),
            whole((1, D)),
            whole((D, 3 * D)),
            whole((1, 3 * D)),
            whole((D, D)),
            whole((1, D)),
        ],
        out_specs=[
            pl.BlockSpec((HALF, PADK, 3 * D), lambda g: (g, 0, 0)),
            pl.BlockSpec((HROWS, D), lambda g: (g, 0)),
            pl.BlockSpec((HROWS, D), lambda g: (g, 0)),
        ],
        out_shape=[
            jax.ShapeDtypeStruct((IMG, PADK, 3 * D), BF),
            jax.ShapeDtypeStruct((ROWS, D), BF),
            jax.ShapeDtypeStruct((ROWS, D), F32),
        ],
        scratch_shapes=[pltpu.VMEM((HROWS + 16, 3 * D), F32), pltpu.VMEM((HROWS + 16, D), F32)],
        compiler_params=params(),
        name="attn_fwd",
    )(x, gain, shift, wqkv, bias, wout, obias)


def attn_bwd_kernel(
    hgrad_ref, att_ref, qkvp_ref, x_ref, gain_ref, shift_ref, wout_ref, wqkv_ref,
    pgrad_ref, wg_ref, obias_ref, qkvb_ref, lng_ref, lns_ref,
    ags, dqs, wqacc, woacc,
):
    g = pl.program_id(0)

    @pl.when(g == 0)
    def _():
        wqacc[...] = jnp.zeros_like(wqacc)
        woacc[...] = jnp.zeros_like(woacc)
        for ref in (obias_ref, qkvb_ref, lng_ref, lns_ref):
            ref[...] = jnp.zeros_like(ref)

    branch = hgrad_ref[...].astype(BF)
    obias_ref[...] += col_sum(branch.astype(F32))
    woacc[...] += dot(att_ref[...], branch, TN)
    ags[:HROWS, :] = dot(branch, wout_ref[...], NT)
    ags[HROWS:, :] = jnp.zeros((16, D), F32)

    def image(i, near, ags, dqs):
        r0 = near * KEEP
        valid = lax.broadcasted_iota(jnp.int32, (PADK, UNIT), 0) < KEEP
        for u in range(UNITS):
            q, k, v = (
                qkvp_ref[i, :, c * D + u * UNIT : c * D + (u + 1) * UNIT] for c in range(3)
            )
            q_diag = block_diag(q * BF(0.125))
            probs = soft_cols(k, q_diag)
            probs_in = probs.astype(BF)
            agrad = jnp.where(
                valid, ags[r0 : r0 + PADK, u * UNIT : (u + 1) * UNIT], 0.0
            ).astype(BF)
            a_diag = block_diag(agrad)
            pgrad = dot(v, a_diag, NT)
            vgrad = dot(probs_in, a_diag)
            inner = jnp.sum(probs * pgrad, axis=0, keepdims=True)
            sgrad = (probs * (pgrad - inner)).astype(BF)
            kgrad = dot(sgrad, q_diag)
            qgrad = 0.125 * fold_heads(
                dot(sgrad[:, :128], k[:, :128], TN), dot(sgrad[:, 128:], k[:, 128:], TN)
            )
            for c, grad in enumerate((qgrad, kgrad, vgrad)):
                dqs[r0 : r0 + 56, c * D + u * UNIT : c * D + (u + 1) * UNIT] = grad[:56]

    each_image(image, ags, dqs)
    unit, inv = norm(x_ref[...].astype(F32))
    first = (unit * gain_ref[...] + shift_ref[...]).astype(BF)
    fgrad = None
    for c in range(3):
        cols = slice(c * D, (c + 1) * D)
        grad = dqs[:HROWS, cols].astype(BF)
        qkvb_ref[:, cols] += col_sum(grad.astype(F32))
        wqacc[:, cols] += dot(first, grad, TN)
        term = dot(grad, wqkv_ref[:, cols], NT)
        fgrad = term if fgrad is None else fgrad + term
    lng_ref[...] += col_sum(fgrad * unit)
    lns_ref[...] += col_sum(fgrad)
    pgrad_ref[...] = (hgrad_ref[...] + norm_back(unit, inv, fgrad, gain_ref[...])).astype(BF)

    @pl.when(g == 1)
    def _():
        wg_ref[:, : 3 * D] = wqacc[...].astype(BF)
        wg_ref[:, 3 * D :] = woacc[...].astype(BF)


def attn_bwd(hgrad, att, qkvp, x, gain, shift, wout, wqkv):
    rows = pl.BlockSpec((HROWS, D), lambda g: (g, 0))
    return pl.pallas_call(
        attn_bwd_kernel,
        grid=(2,),
        in_specs=[
            rows,
            rows,
            pl.BlockSpec((HALF, PADK, 3 * D), lambda g: (g, 0, 0)),
            rows,
            whole((1, D)),
            whole((1, D)),
            whole((D, D)),
            whole((D, 3 * D)),
        ],
        out_specs=[
            rows,
            whole((D, 4 * D)),
            whole((1, D)),
            whole((1, 3 * D)),
            whole((1, D)),
            whole((1, D)),
        ],
        out_shape=[
            jax.ShapeDtypeStruct((ROWS, D), BF),
            jax.ShapeDtypeStruct((D, 4 * D), BF),
            jax.ShapeDtypeStruct((1, D), F32),
            jax.ShapeDtypeStruct((1, 3 * D), F32),
            jax.ShapeDtypeStruct((1, D), F32),
            jax.ShapeDtypeStruct((1, D), F32),
        ],
        scratch_shapes=[
            pltpu.VMEM((HROWS + 16, D), F32),
            pltpu.VMEM((HROWS + 16, 3 * D), F32),
            pltpu.VMEM((D, 3 * D), F32),
            pltpu.VMEM((D, D), F32),
        ],
        compiler_params=params(),
        name="attn_bwd",
    )(hgrad, att, qkvp, x, gain, shift, wout, wqkv)


FTILE = 512
FSTEPS = FF // FTILE


def mlp_fwd_kernel(
    hidden_ref, gain_ref, shift_ref, w1_ref, b1_ref, w2_ref, b2_ref, we_ref, be_ref,
    act_ref, slope_ref, block_ref, emb_ref, second, acc,
):
    f = pl.program_id(0)

    @pl.when(f == 0)
    def _():
        unit, _ = norm(hidden_ref[...])
        second[...] = (unit * gain_ref[...] + shift_ref[...]).astype(BF)
        acc[...] = hidden_ref[...] + b2_ref[...]

    for h in range(2):
        rows = slice(h * HROWS, (h + 1) * HROWS)
        active, slope = gelu_pair(dot(second[rows, :], w1_ref[...]) + b1_ref[...])
        active = active.astype(BF)
        act_ref[rows, :] = active
        slope_ref[rows, :] = slope.astype(BF)
        acc[rows, :] += dot(active, w2_ref[...])

    @pl.when(f == FSTEPS - 1)
    def _():
        block_in = acc[...].astype(BF)
        block_ref[...] = block_in
        emb_ref[...] = (dot(block_in, we_ref[...]) + be_ref[...]).astype(BF)


def mlp_fwd(hidden, gain, shift, w1, b1, w2, b2, we, be):
    tile = pl.BlockSpec((ROWS, FTILE), lambda f: (0, f))
    return pl.pallas_call(
        mlp_fwd_kernel,
        grid=(FSTEPS,),
        in_specs=[
            whole((ROWS, D)),
            whole((1, D)),
            whole((1, D)),
            pl.BlockSpec((D, FTILE), lambda f: (0, f)),
            pl.BlockSpec((1, FTILE), lambda f: (0, f)),
            pl.BlockSpec((FTILE, D), lambda f: (f, 0)),
            whole((1, D)),
            whole((D, DEC)),
            whole((1, DEC)),
        ],
        out_specs=[tile, tile, whole((ROWS, D)), whole((ROWS, DEC))],
        out_shape=[
            jax.ShapeDtypeStruct((ROWS, FF), BF),
            jax.ShapeDtypeStruct((ROWS, FF), BF),
            jax.ShapeDtypeStruct((ROWS, D), BF),
            jax.ShapeDtypeStruct((ROWS, DEC), BF),
        ],
        scratch_shapes=[pltpu.VMEM((ROWS, D), BF), pltpu.VMEM((ROWS, D), F32)],
        compiler_params=params(),
        name="mlp_fwd",
    )(hidden, gain, shift, w1, b1, w2, b2, we, be)


def mlp_bwd_kernel(
    egrad_ref, block_ref, hidden_ref, gain_ref, shift_ref, we_ref, act_ref, slope_ref, w2_ref, w1_ref,
    hgrad_ref, weg_ref, ebias_ref, w2g_ref, b2_ref, w1g_ref, b1_ref, lng_ref, lns_ref,
    two, second, acc,
):
    f = pl.program_id(0)

    @pl.when(f == 0)
    def _():
        egrad = egrad_ref[...]
        weg_ref[...] = dot(block_ref[...], egrad, TN).astype(BF)
        ebias_ref[...] = col_sum(egrad.astype(F32))
        out_grad = dot(egrad, we_ref[...], NT)
        hgrad_ref[...] = out_grad
        two_grad = out_grad.astype(BF)
        two[...] = two_grad
        b2_ref[...] = col_sum(two_grad.astype(F32))
        unit, _ = norm(hidden_ref[...])
        second[...] = (unit * gain_ref[...] + shift_ref[...]).astype(BF)
        acc[...] = jnp.zeros_like(acc)

    w2g_ref[...] = dot(act_ref[...], two[...], TN).astype(BF)
    inner = (dot(two[...], w2_ref[...], NT) * slope_ref[...].astype(F32)).astype(BF)
    b1_ref[...] = col_sum(inner.astype(F32))
    w1g_ref[...] = dot(second[...], inner, TN).astype(BF)
    acc[...] += dot(inner, w1_ref[...], NT)

    @pl.when(f == FSTEPS - 1)
    def _():
        unit, inv = norm(hidden_ref[...])
        grad = acc[...]
        lng_ref[...] = col_sum(grad * unit)
        lns_ref[...] = col_sum(grad)
        hgrad_ref[...] += norm_back(unit, inv, grad, gain_ref[...])


def mlp_bwd(egrad, block_in, hidden, gain, shift, we, act, slope, w2, w1):
    tile = pl.BlockSpec((ROWS, FTILE), lambda f: (0, f))
    return pl.pallas_call(
        mlp_bwd_kernel,
        grid=(FSTEPS,),
        in_specs=[
            whole((ROWS, DEC)),
            whole((ROWS, D)),
            whole((ROWS, D)),
            whole((1, D)),
            whole((1, D)),
            whole((D, DEC)),
            tile,
            tile,
            pl.BlockSpec((FTILE, D), lambda f: (f, 0)),
            pl.BlockSpec((D, FTILE), lambda f: (0, f)),
        ],
        out_specs=[
            whole((ROWS, D)),
            whole((D, DEC)),
            whole((1, DEC)),
            pl.BlockSpec((FTILE, D), lambda f: (f, 0)),
            whole((1, D)),
            pl.BlockSpec((D, FTILE), lambda f: (0, f)),
            pl.BlockSpec((1, FTILE), lambda f: (0, f)),
            whole((1, D)),
            whole((1, D)),
        ],
        out_shape=[
            jax.ShapeDtypeStruct((ROWS, D), F32),
            jax.ShapeDtypeStruct((D, DEC), BF),
            jax.ShapeDtypeStruct((1, DEC), F32),
            jax.ShapeDtypeStruct((FF, D), BF),
            jax.ShapeDtypeStruct((1, D), F32),
            jax.ShapeDtypeStruct((D, FF), BF),
            jax.ShapeDtypeStruct((1, FF), F32),
            jax.ShapeDtypeStruct((1, D), F32),
            jax.ShapeDtypeStruct((1, D), F32),
        ],
        scratch_shapes=[
            pltpu.VMEM((ROWS, D), BF),
            pltpu.VMEM((ROWS, D), BF),
            pltpu.VMEM((ROWS, D), F32),
        ],
        compiler_params=params(),
        name="mlp_bwd",
    )(egrad, block_in, hidden, gain, shift, we, act, slope, w2, w1)


MESH = pl.DeviceIdType.MESH


def axis_sizes(dp_count, seq_count):
    z = 4 if seq_count % 4 == 0 else 1
    return {"core": 2, "x": dp_count // 2, "y": seq_count // z, "z": z}


def cut(dp_count, rows, cols):
    for a in range(1, dp_count + 1):
        b = dp_count // a
        if a * b == dp_count and rows % (16 * a) == 0 and cols % (128 * b) == 0:
            return a, b
    raise ValueError("no cut")


def chunk_list(dp_count, shapes):
    chunks = []
    for at, (rows, cols) in enumerate(shapes):
        a, b = cut(dp_count, rows, cols)
        r, c = rows // a, cols // b
        halves = 2 if r % 32 == 0 and r * c > 32768 else 1
        for h in range(halves):
            chunks.append((at, a, b, r, h * (r // halves), r // halves, c))
    return chunks


ORDERS = (("x", "y", "z"), ("y", "x", "z"))
OWN_DIMS = {"x": 0, "z": 1, "y": 2}


def reduce_kernel(sizes, shapes, chunks, *refs):
    n = len(shapes)
    ins, outs, refs = refs[:n], refs[n : 2 * n], refs[2 * n :]
    per = 6
    bufs = [refs[per * i : per * (i + 1)] for i in range(len(chunks))]
    local_sem, send_sem, recv_sem = refs[per * len(chunks) :]
    dp, sq = lax.axis_index("dp"), lax.axis_index("seq")
    ny = sizes["y"]
    me = {"core": lax.rem(dp, 2), "x": dp // 2, "y": lax.rem(sq, ny), "z": sq // ny}

    def device(coord):
        return {"dp": coord["x"] * 2 + coord["core"], "seq": coord["z"] * ny + coord["y"]}

    def peer(axis, d):
        coord = dict(me)
        coord[axis] = lax.rem(me[axis] + d, sizes[axis])
        return coord

    count = 0
    barrier = pltpu.get_barrier_semaphore()
    for axis in sizes:
        for d in range(1, sizes[axis]):
            pl.semaphore_signal(barrier, inc=1, device_id=device(peer(axis, d)), device_id_type=MESH)
            count += 1
    pl.semaphore_wait(barrier, count)

    most = max(sizes.values())

    def copy(i, stage, d, src, dst, coord):
        slot = (i * 6 + stage) * most + d
        return pltpu.make_async_remote_copy(
            src_ref=src,
            dst_ref=dst,
            send_sem=send_sem.at[slot],
            recv_sem=recv_sem.at[slot],
            device_id=device(coord),
            device_id_type=MESH,
        )

    def piece(i, x, core):
        at, a, b, r, r0, rows, cols = chunks[i]
        q = x * 2 + core
        row = (q // b) * r + r0
        return ins[at].at[
            :, :, pl.ds(pl.multiple_of(row, 16), rows), pl.ds(pl.multiple_of(lax.rem(q, b) * cols, 128), cols)
        ]

    def index(done, axis=None, value=None):
        at = [slice(None)] * 3
        for name in done:
            at[OWN_DIMS[name]] = me[name]
        if axis is not None:
            at[OWN_DIMS[axis]] = value
        return tuple(at)

    nx = sizes["x"]
    loads, sends = [], {}
    for i in range(len(chunks)):
        own, recv = bufs[i][:2]
        sends[i, 0] = []
        for x in range(nx):
            sends[i, 0].append(
                copy(i, 0, x, piece(i, x, 1 - me["core"]), recv.at[x], peer("core", 1))
            )
            sends[i, 0][-1].start()
        load = []
        for x in range(nx):
            load.append(
                pltpu.make_async_copy(piece(i, x, me["core"]), own.at[x], local_sem.at[i * nx + x])
            )
            load[-1].start()
        loads.append(load)

    def add_core(i):
        own, recv = bufs[i][:2]
        for x in range(nx):
            loads[i][x].wait()
            sends[i, 0][x].wait()

        def body(k, carry):
            x, z, y = k // (sizes["z"] * ny), lax.rem(k // ny, sizes["z"]), lax.rem(k, ny)
            own[x, z, y] = own[x, z, y] + recv[x, z, y]
            return carry

        lax.fori_loop(0, nx * sizes["z"] * ny, body, 0)

    def start(i, stage):
        order = ORDERS[i % 2]
        axis, done = order[stage - 1], order[: stage - 1]
        own, recv = bufs[i][0], bufs[i][1 + stage]
        sends[i, stage] = []
        for d in range(1, sizes[axis]):
            coord = peer(axis, d)
            sends[i, stage].append(
                copy(i, stage, d - 1, own.at[index(done, axis, coord[axis])], recv.at[d - 1], coord)
            )
            sends[i, stage][-1].start()

    def add(i, stage):
        order = ORDERS[i % 2]
        done = order[:stage]
        own, recv, gathered = bufs[i][0], bufs[i][1 + stage], bufs[i][5]
        for c in sends[i, stage]:
            c.wait()
        left = [name for name in ("x", "z", "y") if name not in done]
        total = math.prod(sizes[name] for name in left)

        def body(k, carry):
            at, rest = {name: me[name] for name in done}, k
            for name in reversed(left):
                at[name] = lax.rem(rest, sizes[name])
                rest = rest // sizes[name]
            here = (at["x"], at["z"], at["y"])
            there = tuple(at[name] for name in left)
            value = own[here].astype(F32)
            for d in range(sizes[order[stage - 1]] - 1):
                value = value + recv[(d,) + there].astype(F32)
            if stage == 3:
                gathered[me["x"] * 2 + me["core"]] = value.astype(BF)
            else:
                own[here] = value.astype(BF)
            return carry

        if total == 1:
            body(0, 0)
        else:
            lax.fori_loop(0, total, body, 0)

    def gather(i, stage):
        gathered = bufs[i][5]
        sends[i, stage] = []
        if stage == 4:
            q = me["x"] * 2 + me["core"]
            for d in range(1, nx):
                sends[i, stage].append(
                    copy(i, stage, d - 1, gathered.at[q], gathered.at[q], peer("x", d))
                )
        else:
            for x in range(nx):
                q = x * 2 + me["core"]
                sends[i, stage].append(
                    copy(i, stage, x, gathered.at[q], gathered.at[q], peer("core", 1))
                )
        for c in sends[i, stage]:
            c.start()

    def finish(i):
        at, a, b, r, r0, rows, cols = chunks[i]
        gathered = bufs[i][5]
        for c in sends[i, 5]:
            c.wait()
        for q in range(a * b):
            row, col = (q // b) * r + r0, (q % b) * cols
            outs[at][row : row + rows, col : col + cols] = gathered[q].astype(F32)

    def wait_all(i, stage):
        for c in sends[i, stage]:
            c.wait()

    pairs = [[i for i in (2 * p, 2 * p + 1) if i < len(chunks)] for p in range((len(chunks) + 1) // 2)]
    steps = [
        lambda i: (add_core(i), start(i, 1)),
        lambda i: (add(i, 1), start(i, 2)),
        lambda i: (add(i, 2), start(i, 3)),
        lambda i: (add(i, 3), gather(i, 4)),
        lambda i: (wait_all(i, 4), gather(i, 5)),
        finish,
    ]
    for step in range(len(pairs) + len(steps) - 1):
        for p in range(len(pairs)):
            if 0 <= step - p < len(steps):
                for i in pairs[p]:
                    steps[step - p](i)


def reduce_all(arrays):
    dp_count, seq_count = lax.axis_size("dp"), lax.axis_size("seq")
    sizes = axis_sizes(dp_count, seq_count)
    shapes = [(v.shape[0] // seq_count, v.shape[1]) for v in arrays]
    chunks = chunk_list(dp_count, shapes)
    nx, ny, nz = sizes["x"], sizes["y"], sizes["z"]
    views = [
        v.reshape(nz, ny, rows, cols) for v, (rows, cols) in zip(arrays, shapes, strict=True)
    ]
    scratch = []
    for i, (_, _, _, _, _, rows, cols) in enumerate(chunks):
        order = ORDERS[i % 2]
        scratch.append(pltpu.VMEM((nx, nz, ny, rows, cols), BF))
        scratch.append(pltpu.VMEM((nx, nz, ny, rows, cols), BF))
        for stage in range(1, 4):
            done = order[:stage]
            left = [sizes[name] for name in ("x", "z", "y") if name not in done]
            scratch.append(pltpu.VMEM((sizes[order[stage - 1]] - 1, *left, rows, cols), BF))
        scratch.append(pltpu.VMEM((dp_count, rows, cols), BF))
    slots = len(chunks) * 6 * max(sizes.values())
    return pl.pallas_call(
        functools.partial(reduce_kernel, sizes, shapes, chunks),
        in_specs=[pl.BlockSpec(memory_space=pl.ANY)] * len(arrays),
        out_specs=[pl.BlockSpec(memory_space=pltpu.VMEM)] * len(arrays),
        out_shape=[jax.ShapeDtypeStruct(shape, F32) for shape in shapes],
        scratch_shapes=scratch
        + [
            pltpu.SemaphoreType.DMA((len(chunks) * nx,)),
            pltpu.SemaphoreType.DMA((slots,)),
            pltpu.SemaphoreType.DMA((slots,)),
        ],
        compiler_params=pltpu.CompilerParams(
            collective_id=0, has_side_effects=True, vmem_limit_bytes=60 * MIB
        ),
        name="reduce_all",
    )(*views)


def decoder_codes(keep_index, slots):
    seq_count = lax.axis_size("seq")
    dev_blocks, _, padded = owner_blocks(seq_count)
    t = jnp.arange(seq_count, dtype=jnp.int32)
    start = first_block(seq_count, t)
    lowest = (lax.axis_index("seq") * PATCHES + start) // seq_count
    m = jnp.arange(padded, dtype=jnp.int32)
    valid = (start[:, None] + m[None, :] * seq_count) < dev_blocks
    place_at = (lowest[:, None] + m[None, :])[None, :, :, None]
    kept = keep_index.T.reshape(KEEP, seq_count, 1, IMG)
    hit = jnp.sum((kept == place_at).astype(jnp.int32), axis=0)
    below = (kept < place_at) & (kept >= lowest[None, :, None, None])
    rank = jnp.sum(below.astype(jnp.int32), axis=0)
    image = jnp.arange(IMG, dtype=jnp.int32)
    code = jnp.where(hit > 0, rank * IMG + image, slots * IMG)
    code = jnp.where(valid[:, :, None], code, -1)
    return code.reshape(seq_count, 1, padded * IMG)


def image_codes(keep_index, slots):
    seq_count = lax.axis_size("seq")
    group_imgs = keep_index.shape[0]
    at = lax.axis_index("seq") * IMG
    own = lax.dynamic_slice_in_dim(keep_index, at, IMG, 0)
    image = jnp.arange(IMG, dtype=jnp.int32)[:, None]
    owner = (own * group_imgs + at + image) // (IMG * PATCHES)
    lower = jnp.sum((owner[:, None, :] < owner[:, :, None]).astype(jnp.int32), axis=2)
    rank = jnp.arange(KEEP, dtype=jnp.int32)[None, :] - lower
    code = (owner * slots + rank) * HALF + image % HALF
    return code.reshape(2, 1, HROWS)


def local(
    patches,
    keep_index,
    ln1_gain,
    ln1_shift,
    w_qkv,
    q_bias,
    v_bias,
    w_out,
    out_bias,
    ln2_gain,
    ln2_shift,
    w_fc1,
    fc1_bias,
    w_fc2,
    fc2_bias,
    w_embed,
    embed_bias,
    mask_token,
    decoder_grad,
):
    seq_count = lax.axis_size("seq")
    slots = 2 * KEEP // seq_count
    row = lambda v: v.reshape(1, -1)
    dec_code = decoder_codes(keep_index, slots)
    img_code = image_codes(keep_index, slots)
    grad_slots, mask_rows = pick(seq_count, slots, dec_code, decoder_grad)
    returned = lax.all_to_all(grad_slots, "seq", split_axis=0, concat_axis=0, tiled=True)

    qkv_bias = jnp.concatenate([q_bias, jnp.zeros_like(q_bias), v_bias])
    qkvp, attended, hidden = attn_fwd(
        patches, row(ln1_gain), row(ln1_shift), w_qkv, row(qkv_bias), w_out, row(out_bias)
    )
    active, slope, block_in, embedded = mlp_fwd(
        hidden, row(ln2_gain), row(ln2_shift), w_fc1, row(fc1_bias), w_fc2, row(fc2_bias),
        w_embed, row(embed_bias),
    )
    send = pack(img_code, embedded, seq_count * slots)
    arrived = lax.all_to_all(send, "seq", split_axis=0, concat_axis=0, tiled=True)

    embed_grad = unpack(img_code, returned)
    hgrad, weg, ebias, w2g, b2, w1g, b1, ln2g, ln2s = mlp_bwd(
        embed_grad, block_in, hidden, row(ln2_gain), row(ln2_shift), w_embed, active, slope,
        w_fc2, w_fc1,
    )
    patches_grad, wg, obias, qkvb, ln1g, ln1s = attn_bwd(
        hgrad, attended, qkvp, patches, row(ln1_gain), row(ln1_shift), w_out, w_qkv
    )
    vectors = [
        ln1g, ln1s, qkvb[:, :D], qkvb[:, 2 * D :], obias, ln2g, ln2s, b1, b2, ebias, mask_rows[:1],
    ]
    packed = jnp.concatenate([v.reshape(seq_count, -1) for v in vectors], axis=1).astype(BF)
    small_rows = D // seq_count
    extra = -(-packed.shape[1] // DEC)
    padded_rows = -(-(small_rows + extra) // 16) * 16
    packed = jnp.pad(packed, ((0, 0), (0, extra * DEC - packed.shape[1])))
    tail = jnp.concatenate(
        [weg.reshape(seq_count, small_rows, DEC), packed.reshape(seq_count, extra, DEC)], axis=1
    )
    tail = jnp.pad(tail, ((0, 0), (0, padded_rows - tail.shape[1]), (0, 0)))
    w1g, w2g, wg, tail = reduce_all([w1g, w2g, wg, tail.reshape(seq_count * padded_rows, DEC)])
    wqkvg, woutg, weg = wg[:, : 3 * D], wg[:, 3 * D :], tail[:small_rows]
    small = tail[small_rows:].reshape(-1)
    parts, at = [], 0
    for v in vectors:
        size = v.shape[1] // seq_count
        parts.append(small[at : at + size])
        at += size
    ln1g, ln1s, qb, vb, obias, ln2g, ln2s, b1, b2, ebias, mask_grad = parts
    decoder_input = place(seq_count, slots, dec_code, arrived, row(mask_token))
    return (
        decoder_input,
        patches_grad,
        ln1g,
        ln1s,
        wqkvg,
        qb,
        vb,
        woutg,
        obias,
        ln2g,
        ln2s,
        w1g,
        b1,
        w2g,
        b2,
        weg,
        ebias,
        mask_grad,
    )


def solution(mesh):
    rows = P(("dp", "seq"), None)
    placed = (rows, P("dp", None)) + (P(),) * 16 + (rows,)
    vec, mat = P("seq"), P("seq", None)
    return jax.shard_map(
        local,
        mesh=mesh,
        in_specs=placed,
        out_specs=(
            rows, rows, vec, vec, mat, vec, vec, mat, vec, vec, vec, mat, vec, mat, vec, mat, vec, vec,
        ),
        check_vma=False,
    )
```

```python
import functools
import math

import jax
import jax.numpy as jnp
from jax import lax
from jax.experimental import pallas as pl
from jax.experimental.pallas import tpu as pltpu
from jax.sharding import PartitionSpec as P

D = 768
HEADS = 12
HEAD = 64
FF = 3072
DEC = 512
PATCHES = 196
KEEP = 49
IMG = 32
HALF = 16
ROWS = IMG * KEEP
HROWS = HALF * KEEP
PADK = 64
UNITS = 3
EPSILON = 1e-06
BF = jnp.bfloat16
F32 = jnp.float32
MIB = 1 << 20

NN = (((1,), (0,)), ((), ()))
NT = (((1,), (1,)), ((), ()))
TN = (((0,), (0,)), ((), ()))


def dot(left, right, dims=NN):
    return lax.dot_general(left, right, dims, preferred_element_type=F32)


def params(mib=60):
    return pltpu.CompilerParams(vmem_limit_bytes=mib * MIB)


def whole(shape):
    return pl.BlockSpec(shape, lambda *_: (0,) * len(shape), pipeline_mode=pl.Buffered(1))


def norm(values):
    centered = values - jnp.mean(values, axis=-1, keepdims=True)
    inv = lax.rsqrt(jnp.mean(centered * centered, axis=-1, keepdims=True) + EPSILON)
    return centered * inv, inv


def norm_back(unit, inv, grad, gain):
    f = grad * gain
    return inv * (
        f
        - jnp.mean(f, axis=-1, keepdims=True)
        - unit * jnp.mean(f * unit, axis=-1, keepdims=True)
    )


def col_sum(values):
    return jnp.sum(values, axis=0, keepdims=True)


def gelu_pair(v):
    z = jnp.abs(v) * (1 / math.sqrt(2.0))
    t = 1.0 / (1.0 + 0.3275911 * z)
    e = jnp.exp(-z * z)
    poly = t * (
        0.5 * 0.254829592
        + t
        * (
            0.5 * -0.284496736
            + t * (0.5 * 1.421413741 + t * (0.5 * -1.453152027 + t * (0.5 * 1.061405429)))
        )
    )
    tail = poly * e
    cdf = jnp.where(v >= 0, 1.0 - tail, tail)
    return v * cdf, cdf + v * (e * (1 / math.sqrt(2 * math.pi)))


def one_hot(rows, code):
    at = lax.broadcasted_iota(jnp.int32, (rows, code.shape[1]), 0)
    return jnp.where(at == code, 1.0, 0.0).astype(BF)


def owner_blocks(seq_count):
    dev_blocks = PATCHES
    most = -(-dev_blocks // seq_count)
    return dev_blocks, most, -(-most // 4) * 4


def first_block(seq_count, t):
    return lax.rem(
        t + seq_count - lax.rem(lax.axis_index("seq") * PATCHES, seq_count), seq_count
    )


def pick_kernel(seq_count, slots, code_ref, dec_ref, out_ref, sum_ref):
    t = pl.program_id(0)
    dev_blocks, most, padded = owner_blocks(seq_count)
    start = first_block(seq_count, t)
    pieces = []
    for m in range(most):
        at = start + m * seq_count
        clamped = jnp.minimum(at, dev_blocks - 1)
        pieces.append(dec_ref[pl.ds(pl.multiple_of(clamped * IMG, IMG), IMG), :])
    if padded > most:
        pieces.append(jnp.zeros(((padded - most) * IMG, DEC), BF))
    picked = dot(one_hot(slots * IMG + 16, code_ref[0]), jnp.concatenate(pieces, axis=0))
    out_ref[...] = picked[: slots * IMG].astype(BF).reshape(slots, IMG, DEC)

    @pl.when(t == 0)
    def _():
        sum_ref[...] = jnp.zeros_like(sum_ref)

    sum_ref[...] += picked[slots * IMG : slots * IMG + 8]


def pick(seq_count, slots, code, dec_grad):
    return pl.pallas_call(
        functools.partial(pick_kernel, seq_count, slots),
        grid=(seq_count,),
        in_specs=[
            pl.BlockSpec((1, 1, code.shape[2]), lambda t: (t, 0, 0)),
            whole(dec_grad.shape),
        ],
        out_specs=[
            pl.BlockSpec((slots, IMG, DEC), lambda t: (t, 0, 0)),
            pl.BlockSpec((8, DEC), lambda t: (0, 0)),
        ],
        out_shape=[
            jax.ShapeDtypeStruct((seq_count * slots, IMG, DEC), BF),
            jax.ShapeDtypeStruct((8, DEC), F32),
        ],
        compiler_params=params(),
        name="pick",
    )(code, dec_grad)


def place_kernel(seq_count, slots, code_ref, arrived_ref, mask_ref, out_ref):
    t = pl.program_id(0)
    dev_blocks, most, padded = owner_blocks(seq_count)
    start = first_block(seq_count, t)
    fill = jnp.where(
        lax.broadcasted_iota(jnp.int32, (16, DEC), 0) == 0, mask_ref[...], 0.0
    ).astype(BF)
    source = jnp.concatenate([arrived_ref[...].reshape(slots * IMG, DEC), fill], axis=0)
    spread = dot(one_hot(slots * IMG + 16, code_ref[0]), source, TN).astype(BF)
    for m in range(most):
        at = start + m * seq_count
        piece = spread[m * IMG : (m + 1) * IMG]
        if (m + 1) * seq_count <= dev_blocks:
            out_ref[pl.ds(pl.multiple_of(at * IMG, IMG), IMG), :] = piece
        else:

            @pl.when(at < dev_blocks)
            def _():
                out_ref[pl.ds(pl.multiple_of(at * IMG, IMG), IMG), :] = piece


def pack_kernel(code_ref, rows_ref, out_ref):
    count = out_ref.shape[0]
    picked = dot(one_hot(count * HALF, code_ref[0]), rows_ref[...])
    out_ref[...] = picked.astype(BF).reshape(count, HALF, DEC)


def pack(code, rows, count):
    return pl.pallas_call(
        pack_kernel,
        grid=(2,),
        in_specs=[
            pl.BlockSpec((1, 1, HROWS), lambda g: (g, 0, 0)),
            pl.BlockSpec((HROWS, DEC), lambda g: (g, 0)),
        ],
        out_specs=pl.BlockSpec((count, HALF, DEC), lambda g: (0, g, 0)),
        out_shape=jax.ShapeDtypeStruct((count, IMG, DEC), BF),
        compiler_params=params(),
        name="pack",
    )(code, rows)


def unpack_kernel(code_ref, slots_ref, out_ref):
    count = slots_ref.shape[0]
    source = slots_ref[...].reshape(count * HALF, DEC)
    out_ref[...] = dot(one_hot(count * HALF, code_ref[0]), source, TN).astype(BF)


def unpack(code, slots):
    count = slots.shape[0]
    return pl.pallas_call(
        unpack_kernel,
        grid=(2,),
        in_specs=[
            pl.BlockSpec((1, 1, HROWS), lambda g: (g, 0, 0)),
            pl.BlockSpec((count, HALF, DEC), lambda g: (0, g, 0)),
        ],
        out_specs=pl.BlockSpec((HROWS, DEC), lambda g: (g, 0)),
        out_shape=jax.ShapeDtypeStruct((ROWS, DEC), BF),
        compiler_params=params(),
        name="unpack",
    )(code, slots)


UNIT = 4 * HEAD
PAIR = 2 * HEAD


def block_diag(rows):
    heads = rows.shape[1] // HEAD
    lane_head = lax.broadcasted_iota(jnp.int32, rows.shape, 1) // HEAD
    zero = jnp.zeros_like(rows)
    return jnp.concatenate([jnp.where(lane_head == h, rows, zero) for h in range(heads)], axis=0)


def fold_pair(rows):
    low = lax.broadcasted_iota(jnp.int32, (PADK, PAIR), 1) < HEAD
    return jnp.where(low, rows[:PADK], rows[PADK:])


def soft(scores, axis):
    valid = lax.broadcasted_iota(jnp.int32, scores.shape, axis) < KEEP
    scores = jnp.where(valid, scores, -1e30)
    e = jnp.exp(scores - jnp.max(scores, axis=axis, keepdims=True))
    return e * (1.0 / jnp.sum(e, axis=axis, keepdims=True))


def each_image(count, image, *refs):
    def group(g, carry):
        base = pl.multiple_of(g * 8 * KEEP, 8)
        views = [ref.at[pl.ds(base, 8 * KEEP + 16)] for ref in refs]
        for near in range(8):
            image(g * 8 + near, near, *views)
        return carry

    lax.fori_loop(0, count // 8, group, 0)


def attn_fwd_kernel(
    x_ref, gain_ref, shift_ref, wqkv_ref, bias_ref, wout_ref, obias_ref,
    qkvp_ref, att_ref, hidden_ref, qs, ats,
):
    x = x_ref[...].astype(F32)
    unit, _ = norm(x)
    first = (unit * gain_ref[...] + shift_ref[...]).astype(BF)
    for c in range(3):
        cols = slice(c * D, (c + 1) * D)
        qs[:HROWS, cols] = (
            (dot(first, wqkv_ref[:, cols]) + bias_ref[:, cols]).astype(BF).astype(F32)
        )
    qs[HROWS:, :] = jnp.zeros((16, 3 * D), F32)

    def image(i, near, qs, ats):
        r0 = near * KEEP
        for u in range(HEADS // 2):
            part = []
            for c in range(3):
                cols = slice(c * D + u * PAIR, c * D + (u + 1) * PAIR)
                rows = qs[r0 : r0 + PADK, cols].astype(BF)
                to = c * UNIT + (u % 2) * PAIR
                qkvp_ref[u // 2, i, :, to : to + PAIR] = rows
                part.append(rows)
            q, k, v = part
            probs = soft(dot(block_diag(q * BF(0.125)), k, NT), 1).astype(BF)
            out = fold_pair(dot(probs, v))
            ats[r0 : r0 + 56, u * PAIR : (u + 1) * PAIR] = out[:56]

    each_image(HALF, image, qs, ats)
    att = ats[:HROWS, :].astype(BF)
    att_ref[...] = att
    hidden_ref[...] = x_ref[...].astype(F32) + (dot(att, wout_ref[...]) + obias_ref[...])


def attn_fwd(x, gain, shift, wqkv, bias, wout, obias):
    return pl.pallas_call(
        attn_fwd_kernel,
        grid=(2,),
        in_specs=[
            pl.BlockSpec((HROWS, D), lambda g: (g, 0)),
            whole((1, D)),
            whole((1, D)),
            whole((D, 3 * D)),
            whole((1, 3 * D)),
            whole((D, D)),
            whole((1, D)),
        ],
        out_specs=[
            pl.BlockSpec((UNITS, HALF, PADK, 3 * UNIT), lambda g: (0, g, 0, 0)),
            pl.BlockSpec((HROWS, D), lambda g: (g, 0)),
            pl.BlockSpec((HROWS, D), lambda g: (g, 0)),
        ],
        out_shape=[
            jax.ShapeDtypeStruct((UNITS, IMG, PADK, 3 * UNIT), BF),
            jax.ShapeDtypeStruct((ROWS, D), BF),
            jax.ShapeDtypeStruct((ROWS, D), F32),
        ],
        scratch_shapes=[pltpu.VMEM((HROWS + 16, 3 * D), F32), pltpu.VMEM((HROWS + 16, D), F32)],
        compiler_params=params(),
        name="attn_fwd",
    )(x, gain, shift, wqkv, bias, wout, obias)


FTILE = 512
FSTEPS = FF // FTILE


def mlp_fwd_kernel(
    hidden_ref, gain_ref, shift_ref, w1_ref, b1_ref, w2_ref, b2_ref, we_ref, be_ref,
    act_ref, slope_ref, block_ref, emb_ref, second, acc,
):
    f = pl.program_id(0)

    @pl.when(f == 0)
    def _():
        unit, _ = norm(hidden_ref[...])
        second[...] = (unit * gain_ref[...] + shift_ref[...]).astype(BF)
        acc[...] = hidden_ref[...] + b2_ref[...]

    for h in range(2):
        rows = slice(h * HROWS, (h + 1) * HROWS)
        active, slope = gelu_pair(dot(second[rows, :], w1_ref[...]) + b1_ref[...])
        active = active.astype(BF)
        act_ref[rows, :] = active
        slope_ref[rows, :] = slope.astype(BF)
        acc[rows, :] += dot(active, w2_ref[...])

    @pl.when(f == FSTEPS - 1)
    def _():
        block_in = acc[...].astype(BF)
        block_ref[...] = block_in
        emb_ref[...] = (dot(block_in, we_ref[...]) + be_ref[...]).astype(BF)


def mlp_fwd(hidden, gain, shift, w1, b1, w2, b2, we, be):
    tile = pl.BlockSpec((ROWS, FTILE), lambda f: (0, f))
    return pl.pallas_call(
        mlp_fwd_kernel,
        grid=(FSTEPS,),
        in_specs=[
            whole((ROWS, D)),
            whole((1, D)),
            whole((1, D)),
            pl.BlockSpec((D, FTILE), lambda f: (0, f)),
            pl.BlockSpec((1, FTILE), lambda f: (0, f)),
            pl.BlockSpec((FTILE, D), lambda f: (f, 0)),
            whole((1, D)),
            whole((D, DEC)),
            whole((1, DEC)),
        ],
        out_specs=[tile, tile, whole((ROWS, D)), whole((ROWS, DEC))],
        out_shape=[
            jax.ShapeDtypeStruct((ROWS, FF), BF),
            jax.ShapeDtypeStruct((ROWS, FF), BF),
            jax.ShapeDtypeStruct((ROWS, D), BF),
            jax.ShapeDtypeStruct((ROWS, DEC), BF),
        ],
        scratch_shapes=[pltpu.VMEM((ROWS, D), BF), pltpu.VMEM((ROWS, D), F32)],
        compiler_params=params(),
        name="mlp_fwd",
    )(hidden, gain, shift, w1, b1, w2, b2, we, be)


def mlp_bwd_kernel(
    egrad_ref, block_ref, hidden_ref, gain_ref, shift_ref, we_ref, act_ref, slope_ref, w2_ref, w1_ref,
    hgrad_ref, weg_ref, ebias_ref, w2g_ref, b2_ref, w1g_ref, b1_ref, lng_ref, lns_ref,
    two, second, acc,
):
    f = pl.program_id(0)

    @pl.when(f == 0)
    def _():
        egrad = egrad_ref[...]
        weg_ref[...] = dot(block_ref[...], egrad, TN).astype(BF)
        ebias_ref[...] = col_sum(egrad.astype(F32))
        out_grad = dot(egrad, we_ref[...], NT)
        hgrad_ref[...] = out_grad
        two_grad = out_grad.astype(BF)
        two[...] = two_grad
        b2_ref[...] = col_sum(two_grad.astype(F32))
        unit, _ = norm(hidden_ref[...])
        second[...] = (unit * gain_ref[...] + shift_ref[...]).astype(BF)
        acc[...] = jnp.zeros_like(acc)

    w2g_ref[...] = dot(act_ref[...], two[...], TN).astype(BF)
    inner = (dot(two[...], w2_ref[...], NT) * slope_ref[...].astype(F32)).astype(BF)
    b1_ref[...] = col_sum(inner.astype(F32))
    w1g_ref[...] = dot(second[...], inner, TN).astype(BF)
    acc[...] += dot(inner, w1_ref[...], NT)

    @pl.when(f == FSTEPS - 1)
    def _():
        unit, inv = norm(hidden_ref[...])
        grad = acc[...]
        lng_ref[...] = col_sum(grad * unit)
        lns_ref[...] = col_sum(grad)
        hgrad_ref[...] += norm_back(unit, inv, grad, gain_ref[...])


def mlp_bwd(egrad, block_in, hidden, gain, shift, we, act, slope, w2, w1):
    tile = pl.BlockSpec((ROWS, FTILE), lambda f: (0, f))
    return pl.pallas_call(
        mlp_bwd_kernel,
        grid=(FSTEPS,),
        in_specs=[
            whole((ROWS, DEC)),
            whole((ROWS, D)),
            whole((ROWS, D)),
            whole((1, D)),
            whole((1, D)),
            whole((D, DEC)),
            tile,
            tile,
            pl.BlockSpec((FTILE, D), lambda f: (f, 0)),
            pl.BlockSpec((D, FTILE), lambda f: (0, f)),
        ],
        out_specs=[
            whole((ROWS, D)),
            whole((D, DEC)),
            whole((1, DEC)),
            pl.BlockSpec((FTILE, D), lambda f: (f, 0)),
            whole((1, D)),
            pl.BlockSpec((D, FTILE), lambda f: (0, f)),
            pl.BlockSpec((1, FTILE), lambda f: (0, f)),
            whole((1, D)),
            whole((1, D)),
        ],
        out_shape=[
            jax.ShapeDtypeStruct((ROWS, D), F32),
            jax.ShapeDtypeStruct((D, DEC), BF),
            jax.ShapeDtypeStruct((1, DEC), F32),
            jax.ShapeDtypeStruct((FF, D), BF),
            jax.ShapeDtypeStruct((1, D), F32),
            jax.ShapeDtypeStruct((D, FF), BF),
            jax.ShapeDtypeStruct((1, FF), F32),
            jax.ShapeDtypeStruct((1, D), F32),
            jax.ShapeDtypeStruct((1, D), F32),
        ],
        scratch_shapes=[
            pltpu.VMEM((ROWS, D), BF),
            pltpu.VMEM((ROWS, D), BF),
            pltpu.VMEM((ROWS, D), F32),
        ],
        compiler_params=params(),
        name="mlp_bwd",
    )(egrad, block_in, hidden, gain, shift, we, act, slope, w2, w1)


MESH = pl.DeviceIdType.MESH
ORDERS = (("x", "y", "z"), ("y", "x", "z"))
DIMS = {"x": 0, "z": 1, "y": 2}
VROWS = 16


def axis_sizes(dp_count, seq_count):
    z = 4 if seq_count % 4 == 0 else 1
    return {"core": 2, "x": dp_count // 2, "y": seq_count // z, "z": z}


def cut(dp_count, rows, cols):
    for padded in range(rows, rows + 256, 16):
        for a in range(1, dp_count + 1):
            b = dp_count // a
            if a * b == dp_count and padded % (16 * a) == 0 and cols % (128 * b) == 0:
                return a, b, padded
    raise ValueError("no cut")


class Chunk:
    def __init__(self, dp_count, rows, cols, half, halves, order):
        self.a, self.b, self.padded = cut(dp_count, rows, cols)
        self.r, self.cols = self.padded // self.a, cols // self.b
        self.rows = self.r // halves
        self.r0 = half * self.rows
        self.order = ORDERS[order]

    def scratch(self, sizes):
        dims = [sizes[name] for name in ("x", "z", "y")]
        shapes = [(*dims, self.rows, self.cols)] * 2
        for stage in range(1, 4):
            left = [sizes[name] for name in ("x", "z", "y") if name not in self.order[:stage]]
            shapes.append((sizes[self.order[stage - 1]] - 1, *left, self.rows, self.cols))
        shapes.append((sizes["x"] * 2, self.rows, self.cols))
        return [pltpu.VMEM(shape, BF) for shape in shapes]


def halves_of(dp_count, rows, cols):
    a, _, padded = cut(dp_count, rows, cols)
    return 2 if (padded // a) % 32 == 0 else 1


def chunk_table(dp_count, seq_count):
    table = {}
    for name, rows, cols in (("fc2", FF, D), ("fc1", D, FF)):
        rows //= seq_count
        halves = halves_of(dp_count, rows, cols)
        for h in range(halves):
            table[f"{name}_{h}"] = Chunk(dp_count, rows, cols, h, halves, h)
    table["embed"] = Chunk(dp_count, D // seq_count, DEC, 0, 1, 0)
    for i, name in enumerate(("out", "unit_0", "unit_1", "unit_2")):
        table[name] = Chunk(dp_count, D // seq_count, D, 0, 1, (i + 1) % 2)
    return table


class Net:
    def __init__(self, sizes, send_sem, recv_sem):
        self.sizes, self.send_sem, self.recv_sem = sizes, send_sem, recv_sem
        self.used = 0
        dp, sq = lax.axis_index("dp"), lax.axis_index("seq")
        ny = sizes["y"]
        self.me = {"core": lax.rem(dp, 2), "x": dp // 2, "y": lax.rem(sq, ny), "z": sq // ny}

    def device(self, axis, value):
        coord = dict(self.me)
        coord[axis] = value
        return {
            "dp": coord["x"] * 2 + coord["core"],
            "seq": coord["z"] * self.sizes["y"] + coord["y"],
        }

    def peer(self, axis, d):
        return lax.rem(self.me[axis] + d, self.sizes[axis])

    def barrier(self):
        sem, count = pltpu.get_barrier_semaphore(), 0
        for axis, size in self.sizes.items():
            for d in range(1, size):
                pl.semaphore_signal(
                    sem, inc=1, device_id=self.device(axis, self.peer(axis, d)), device_id_type=MESH
                )
                count += 1
        pl.semaphore_wait(sem, count)

    def copy(self, src, dst, axis, value):
        slot = self.used
        self.used += 1
        c = pltpu.make_async_remote_copy(
            src_ref=src,
            dst_ref=dst,
            send_sem=self.send_sem.at[slot],
            recv_sem=self.recv_sem.at[slot],
            device_id=self.device(axis, value),
            device_id_type=MESH,
        )
        c.start()
        return c


class Sum:
    def __init__(self, net, chunk, source, bufs, local_sems, out):
        self.net, self.chunk, self.source, self.out = net, chunk, source, out
        self.own, self.recv, self.gathered = bufs[0], bufs[1:5], bufs[5]
        self.local_sems = local_sems
        self.at = 0
        self.copies, self.loads = [], []

    def next(self):
        steps = (self.core, self.first, self.second, self.third, self.spread_x, self.spread_core, self.leave)
        steps[self.at]()
        self.at += 1

    def wait(self):
        for c in self.copies:
            c.wait()
        self.copies = []

    def piece(self, x, core):
        k = self.chunk
        q = x * 2 + core
        row = pl.multiple_of((q // k.b) * k.r + k.r0, 16)
        col = pl.multiple_of(lax.rem(q, k.b) * k.cols, 128)
        return self.source.at[:, :, pl.ds(row, k.rows), pl.ds(col, k.cols)]

    def core(self):
        net = self.net
        for x in range(net.sizes["x"]):
            other = net.peer("core", 1)
            self.copies.append(net.copy(self.piece(x, other), self.recv[0].at[x], "core", other))
        for x in range(net.sizes["x"]):
            load = pltpu.make_async_copy(
                self.piece(x, net.me["core"]), self.own.at[x], self.local_sems[x]
            )
            load.start()
            self.loads.append(load)

    def first(self):
        for load in self.loads:
            load.wait()
        self.wait()
        self.add(0)
        self.start(1)

    def second(self):
        self.wait()
        self.add(1)
        self.start(2)

    def third(self):
        self.wait()
        self.add(2)
        self.start(3)

    def start(self, stage):
        net, order = self.net, self.chunk.order
        axis, done = order[stage - 1], order[: stage - 1]
        for d in range(1, net.sizes[axis]):
            value = net.peer(axis, d)
            at = [slice(None)] * 3
            for name in done:
                at[DIMS[name]] = net.me[name]
            at[DIMS[axis]] = value
            self.copies.append(
                net.copy(self.own.at[tuple(at)], self.recv[stage].at[d - 1], axis, value)
            )

    def add(self, stage):
        sizes, me = self.net.sizes, self.net.me
        done = self.chunk.order[:stage]
        left = [name for name in ("x", "z", "y") if name not in done]
        terms = 1 if stage == 0 else sizes[done[-1]] - 1

        def body(k, carry):
            at, rest = {name: me[name] for name in done}, k
            for name in reversed(left):
                at[name] = lax.rem(rest, sizes[name])
                rest = rest // sizes[name]
            here = (at["x"], at["z"], at["y"])
            there = tuple(at[name] for name in left)
            if terms == 1 and stage < 3:
                other = self.recv[stage][there if stage == 0 else (0,) + there]
                self.own[here] = self.own[here] + other
                return carry
            value = self.own[here].astype(F32)
            for d in range(terms):
                value = value + self.recv[stage][(d,) + there].astype(F32)
            if stage == 3:
                self.gathered[me["x"] * 2 + me["core"]] = value.astype(BF)
            else:
                self.own[here] = value.astype(BF)
            return carry

        total = math.prod(sizes[name] for name in left)
        if total == 1:
            body(0, 0)
        else:
            lax.fori_loop(0, total, body, 0)

    def spread_x(self):
        self.wait()
        self.add(3)
        net = self.net
        mine = self.gathered.at[net.me["x"] * 2 + net.me["core"]]
        for d in range(1, net.sizes["x"]):
            self.copies.append(net.copy(mine, mine, "x", net.peer("x", d)))

    def spread_core(self):
        self.wait()
        net = self.net
        for x in range(net.sizes["x"]):
            mine = self.gathered.at[x * 2 + net.me["core"]]
            self.copies.append(net.copy(mine, mine, "core", net.peer("core", 1)))

    def leave(self):
        self.wait()
        store = pltpu.make_async_copy(self.gathered, self.out, self.local_sems[0])
        store.start()
        self.loads = [store]

    def end(self):
        while self.at < 7:
            self.next()
        self.loads[0].wait()


class VectorSum:
    def __init__(self, net, value, slots):
        self.net, self.value, self.slots = net, value, slots
        self.left = [name for name, size in net.sizes.items() if size > 1]
        self.copies = []

    def next(self):
        if self.copies:
            for c in self.copies:
                c.wait()
            total = self.now[0]
            for i in range(1, self.net.sizes[self.axis]):
                total = total + self.now[i]
            self.value[...] = total
            self.copies = []
        if self.left:
            net, self.axis = self.net, self.left.pop(0)
            self.now = self.slots[self.axis]
            mine = self.now.at[net.me[self.axis]]
            self.now[net.me[self.axis]] = self.value[...]
            for d in range(1, net.sizes[self.axis]):
                self.copies.append(net.copy(mine, mine, self.axis, net.peer(self.axis, d)))

    def end(self):
        while self.left or self.copies:
            self.next()


PROWS = ROWS + 16
SLOT = {"out": 0, "unit_0": 1, "unit_1": 2, "unit_2": 0}


def attn_unit_back(u, half, qbuf, slot, ags, dqs):
    def image(i, near, ags, dqs):
        r0 = near * KEEP
        valid = lax.broadcasted_iota(jnp.int32, (PADK, UNIT), 0) < KEEP
        q, k, v = (qbuf[slot, i, :, c * UNIT : (c + 1) * UNIT] for c in range(3))
        q_diag = block_diag(q * BF(0.125))
        probs = soft(dot(k, q_diag, NT), 0)
        probs_in = probs.astype(BF)
        agrad = jnp.where(valid, ags[r0 : r0 + PADK, u * UNIT : (u + 1) * UNIT], 0.0).astype(BF)
        a_diag = block_diag(agrad)
        pgrad = dot(v, a_diag, NT)
        inner = jnp.sum(probs * pgrad, axis=0, keepdims=True)
        sgrad = (probs * (pgrad - inner)).astype(BF)
        whole_q = dot(sgrad, k, TN)
        qgrad = 0.125 * jnp.concatenate(
            [
                fold_pair(whole_q[e * 2 * PADK : (e + 1) * 2 * PADK, e * PAIR : (e + 1) * PAIR])
                for e in range(2)
            ],
            axis=1,
        )
        for c, grad in enumerate((qgrad, dot(sgrad, q_diag), dot(probs_in, a_diag))):
            dqs[r0 : r0 + 56, c * UNIT : (c + 1) * UNIT] = grad[:56]

    rows = pl.ds(half * HROWS, HROWS + 16)
    each_image(HALF, image, ags.at[rows], dqs.at[rows])


def back_kernel(sizes, table, *refs):
    names = list(table)
    (
        hgrad_in, att_in, qkvp_in, x_in, wout_in, wqkv_in, w2g_in, w1g_in, weg_in,
        gain_ref, shift_ref, ln2g_ref, ln2s_ref, b2_ref, b1_ref, ebias_ref, mask_ref,
    ) = refs[:17]
    pgrad_out, vec_ref = refs[17:19]
    outs, refs = refs[19 : 19 + len(names)], refs[19 + len(names) :]
    (
        wide_a, ags, dqs, tall, qbuf, wout, wqkv, rows_b, wgs, load_sem, send_sem, recv_sem, local_sem,
    ) = refs[:13]
    refs = refs[13:]
    vec_slots = {name: refs[i] for i, name in enumerate(sizes)}
    refs = refs[len(sizes) :]

    net = Net(sizes, send_sem, recv_sem)
    net.barrier()
    sources = {"fc2": w2g_in, "fc1": w1g_in, "embed": weg_in}
    sums = {}
    for i, name in enumerate(names):
        key = name.split("_")[0]
        source = wgs.at[SLOT[name]] if name in SLOT else sources[key]
        sums[name] = Sum(
            net,
            table[name],
            source,
            refs[6 * i : 6 * (i + 1)],
            [local_sem.at[i * sizes["x"] + x] for x in range(sizes["x"])],
            outs[i],
        )
    fc2 = [sums[n] for n in names if n.startswith("fc2")]
    fc1 = [sums[n] for n in names if n.startswith("fc1")]
    embed, out = sums["embed"], sums["out"]
    units = [sums[f"unit_{u}"] for u in range(UNITS)]

    def each(*items):
        for item in items:
            item.next()

    def load(src, dst, slot):
        c = pltpu.make_async_copy(src, dst, load_sem.at[slot])
        c.start()
        return c

    hg_load = load(hgrad_in, wide_a, 0)
    wout_load = load(wout_in, wout, 1)
    att_load = load(att_in, tall, 2)
    each(*fc2)
    q_loads = []

    def load_next():
        k = len(q_loads)
        if k < 2 * UNITS:
            part = qkvp_in.at[k // 2, pl.ds((k % 2) * HALF, HALF)]
            q_loads.append(load(part, qbuf.at[k % 2], 10 + k))

    load_next()
    wqkv_load = load(wqkv_in, wqkv, 5)
    each(*fc1, embed)

    blocks = sizes["y"] * sizes["z"]
    block_rows = D // blocks

    def put_grad(slot, cols, value):
        for t in range(blocks):
            wgs[slot, t // sizes["y"], t % sizes["y"], :block_rows, cols] = value[
                t * block_rows : (t + 1) * block_rows
            ].astype(BF)

    if table["out"].padded > block_rows:
        pad = table["out"].padded - block_rows
        wgs[:, :, :, block_rows:, :] = jnp.zeros((3, sizes["z"], sizes["y"], pad, D), BF)

    vec_ref[...] = jnp.zeros_like(vec_ref)
    hg_load.wait()
    wout_load.wait()
    halves = [slice(0, HROWS), slice(HROWS, ROWS)]
    for rows in halves:
        branch = wide_a[rows, :].astype(BF)
        rows_b[rows, :] = branch
        vec_ref[4:5] += col_sum(branch.astype(F32))
        ags[rows, :] = dot(branch, wout[...], NT)
    ags[ROWS:, :] = jnp.zeros((PROWS - ROWS, D), F32)
    att_load.wait()
    for c in range(3):
        cols = slice(c * UNIT, (c + 1) * UNIT)
        put_grad(0, cols, dot(tall[...], rows_b[:, cols], TN))
    x_load = load(x_in, rows_b, 3)
    each(out)
    each(*fc2)
    x_load.wait()
    for rows in halves:
        unit, _ = norm(rows_b[rows, :].astype(F32))
        tall[rows, :] = (unit * gain_ref[...] + shift_ref[...]).astype(BF)

    def unit_products(u):
        for c in range(3):
            rows_b[:, c * UNIT : (c + 1) * UNIT] = dqs[:ROWS, c * UNIT : (c + 1) * UNIT].astype(BF)
        for c in range(3):
            cols = slice(c * UNIT, (c + 1) * UNIT)
            put_grad(SLOT[f"unit_{u}"], cols, dot(tall[...], rows_b[:, cols], TN))
        for c, row in ((0, 2), (2, 3)):
            vec_ref[row : row + 1, u * UNIT : (u + 1) * UNIT] = col_sum(
                rows_b[:, c * UNIT : (c + 1) * UNIT].astype(F32)
            )

    def unit_first_grad(u):
        for rows in halves:
            total = None
            for c in range(3):
                weight = wqkv[:, c * D + u * UNIT : c * D + (u + 1) * UNIT]
                term = dot(rows_b[rows, c * UNIT : (c + 1) * UNIT], weight, NT)
                total = term if total is None else total + term
            wide_a[rows, :] = total if u == 0 else wide_a[rows, :] + total

    def unit_step(u):
        for half in range(2):
            q_loads[2 * u + half].wait()
            load_next()
            attn_unit_back(u, half, qbuf, half, ags, dqs)

    unit_step(0)
    each(*fc1, embed)
    unit_products(0)
    each(units[0])
    wqkv_load.wait()
    unit_first_grad(0)
    each(out)
    unit_step(1)
    each(*fc2)
    unit_products(1)
    each(units[1])
    unit_first_grad(1)
    each(units[0])
    unit_step(2)
    hg_again = load(hgrad_in, ags.at[pl.ds(0, ROWS)], 8)
    each(*fc1, embed, out)
    unit_products(2)
    each(units[2])
    each(*fc2)
    each(units[1])
    unit_first_grad(2)
    x_again = load(x_in, rows_b, 6)
    each(units[2])
    each(units[0])
    hg_again.wait()
    x_again.wait()
    stores = []
    for h, rows in enumerate(halves):
        unit, inv = norm(rows_b[rows, :].astype(F32))
        grad = wide_a[rows, :]
        vec_ref[0:1] += col_sum(grad * unit)
        vec_ref[1:2] += col_sum(grad)
        tall[rows, :] = (ags[rows, :] + norm_back(unit, inv, grad, gain_ref[...])).astype(BF)
    stores.append(load(tall, pgrad_out, 9))
    vec_ref[5:6] = ln2g_ref[...]
    vec_ref[6:7] = ln2s_ref[...]
    vec_ref[7:8] = b2_ref[...]
    for i in range(4):
        vec_ref[8 + i : 9 + i] = b1_ref[:, i * D : (i + 1) * D]
    vec_ref[12:13, :DEC] = ebias_ref[...]
    vec_ref[13:14, :DEC] = mask_ref[:1]
    vec = VectorSum(net, vec_ref, vec_slots)
    each(vec)
    each(*fc1, embed, out)
    each(*fc2)
    each(vec)
    each(units[1])
    each(units[2])
    each(units[0])
    each(*fc1, embed, out)
    each(vec)
    each(*fc2)
    each(units[1])
    each(units[2])
    each(units[0])
    each(vec)
    each(*fc1, embed, out)
    each(*fc2)
    each(units[1])
    each(units[2])
    each(units[0])
    vec.end()
    for item in sums.values():
        item.end()
    for store in stores:
        store.wait()


def attn_back_and_sums(
    hgrad, att, qkvp, x, wout, wqkv, w2g, w1g, weg, gain, shift, ln2g, ln2s, b2, b1, ebias, mask_rows,
):
    dp_count, seq_count = lax.axis_size("dp"), lax.axis_size("seq")
    sizes = axis_sizes(dp_count, seq_count)
    table = chunk_table(dp_count, seq_count)
    nz, ny = sizes["z"], sizes["y"]
    blocked = lambda v: v.reshape(nz, ny, v.shape[0] // seq_count, v.shape[1])
    weg = weg.reshape(nz, ny, D // seq_count, DEC)
    pad = table["embed"].padded - D // seq_count
    if pad:
        weg = jnp.pad(weg, ((0, 0), (0, 0), (0, pad), (0, 0)))
    scratch = [
        pltpu.VMEM((ROWS, D), F32),
        pltpu.VMEM((PROWS, D), F32),
        pltpu.VMEM((PROWS, D), F32),
        pltpu.VMEM((ROWS, D), BF),
        pltpu.VMEM((2, HALF, PADK, 3 * UNIT), BF),
        pltpu.VMEM((D, D), BF),
        pltpu.VMEM((D, 3 * D), BF),
        pltpu.VMEM((ROWS, D), BF),
        pltpu.VMEM((3, nz, ny, table["out"].padded, D), BF),
        pltpu.SemaphoreType.DMA((16,)),
    ]
    copies = sum(sizes["x"] * 3 + sizes["y"] + sizes["z"] for _ in table)
    copies += sum(sizes.values())
    scratch += [
        pltpu.SemaphoreType.DMA((copies,)),
        pltpu.SemaphoreType.DMA((copies,)),
        pltpu.SemaphoreType.DMA((len(table) * sizes["x"],)),
    ]
    scratch += [pltpu.VMEM((size, VROWS, D), F32) for size in sizes.values()]
    for chunk in table.values():
        scratch += chunk.scratch(sizes)
    anywhere = pl.BlockSpec(memory_space=pl.ANY)
    vmem = pl.BlockSpec(memory_space=pltpu.VMEM)
    outs = pl.pallas_call(
        functools.partial(back_kernel, sizes, table),
        in_specs=[anywhere] * 9 + [vmem] * 8,
        out_specs=[anywhere, vmem] + [anywhere] * len(table),
        out_shape=[
            jax.ShapeDtypeStruct((ROWS, D), BF),
            jax.ShapeDtypeStruct((VROWS, D), F32),
        ]
        + [jax.ShapeDtypeStruct((dp_count, c.rows, c.cols), BF) for c in table.values()],
        scratch_shapes=scratch,
        compiler_params=pltpu.CompilerParams(
            collective_id=0, has_side_effects=True, vmem_limit_bytes=63 * MIB
        ),
        name="attn_back_and_sums",
    )(
        hgrad, att, qkvp, x, wout, wqkv, blocked(w2g), blocked(w1g), weg,
        gain, shift, ln2g, ln2s, b2, b1, ebias, mask_rows,
    )
    return outs[0], outs[1], outs[2:]


def finish_kernel(seq_count, slots, table, *refs):
    code_ref, arrived_ref, mask_ref, vec_ref = refs[:4]
    parts, refs = refs[4 : 4 + len(table)], refs[4 + len(table) :]
    out_ref, w2_ref, w1_ref, we_ref, wo_ref, wqkv_ref, rows_ref, b1_ref, dec_ref = refs
    t = pl.program_id(0)
    place_kernel(seq_count, slots, code_ref, arrived_ref, mask_ref, out_ref)

    @pl.when(t == 0)
    def _():
        def pieces(name):
            chunk, ref = table[name], parts[list(table).index(name)]
            for q in range(chunk.a * chunk.b):
                row, col = (q // chunk.b) * chunk.r + chunk.r0, (q % chunk.b) * chunk.cols
                yield row, col, ref[q].astype(F32)

        for name, ref in (("fc2", w2_ref), ("fc1", w1_ref), ("embed", we_ref), ("out", wo_ref)):
            for key in table:
                if key.split("_")[0] == name:
                    for row, col, value in pieces(key):
                        rows = min(value.shape[0], ref.shape[0] - row)
                        if rows > 0:
                            ref[row : row + rows, col : col + value.shape[1]] = value[:rows]
        for u in range(UNITS):
            for row, col, value in pieces(f"unit_{u}"):
                rows = min(value.shape[0], wqkv_ref.shape[0] - row)
                if rows > 0:
                    for i in range(value.shape[1] // 128):
                        c, within = (col + i * 128) // UNIT, (col + i * 128) % UNIT
                        to = c * D + u * UNIT + within
                        wqkv_ref[row : row + rows, to : to + 128] = value[
                            :rows, i * 128 : (i + 1) * 128
                        ]

        me = lax.axis_index("seq")

        def mine(row, size, first):
            shift = lax.rem(D - first, D)
            return pltpu.roll(vec_ref[row : row + 8], shift, 1)[:, :size]

        rows_ref[...] = mine(0, D // seq_count, me * (D // seq_count))
        per = seq_count // 4
        chosen = mine(8, FF // seq_count, lax.rem(me, per) * (FF // seq_count))
        at = lax.broadcasted_iota(jnp.int32, chosen.shape, 0)
        b1_ref[...] = jnp.sum(jnp.where(at == me // per, chosen, 0.0), axis=0, keepdims=True)
        dec_ref[...] = mine(8, DEC // seq_count, me * (DEC // seq_count))


def finish(seq_count, slots, code, arrived, mask_token, vec, parts, table):
    def share(rows, cols):
        return jax.ShapeDtypeStruct((rows // seq_count, cols), F32)

    out_shape = [
        jax.ShapeDtypeStruct((PATCHES * IMG, DEC), BF),
        share(FF, D),
        share(D, FF),
        share(D, DEC),
        share(D, D),
        share(D, 3 * D),
        jax.ShapeDtypeStruct((8, D // seq_count), F32),
        jax.ShapeDtypeStruct((1, FF // seq_count), F32),
        jax.ShapeDtypeStruct((8, DEC // seq_count), F32),
    ]
    return pl.pallas_call(
        functools.partial(finish_kernel, seq_count, slots, table),
        grid=(seq_count,),
        in_specs=[
            pl.BlockSpec((1, 1, code.shape[2]), lambda t: (t, 0, 0)),
            pl.BlockSpec((slots, IMG, DEC), lambda t: (t, 0, 0)),
            whole((1, DEC)),
            whole(vec.shape),
        ]
        + [whole(p.shape) for p in parts],
        out_specs=[whole(s.shape) for s in out_shape],
        out_shape=out_shape,
        compiler_params=params(),
        name="finish",
    )(code, arrived, mask_token, vec, *parts)


def decoder_codes(keep_index, slots):
    seq_count = lax.axis_size("seq")
    dev_blocks, _, padded = owner_blocks(seq_count)
    t = jnp.arange(seq_count, dtype=jnp.int32)
    start = first_block(seq_count, t)
    lowest = (lax.axis_index("seq") * PATCHES + start) // seq_count
    m = jnp.arange(padded, dtype=jnp.int32)
    valid = (start[:, None] + m[None, :] * seq_count) < dev_blocks
    place_at = (lowest[:, None] + m[None, :])[None, :, :, None]
    kept = keep_index.T.reshape(KEEP, seq_count, 1, IMG)
    hit = jnp.sum((kept == place_at).astype(jnp.int32), axis=0)
    below = (kept < place_at) & (kept >= lowest[None, :, None, None])
    rank = jnp.sum(below.astype(jnp.int32), axis=0)
    image = jnp.arange(IMG, dtype=jnp.int32)
    code = jnp.where(hit > 0, rank * IMG + image, slots * IMG)
    code = jnp.where(valid[:, :, None], code, -1)
    return code.reshape(seq_count, 1, padded * IMG)


def image_codes(keep_index, slots):
    seq_count = lax.axis_size("seq")
    group_imgs = keep_index.shape[0]
    at = lax.axis_index("seq") * IMG
    own = lax.dynamic_slice_in_dim(keep_index, at, IMG, 0)
    image = jnp.arange(IMG, dtype=jnp.int32)[:, None]
    owner = (own * group_imgs + at + image) // (IMG * PATCHES)
    lower = jnp.sum((owner[:, None, :] < owner[:, :, None]).astype(jnp.int32), axis=2)
    rank = jnp.arange(KEEP, dtype=jnp.int32)[None, :] - lower
    code = (owner * slots + rank) * HALF + image % HALF
    return code.reshape(2, 1, HROWS)


def local(
    patches,
    keep_index,
    ln1_gain,
    ln1_shift,
    w_qkv,
    q_bias,
    v_bias,
    w_out,
    out_bias,
    ln2_gain,
    ln2_shift,
    w_fc1,
    fc1_bias,
    w_fc2,
    fc2_bias,
    w_embed,
    embed_bias,
    mask_token,
    decoder_grad,
):
    seq_count = lax.axis_size("seq")
    slots = 2 * KEEP // seq_count
    row = lambda v: v.reshape(1, -1)
    dec_code = decoder_codes(keep_index, slots)
    img_code = image_codes(keep_index, slots)
    grad_slots, mask_rows = pick(seq_count, slots, dec_code, decoder_grad)
    returned = lax.all_to_all(grad_slots, "seq", split_axis=0, concat_axis=0, tiled=True)

    qkv_bias = jnp.concatenate([q_bias, jnp.zeros_like(q_bias), v_bias])
    qkvp, attended, hidden = attn_fwd(
        patches, row(ln1_gain), row(ln1_shift), w_qkv, row(qkv_bias), w_out, row(out_bias)
    )
    active, slope, block_in, embedded = mlp_fwd(
        hidden, row(ln2_gain), row(ln2_shift), w_fc1, row(fc1_bias), w_fc2, row(fc2_bias),
        w_embed, row(embed_bias),
    )
    send = pack(img_code, embedded, seq_count * slots)
    arrived = lax.all_to_all(send, "seq", split_axis=0, concat_axis=0, tiled=True)

    embed_grad = unpack(img_code, returned)
    hgrad, weg, ebias, w2g, b2, w1g, b1, ln2g, ln2s = mlp_bwd(
        embed_grad, block_in, hidden, row(ln2_gain), row(ln2_shift), w_embed, active, slope,
        w_fc2, w_fc1,
    )
    patches_grad, vec, parts = attn_back_and_sums(
        hgrad, attended, qkvp, patches, w_out, w_qkv, w2g, w1g, weg,
        row(ln1_gain), row(ln1_shift), ln2g, ln2s, b2, b1, ebias, mask_rows,
    )
    table = chunk_table(lax.axis_size("dp"), seq_count)
    decoder_input, w2g, w1g, weg, woutg, wqkvg, rows, b1, dec_rows = finish(
        seq_count, slots, dec_code, arrived, row(mask_token), vec, parts, table
    )
    ln1g, ln1s, qb, vb, obias, ln2g, ln2s, b2 = (rows[i] for i in range(8))
    b1, ebias, mask_grad = b1[0], dec_rows[4], dec_rows[5]
    return (
        decoder_input,
        patches_grad,
        ln1g,
        ln1s,
        wqkvg,
        qb,
        vb,
        woutg,
        obias,
        ln2g,
        ln2s,
        w1g,
        b1,
        w2g,
        b2,
        weg,
        ebias,
        mask_grad,
    )


def solution(mesh):
    rows = P(("dp", "seq"), None)
    placed = (rows, P("dp", None)) + (P(),) * 16 + (rows,)
    vec, mat = P("seq"), P("seq", None)
    return jax.shard_map(
        local,
        mesh=mesh,
        in_specs=placed,
        out_specs=(
            rows, rows, vec, vec, mat, vec, vec, mat, vec, vec, vec, mat, vec, mat, vec, mat, vec, vec,
        ),
        check_vma=False,
    )
```

```python
import functools
import math

import jax
import jax.numpy as jnp
from jax import lax
from jax.experimental import pallas as pl
from jax.experimental.pallas import tpu as pltpu
from jax.sharding import PartitionSpec as P

D = 768
HEADS = 12
HEAD = 64
FF = 3072
DEC = 512
PATCHES = 196
KEEP = 49
IMG = 32
HALF = 16
ROWS = IMG * KEEP
HROWS = HALF * KEEP
PADK = 64
UNITS = 3
EPSILON = 1e-06
BF = jnp.bfloat16
F32 = jnp.float32
MIB = 1 << 20

NN = (((1,), (0,)), ((), ()))
NT = (((1,), (1,)), ((), ()))
TN = (((0,), (0,)), ((), ()))


def dot(left, right, dims=NN):
    return lax.dot_general(left, right, dims, preferred_element_type=F32)


def params(mib=60):
    return pltpu.CompilerParams(vmem_limit_bytes=mib * MIB)


def whole(shape):
    return pl.BlockSpec(shape, lambda *_: (0,) * len(shape), pipeline_mode=pl.Buffered(1))


def norm(values):
    centered = values - jnp.mean(values, axis=-1, keepdims=True)
    inv = lax.rsqrt(jnp.mean(centered * centered, axis=-1, keepdims=True) + EPSILON)
    return centered * inv, inv


def norm_back(unit, inv, grad, gain):
    f = grad * gain
    return inv * (
        f
        - jnp.mean(f, axis=-1, keepdims=True)
        - unit * jnp.mean(f * unit, axis=-1, keepdims=True)
    )


def col_sum(values):
    return jnp.sum(values, axis=0, keepdims=True)


def gelu_pair(v):
    z = jnp.abs(v) * (1 / math.sqrt(2.0))
    t = 1.0 / (1.0 + 0.3275911 * z)
    e = jnp.exp(-z * z)
    poly = t * (
        0.5 * 0.254829592
        + t
        * (
            0.5 * -0.284496736
            + t * (0.5 * 1.421413741 + t * (0.5 * -1.453152027 + t * (0.5 * 1.061405429)))
        )
    )
    tail = poly * e
    cdf = jnp.where(v >= 0, 1.0 - tail, tail)
    return v * cdf, cdf + v * (e * (1 / math.sqrt(2 * math.pi)))


def one_hot(rows, code):
    at = lax.broadcasted_iota(jnp.int32, (rows, code.shape[1]), 0)
    return jnp.where(at == code, 1.0, 0.0).astype(BF)


def owner_blocks(seq_count):
    dev_blocks = PATCHES
    most = -(-dev_blocks // seq_count)
    return dev_blocks, most, -(-most // 4) * 4


def first_block(seq_count, t):
    return lax.rem(
        t + seq_count - lax.rem(lax.axis_index("seq") * PATCHES, seq_count), seq_count
    )


def pick_kernel(seq_count, slots, code_ref, dec_ref, out_ref, sum_ref):
    t = pl.program_id(0)
    dev_blocks, most, padded = owner_blocks(seq_count)
    start = first_block(seq_count, t)
    pieces = []
    for m in range(most):
        at = start + m * seq_count
        clamped = jnp.minimum(at, dev_blocks - 1)
        pieces.append(dec_ref[pl.ds(pl.multiple_of(clamped * IMG, IMG), IMG), :])
    if padded > most:
        pieces.append(jnp.zeros(((padded - most) * IMG, DEC), BF))
    picked = dot(one_hot(slots * IMG + 16, code_ref[0]), jnp.concatenate(pieces, axis=0))
    out_ref[...] = picked[: slots * IMG].astype(BF).reshape(slots, IMG, DEC)

    @pl.when(t == 0)
    def _():
        sum_ref[...] = jnp.zeros_like(sum_ref)

    sum_ref[...] += picked[slots * IMG : slots * IMG + 8]


def pick(seq_count, slots, code, dec_grad):
    return pl.pallas_call(
        functools.partial(pick_kernel, seq_count, slots),
        grid=(seq_count,),
        in_specs=[
            pl.BlockSpec((1, 1, code.shape[2]), lambda t: (t, 0, 0)),
            whole(dec_grad.shape),
        ],
        out_specs=[
            pl.BlockSpec((slots, IMG, DEC), lambda t: (t, 0, 0)),
            pl.BlockSpec((8, DEC), lambda t: (0, 0)),
        ],
        out_shape=[
            jax.ShapeDtypeStruct((seq_count * slots, IMG, DEC), BF),
            jax.ShapeDtypeStruct((8, DEC), F32),
        ],
        compiler_params=params(),
        name="pick",
    )(code, dec_grad)


def pack_kernel(code_ref, rows_ref, out_ref):
    count = out_ref.shape[0]
    picked = dot(one_hot(count * HALF, code_ref[0]), rows_ref[...])
    out_ref[...] = picked.astype(BF).reshape(count, HALF, DEC)


def pack(code, rows, count):
    return pl.pallas_call(
        pack_kernel,
        grid=(2,),
        in_specs=[
            pl.BlockSpec((1, 1, HROWS), lambda g: (g, 0, 0)),
            pl.BlockSpec((HROWS, DEC), lambda g: (g, 0)),
        ],
        out_specs=pl.BlockSpec((count, HALF, DEC), lambda g: (0, g, 0)),
        out_shape=jax.ShapeDtypeStruct((count, IMG, DEC), BF),
        compiler_params=params(),
        name="pack",
    )(code, rows)


def unpack_kernel(code_ref, slots_ref, out_ref):
    count = slots_ref.shape[0]
    source = slots_ref[...].reshape(count * HALF, DEC)
    out_ref[...] = dot(one_hot(count * HALF, code_ref[0]), source, TN).astype(BF)


def unpack(code, slots):
    count = slots.shape[0]
    return pl.pallas_call(
        unpack_kernel,
        grid=(2,),
        in_specs=[
            pl.BlockSpec((1, 1, HROWS), lambda g: (g, 0, 0)),
            pl.BlockSpec((count, HALF, DEC), lambda g: (0, g, 0)),
        ],
        out_specs=pl.BlockSpec((HROWS, DEC), lambda g: (g, 0)),
        out_shape=jax.ShapeDtypeStruct((ROWS, DEC), BF),
        compiler_params=params(),
        name="unpack",
    )(code, slots)


UNIT = 4 * HEAD
PAIR = 2 * HEAD


def block_diag(rows):
    heads = rows.shape[1] // HEAD
    lane_head = lax.broadcasted_iota(jnp.int32, rows.shape, 1) // HEAD
    zero = jnp.zeros_like(rows)
    return jnp.concatenate([jnp.where(lane_head == h, rows, zero) for h in range(heads)], axis=0)


def fold_pair(rows):
    low = lax.broadcasted_iota(jnp.int32, (PADK, PAIR), 1) < HEAD
    return jnp.where(low, rows[:PADK], rows[PADK:])


def soft(scores, axis):
    valid = lax.broadcasted_iota(jnp.int32, scores.shape, axis) < KEEP
    scores = jnp.where(valid, scores, -1e30)
    e = jnp.exp(scores - jnp.max(scores, axis=axis, keepdims=True))
    return e * (1.0 / jnp.sum(e, axis=axis, keepdims=True))


def each_image(count, image, *refs):
    def group(g, carry):
        base = pl.multiple_of(g * 8 * KEEP, 8)
        views = [ref.at[pl.ds(base, 8 * KEEP + 16)] for ref in refs]
        for near in range(8):
            image(g * 8 + near, near, *views)
        return carry

    lax.fori_loop(0, count // 8, group, 0)


def attn_fwd_kernel(
    x_ref, gain_ref, shift_ref, wqkv_ref, bias_ref, wout_ref, obias_ref,
    qkvp_ref, att_ref, hidden_ref, qs, ats,
):
    x = x_ref[...].astype(F32)
    unit, _ = norm(x)
    first = (unit * gain_ref[...] + shift_ref[...]).astype(BF)
    for c in range(3):
        cols = slice(c * D, (c + 1) * D)
        qs[:HROWS, cols] = (
            (dot(first, wqkv_ref[:, cols]) + bias_ref[cols]).astype(BF).astype(F32)
        )
    qs[HROWS:, :] = jnp.zeros((16, 3 * D), F32)

    def image(i, near, qs, ats):
        r0 = near * KEEP
        for u in range(HEADS // 2):
            part = []
            for c in range(3):
                cols = slice(c * D + u * PAIR, c * D + (u + 1) * PAIR)
                rows = qs[r0 : r0 + PADK, cols].astype(BF)
                to = c * UNIT + (u % 2) * PAIR
                qkvp_ref[u // 2, i, :, to : to + PAIR] = rows
                part.append(rows)
            q, k, v = part
            probs = soft(dot(block_diag(q * BF(0.125)), k, NT), 1).astype(BF)
            out = fold_pair(dot(probs, v))
            ats[r0 : r0 + 56, u * PAIR : (u + 1) * PAIR] = out[:56]

    each_image(HALF, image, qs, ats)
    att = ats[:HROWS, :].astype(BF)
    att_ref[...] = att
    hidden_ref[...] = x_ref[...].astype(F32) + (dot(att, wout_ref[...]) + obias_ref[...])


def attn_fwd(x, gain, shift, wqkv, bias, wout, obias):
    return pl.pallas_call(
        attn_fwd_kernel,
        grid=(2,),
        in_specs=[
            pl.BlockSpec((HROWS, D), lambda g: (g, 0)),
            whole((D,)),
            whole((D,)),
            whole((D, 3 * D)),
            whole((3 * D,)),
            whole((D, D)),
            whole((D,)),
        ],
        out_specs=[
            pl.BlockSpec((UNITS, HALF, PADK, 3 * UNIT), lambda g: (0, g, 0, 0)),
            pl.BlockSpec((HROWS, D), lambda g: (g, 0)),
            pl.BlockSpec((HROWS, D), lambda g: (g, 0)),
        ],
        out_shape=[
            jax.ShapeDtypeStruct((UNITS, IMG, PADK, 3 * UNIT), BF),
            jax.ShapeDtypeStruct((ROWS, D), BF),
            jax.ShapeDtypeStruct((ROWS, D), F32),
        ],
        scratch_shapes=[pltpu.VMEM((HROWS + 16, 3 * D), F32), pltpu.VMEM((HROWS + 16, D), F32)],
        compiler_params=params(),
        name="attn_fwd",
    )(x, gain, shift, wqkv, bias, wout, obias)


FTILE = 512
FSTEPS = FF // FTILE


def mlp_fwd_kernel(
    hidden_ref, gain_ref, shift_ref, w1_ref, b1_ref, w2_ref, b2_ref, we_ref, be_ref,
    act_ref, slope_ref, block_ref, emb_ref, second, acc,
):
    f = pl.program_id(0)

    @pl.when(f == 0)
    def _():
        unit, _ = norm(hidden_ref[...])
        second[...] = (unit * gain_ref[...] + shift_ref[...]).astype(BF)
        acc[...] = hidden_ref[...] + b2_ref[...]

    for h in range(2):
        rows = slice(h * HROWS, (h + 1) * HROWS)
        active, slope = gelu_pair(dot(second[rows, :], w1_ref[...]) + b1_ref[...])
        active = active.astype(BF)
        act_ref[rows, :] = active
        slope_ref[rows, :] = slope.astype(BF)
        acc[rows, :] += dot(active, w2_ref[...])

    @pl.when(f == FSTEPS - 1)
    def _():
        block_in = acc[...].astype(BF)
        block_ref[...] = block_in
        emb_ref[...] = (dot(block_in, we_ref[...]) + be_ref[...]).astype(BF)


def mlp_fwd(hidden, gain, shift, w1, b1, w2, b2, we, be):
    tile = pl.BlockSpec((ROWS, FTILE), lambda f: (0, f))
    return pl.pallas_call(
        mlp_fwd_kernel,
        grid=(FSTEPS,),
        in_specs=[
            whole((ROWS, D)),
            whole((D,)),
            whole((D,)),
            pl.BlockSpec((D, FTILE), lambda f: (0, f)),
            pl.BlockSpec((FTILE,), lambda f: (f,)),
            pl.BlockSpec((FTILE, D), lambda f: (f, 0)),
            whole((D,)),
            whole((D, DEC)),
            whole((DEC,)),
        ],
        out_specs=[tile, tile, whole((ROWS, D)), whole((ROWS, DEC))],
        out_shape=[
            jax.ShapeDtypeStruct((ROWS, FF), BF),
            jax.ShapeDtypeStruct((ROWS, FF), BF),
            jax.ShapeDtypeStruct((ROWS, D), BF),
            jax.ShapeDtypeStruct((ROWS, DEC), BF),
        ],
        scratch_shapes=[pltpu.VMEM((ROWS, D), BF), pltpu.VMEM((ROWS, D), F32)],
        compiler_params=params(),
        name="mlp_fwd",
    )(hidden, gain, shift, w1, b1, w2, b2, we, be)


MESH = pl.DeviceIdType.MESH
ORDERS = (("x", "y", "z"), ("y", "x", "z"))
DIMS = {"x": 0, "z": 1, "y": 2}
VROWS = 16
FC1_PARTS = 3


def axis_sizes(dp_count, seq_count):
    z = 4 if seq_count % 4 == 0 else 1
    return {"core": 2, "x": dp_count // 2, "y": seq_count // z, "z": z}


def cut(dp_count, rows, cols):
    for padded in range(rows, rows + 256, 16):
        for a in range(1, dp_count + 1):
            b = dp_count // a
            if a * b == dp_count and padded % (16 * a) == 0 and cols % (128 * b) == 0:
                return a, b, padded
    raise ValueError("no cut")


class Chunk:
    def __init__(self, dp_count, rows, cols, order, half=0, halves=1, first_col=0):
        self.a, self.b, self.padded = cut(dp_count, rows, cols)
        self.r, self.cols = self.padded // self.a, cols // self.b
        self.rows = self.r // halves
        self.r0, self.c0 = half * self.rows, first_col
        self.order = ORDERS[order]

    def scratch(self, sizes):
        dims = [sizes[name] for name in ("x", "z", "y")]
        shapes = [(*dims, self.rows, self.cols)] * 2
        for stage in range(1, 4):
            left = [sizes[name] for name in ("x", "z", "y") if name not in self.order[:stage]]
            shapes.append((sizes[self.order[stage - 1]] - 1, *left, self.rows, self.cols))
        shapes.append((sizes["x"] * 2, self.rows, self.cols))
        return [pltpu.VMEM(shape, BF) for shape in shapes]


def halves_of(dp_count, rows, cols):
    a, _, padded = cut(dp_count, rows, cols)
    return 2 if (padded // a) % 32 == 0 else 1


def chunk_table(dp_count, seq_count):
    table = {}
    rows, span = D // seq_count, FF // FC1_PARTS
    for i in range(FC1_PARTS):
        table[f"fc1_{i}"] = Chunk(dp_count, rows, span, i % 2, first_col=i * span)
    halves = halves_of(dp_count, FF // seq_count, D)
    for h in range(halves):
        table[f"fc2_{h}"] = Chunk(dp_count, FF // seq_count, D, (h + 1) % 2, h, halves)
    table["embed"] = Chunk(dp_count, rows, DEC, 1)
    for i, name in enumerate(("out", "unit_0", "unit_1", "unit_2")):
        table[name] = Chunk(dp_count, rows, D, (i + 1) % 2)
    return table


class Net:
    def __init__(self, sizes, send_sem, recv_sem):
        self.sizes, self.send_sem, self.recv_sem = sizes, send_sem, recv_sem
        self.used = 0
        dp, sq = lax.axis_index("dp"), lax.axis_index("seq")
        ny = sizes["y"]
        self.me = {"core": lax.rem(dp, 2), "x": dp // 2, "y": lax.rem(sq, ny), "z": sq // ny}

    def device(self, axis, value):
        if axis == "seq":
            return {"dp": lax.axis_index("dp"), "seq": value}
        coord = dict(self.me)
        coord[axis] = value
        return {
            "dp": coord["x"] * 2 + coord["core"],
            "seq": coord["z"] * self.sizes["y"] + coord["y"],
        }

    def peer(self, axis, d):
        return lax.rem(self.me[axis] + d, self.sizes[axis])

    def barrier(self):
        sem, count = pltpu.get_barrier_semaphore(), 0
        for axis, size in self.sizes.items():
            if axis in ("core", "x"):
                for d in range(1, size):
                    pl.semaphore_signal(
                        sem, inc=1, device_id=self.device(axis, self.peer(axis, d)), device_id_type=MESH
                    )
                    count += 1
        seq_count = self.sizes["y"] * self.sizes["z"]
        for d in range(1, seq_count):
            to = lax.rem(lax.axis_index("seq") + d, seq_count)
            pl.semaphore_signal(sem, inc=1, device_id=self.device("seq", to), device_id_type=MESH)
            count += 1
        pl.semaphore_wait(sem, count)

    def copy(self, what):
        slot = self.used
        self.used += 1

        def make():
            src, dst, axis, value = what()
            return pltpu.make_async_remote_copy(
                src_ref=src,
                dst_ref=dst,
                send_sem=self.send_sem.at[slot],
                recv_sem=self.recv_sem.at[slot],
                device_id=self.device(axis, value),
                device_id_type=MESH,
            )

        make().start()
        return make


class Sum:
    def __init__(self, net, chunk, source, bufs, local_sems, out):
        self.net, self.chunk, self.source, self.out = net, chunk, source, out
        self.own, self.recv, self.gathered = bufs[0], bufs[1:5], bufs[5]
        self.local_sems = local_sems
        self.at = 0
        self.copies, self.loads = [], []

    def next(self):
        steps = (self.core, self.first, self.second, self.third, self.spread_x, self.spread_core, self.leave)
        if self.at < len(steps):
            steps[self.at]()
            self.at += 1

    def wait(self):
        for make in self.copies:
            make().wait()
        self.copies = []

    def piece(self, x, core):
        k = self.chunk
        q = x * 2 + core
        row = pl.multiple_of((q // k.b) * k.r + k.r0, 16)
        col = pl.multiple_of(k.c0 + lax.rem(q, k.b) * k.cols, 128)
        return self.source.at[:, :, pl.ds(row, k.rows), pl.ds(col, k.cols)]

    def core(self):
        net = self.net

        def send(x):
            other = net.peer("core", 1)
            return self.piece(x, other), self.recv[0].at[x], "core", other

        def load(x):
            return pltpu.make_async_copy(
                self.piece(x, net.me["core"]), self.own.at[x], self.local_sems[x]
            )

        for x in range(net.sizes["x"]):
            self.copies.append(net.copy(functools.partial(send, x)))
        for x in range(net.sizes["x"]):
            load(x).start()
            self.loads.append(functools.partial(load, x))

    def first(self):
        for load in self.loads:
            load().wait()
        self.wait()
        self.add(0)
        self.start(1)

    def second(self):
        self.wait()
        self.add(1)
        self.start(2)

    def third(self):
        self.wait()
        self.add(2)
        self.start(3)

    def start(self, stage):
        net, order = self.net, self.chunk.order
        axis, done = order[stage - 1], order[: stage - 1]

        def send(d):
            value = net.peer(axis, d)
            at = [slice(None)] * 3
            for name in done:
                at[DIMS[name]] = net.me[name]
            at[DIMS[axis]] = value
            return self.own.at[tuple(at)], self.recv[stage].at[d - 1], axis, value

        for d in range(1, net.sizes[axis]):
            self.copies.append(net.copy(functools.partial(send, d)))

    def add(self, stage):
        sizes, me = self.net.sizes, self.net.me
        done = self.chunk.order[:stage]
        left = [name for name in ("x", "z", "y") if name not in done]
        terms = 1 if stage == 0 else sizes[done[-1]] - 1

        def body(k, carry):
            at, rest = {name: me[name] for name in done}, k
            for name in reversed(left):
                at[name] = lax.rem(rest, sizes[name])
                rest = rest // sizes[name]
            here = (at["x"], at["z"], at["y"])
            there = tuple(at[name] for name in left)
            if terms == 1 and stage < 3:
                other = self.recv[stage][there if stage == 0 else (0,) + there]
                self.own[here] = self.own[here] + other
                return carry
            value = self.own[here].astype(F32)
            for d in range(terms):
                value = value + self.recv[stage][(d,) + there].astype(F32)
            if stage == 3:
                self.gathered[me["x"] * 2 + me["core"]] = value.astype(BF)
            else:
                self.own[here] = value.astype(BF)
            return carry

        total = math.prod(sizes[name] for name in left)
        if total == 1:
            body(0, 0)
        else:
            lax.fori_loop(0, total, body, 0)

    def spread_x(self):
        self.wait()
        self.add(3)
        net = self.net

        def send(d):
            mine = self.gathered.at[net.me["x"] * 2 + net.me["core"]]
            return mine, mine, "x", net.peer("x", d)

        for d in range(1, net.sizes["x"]):
            self.copies.append(net.copy(functools.partial(send, d)))

    def spread_core(self):
        self.wait()
        net = self.net

        def send(x):
            mine = self.gathered.at[x * 2 + net.me["core"]]
            return mine, mine, "core", net.peer("core", 1)

        for x in range(net.sizes["x"]):
            self.copies.append(net.copy(functools.partial(send, x)))

    def leave(self):
        self.wait()

        def store():
            return pltpu.make_async_copy(self.gathered, self.out, self.local_sems[0])

        store().start()
        self.loads = [store]

    def end(self):
        while self.at < 7:
            self.next()
        self.loads[0]().wait()


class VectorSum:
    def __init__(self, net, value, slots):
        self.net, self.value, self.slots = net, value, slots
        self.left = [name for name, size in net.sizes.items() if size > 1]
        self.copies = []

    def next(self):
        net = self.net
        if self.copies:
            for make in self.copies:
                make().wait()
            total = self.now[0]
            for i in range(1, net.sizes[self.axis]):
                total = total + self.now[i]
            self.value[...] = total
            self.copies = []
        if self.left:
            axis = self.axis = self.left.pop(0)
            now = self.now = self.slots[axis]
            now[net.me[axis]] = self.value[...]

            def send(d):
                mine = now.at[net.me[axis]]
                return mine, mine, axis, net.peer(axis, d)

            for d in range(1, net.sizes[axis]):
                self.copies.append(net.copy(functools.partial(send, d)))

    def end(self):
        while self.left or self.copies:
            self.next()


PROWS = ROWS + 16
SLOT = {"out": 0, "unit_0": 1, "unit_1": 2, "unit_2": 0}


def attn_unit_back(u, half, qbuf, slot, ags, dqs):
    def image(i, near, ags, dqs):
        r0 = near * KEEP
        valid = lax.broadcasted_iota(jnp.int32, (PADK, UNIT), 0) < KEEP
        q, k, v = (qbuf[slot, i, :, c * UNIT : (c + 1) * UNIT] for c in range(3))
        q_diag = block_diag(q * BF(0.125))
        probs = soft(dot(k, q_diag, NT), 0)
        probs_in = probs.astype(BF)
        agrad = jnp.where(valid, ags[r0 : r0 + PADK, u * UNIT : (u + 1) * UNIT], 0.0).astype(BF)
        a_diag = block_diag(agrad)
        pgrad = dot(v, a_diag, NT)
        inner = jnp.sum(probs * pgrad, axis=0, keepdims=True)
        sgrad = (probs * (pgrad - inner)).astype(BF)
        whole_q = dot(sgrad, k, TN)
        qgrad = 0.125 * jnp.concatenate(
            [
                fold_pair(whole_q[e * 2 * PADK : (e + 1) * 2 * PADK, e * PAIR : (e + 1) * PAIR])
                for e in range(2)
            ],
            axis=1,
        )
        for c, grad in enumerate((qgrad, dot(sgrad, q_diag), dot(probs_in, a_diag))):
            dqs[r0 : r0 + 56, c * UNIT : (c + 1) * UNIT] = grad[:56]

    rows = pl.ds(half * HROWS, HROWS + 16)
    each_image(HALF, image, ags.at[rows], dqs.at[rows])


BT = 512
TILES = FF // BT


def back_kernel(sizes, table, *refs):
    names = list(table)
    (
        egrad_in, block_in, hidden_in, act_in, slope_in, we_in, w2_in, w1_in, att_in, qkvp_in, x_in, wout_in, wqkv_in,
        send_in, gain1_ref, shift1_ref, gain2_ref, shift2_ref, mask_ref, code_ref, token_ref,
    ) = refs[:21]
    pgrad_out, vec_ref, dec_out, hgrad_hbm, w2g_hbm, w1g_hbm, weg_hbm, arrived = refs[21:29]
    outs, refs = refs[29 : 29 + len(names)], refs[29 + len(names) :]
    (
        wide_a, ags, dqs, tall, rows_b, wgs, b1_ref, load_sem, tile_sem, store_sem, send_sem, recv_sem, local_sem,
    ) = refs[:13]
    refs = refs[13:]
    vec_slots = {name: refs[i] for i, name in enumerate(sizes)}
    refs = refs[len(sizes) :]

    net = Net(sizes, send_sem, recv_sem)
    net.barrier()
    seq_count = sizes["y"] * sizes["z"]
    slots = arrived.shape[0] // seq_count
    seq_me = lax.axis_index("seq")

    def slot_rows(owner):
        return pl.ds(owner * slots, slots)

    def slot_send(d):
        to = lax.rem(seq_me + d, seq_count)
        return send_in.at[slot_rows(to)], arrived.at[slot_rows(seq_me)], "seq", to

    slot_copies = [net.copy(functools.partial(slot_send, d)) for d in range(1, seq_count)]

    def own_slots():
        return pltpu.make_async_copy(
            send_in.at[slot_rows(seq_me)], arrived.at[slot_rows(seq_me)], load_sem.at[2]
        )

    own_slots().start()
    sources = {"fc2": w2g_hbm, "fc1": w1g_hbm, "embed": weg_hbm}
    sums = {}
    for i, name in enumerate(names):
        sums[name] = Sum(
            net,
            table[name],
            wgs.at[SLOT[name]] if name in SLOT else sources[name.split("_")[0]],
            refs[6 * i : 6 * (i + 1)],
            [local_sem.at[i * sizes["x"] + x] for x in range(sizes["x"])],
            outs[i],
        )
    fc2 = [sums.get(f"fc2_{h}") for h in range(2)]
    fc1 = [sums[n] for n in names if n.startswith("fc1")]
    embed, out = sums["embed"], sums["out"]
    units = [sums[f"unit_{u}"] for u in range(UNITS)]

    def each(*items):
        for item in items:
            if item is not None:
                item.next()

    def load(src, dst, slot):
        c = pltpu.make_async_copy(src, dst, load_sem.at[slot])
        c.start()
        return c

    ny, blocks = sizes["y"], sizes["y"] * sizes["z"]
    block_rows = D // blocks
    halves = [slice(0, HROWS), slice(HROWS, ROWS)]

    def put_blocks(ref, cols, value):
        for t in range(blocks):
            ref[t // ny, t % ny, :block_rows, cols] = value[
                t * block_rows : (t + 1) * block_rows
            ].astype(BF)

    def clear_padding(ref):
        pad = ref.shape[-2] - block_rows
        if pad:
            ref[..., block_rows:, :] = jnp.zeros((*ref.shape[:-2], pad, ref.shape[-1]), BF)

    clear_padding(wgs)
    vec_ref[...] = jnp.zeros_like(vec_ref)
    vec_ref[13:14, :DEC] = mask_ref[:1]

    third = FF // blocks // 3

    def columns(k):
        return pl.ds(pl.multiple_of(k * BT, BT), BT)

    hidden_load = load(hidden_in, ags.at[pl.ds(0, ROWS)], 3)

    def embedding(egrad, block, we, weg):
        clear_padding(weg)
        eg_load = load(egrad_in, egrad, 0)
        we_load = load(we_in, we, 1)
        block_load = load(block_in, block, 4)
        eg_load.wait()
        we_load.wait()
        for rows in halves:
            out_grad = dot(egrad[rows, :], we[...], NT)
            wide_a[rows, :] = out_grad
            two = out_grad.astype(BF)
            rows_b[rows, :] = two
            vec_ref[7:8] += col_sum(two.astype(F32))
            vec_ref[12:13, :DEC] += col_sum(egrad[rows, :].astype(F32))
        block_load.wait()
        put_blocks(weg, slice(None), dot(block[...], egrad[...], TN))
        load(weg, weg_hbm, 5).wait()
        each(embed)

    pl.run_scoped(
        embedding,
        pltpu.VMEM((ROWS, DEC), BF),
        pltpu.VMEM((ROWS, D), BF),
        pltpu.VMEM((D, DEC), BF),
        pltpu.VMEM(weg_hbm.shape, BF),
    )

    def second_weight(acts, stage):
        def act_load(k, slot):
            return pltpu.make_async_copy(act_in.at[:, columns(k)], acts.at[slot], tile_sem.at[slot])

        def stores(k, slot):
            copies = []
            for i in range(BT // third):
                block = k * (BT // third) + i
                owner = block // 3
                rows = pl.ds(pl.multiple_of(lax.rem(block, 3) * third, third), third)
                copies.append(
                    pltpu.make_async_copy(
                        stage.at[slot, pl.ds(i * third, third)],
                        w2g_hbm.at[owner // ny, lax.rem(owner, ny), rows],
                        store_sem.at[slot * (BT // third) + i],
                    )
                )
            return copies

        act_load(0, 0).start()

        def tile(k, carry):
            slot = lax.rem(k, 2)
            act_load(k, slot).wait()

            @pl.when(k + 1 < TILES)
            def _():
                act_load(k + 1, 1 - slot).start()

            @pl.when(k >= 2)
            def _():
                for c in stores(k - 2, slot):
                    c.wait()

            stage[slot] = dot(acts[slot], rows_b[...], TN).astype(BF)
            for c in stores(k, slot):
                c.start()
            return carry

        lax.fori_loop(0, TILES, tile, 0)
        for k in (TILES - 2, TILES - 1):
            for c in stores(k, k % 2):
                c.wait()

    pl.run_scoped(second_weight, pltpu.VMEM((2, ROWS, BT), BF), pltpu.VMEM((2, BT, D), BF))
    each(*fc2, embed)

    def first_weight(slopes, w2s, w1s, stage):
        def loads(k, slot):
            pairs = (
                (slope_in.at[:, columns(k)], slopes),
                (w2_in.at[columns(k), :], w2s),
                (w1_in.at[:, columns(k)], w1s),
            )
            return [
                pltpu.make_async_copy(src, dst.at[slot], tile_sem.at[slot * 3 + i])
                for i, (src, dst) in enumerate(pairs)
            ]

        def store(k):
            return pltpu.make_async_copy(stage, w1g_hbm.at[:, :, :, columns(k)], store_sem.at[0])

        per = TILES // FC1_PARTS
        for c in loads(0, 0):
            c.start()
        hidden_load.wait()
        for rows in halves:
            unit, _ = norm(ags[rows, :])
            tall[:, rows] = (unit * gain2_ref[...] + shift2_ref[...]).astype(BF).T
        dqs[...] = jnp.zeros_like(dqs)

        def tile(k, carry):
            slot = lax.rem(k, 2)
            for c in loads(k, slot):
                c.wait()

            @pl.when(k + 1 < TILES)
            def _():
                for c in loads(k + 1, 1 - slot):
                    c.start()

            inner = (dot(rows_b[...], w2s[slot], NT) * slopes[slot].astype(F32)).astype(BF)
            b1_ref[:, columns(k)] = col_sum(inner.astype(F32))
            grad = dot(tall[...], inner)

            @pl.when(lax.rem(k, per) > 0)
            def _():
                store(k - 1).wait()

            put_blocks(stage, slice(None), grad)
            store(k).start()
            dqs[:ROWS, :] += dot(inner, w1s[slot], NT)
            return carry

        for part in range(FC1_PARTS):
            lax.fori_loop(part * per, (part + 1) * per, tile, 0)
            store((part + 1) * per - 1).wait()
            if part == 0:
                each(fc1[0], embed, *fc2)
            if part == 1:
                each(fc1[1], embed, fc1[0])
            if part == 2:
                each(fc1[2], fc2[1], fc1[1])

    pl.run_scoped(
        first_weight,
        pltpu.VMEM((2, ROWS, BT), BF),
        pltpu.VMEM((2, BT, D), BF),
        pltpu.VMEM((2, D, BT), BF),
        pltpu.VMEM((sizes["z"], ny, block_rows, BT), BF),
    )

    def attention_out(wout, att):
        wout_load = load(wout_in, wout, 4)
        att_load = load(att_in, att, 5)
        for rows in halves:
            unit, inv = norm(ags[rows, :])
            grad = dqs[rows, :]
            vec_ref[5:6] += col_sum(grad * unit)
            vec_ref[6:7] += col_sum(grad)
            hgrad = wide_a[rows, :] + norm_back(unit, inv, grad, gain2_ref[...])
            wide_a[rows, :] = hgrad
            branch = hgrad.astype(BF)
            rows_b[rows, :] = branch
            vec_ref[4:5] += col_sum(branch.astype(F32))
        hg_store = load(wide_a, hgrad_hbm, 7)
        each(fc1[0], fc1[2])
        wout_load.wait()
        for rows in halves:
            ags[rows, :] = dot(rows_b[rows, :], wout[...], NT)
        ags[ROWS:, :] = jnp.zeros((PROWS - ROWS, D), F32)
        each(embed, fc2[0])
        att_load.wait()
        put_blocks(wgs.at[0], slice(None), dot(att[...], rows_b[...], TN))
        each(out)
        hg_store.wait()

    pl.run_scoped(attention_out, pltpu.VMEM((D, D), BF), pltpu.VMEM((ROWS, D), BF))

    def attention(qbuf, wqkv):
        q_loads = []

        def load_next():
            k = len(q_loads)
            if k < 2 * UNITS:
                part = qkvp_in.at[k // 2, pl.ds((k % 2) * HALF, HALF)]
                q_loads.append(load(part, qbuf.at[k % 2], 10 + k))

        x_load = load(x_in, rows_b, 3)
        load_next()
        wqkv_load = load(wqkv_in, wqkv, 6)
        x_load.wait()
        for rows in halves:
            unit, _ = norm(rows_b[rows, :].astype(F32))
            tall[:, rows] = (unit * gain1_ref[...] + shift1_ref[...]).astype(BF).T

        def unit_products(u):
            rows_b[...] = dqs[:ROWS, :].astype(BF)
            put_blocks(wgs.at[SLOT[f"unit_{u}"]], slice(None), dot(tall[...], rows_b[...]))
            for c, row in ((0, 2), (2, 3)):
                vec_ref[row : row + 1, u * UNIT : (u + 1) * UNIT] = col_sum(
                    rows_b[:, c * UNIT : (c + 1) * UNIT].astype(F32)
                )

        def unit_first_grad(u):
            weight = jnp.concatenate(
                [wqkv[:, c * D + u * UNIT : c * D + (u + 1) * UNIT] for c in range(3)], axis=1
            )
            for rows in halves:
                total = dot(rows_b[rows, :], weight, NT)
                wide_a[rows, :] = total if u == 0 else wide_a[rows, :] + total

        def half_unit(u, half):
            q_loads[2 * u + half].wait()
            load_next()
            attn_unit_back(u, half, qbuf, half, ags, dqs)

        half_unit(0, 0)
        each(embed, fc2[1], fc1[2], out)
        half_unit(0, 1)
        each(embed, fc2[0])
        unit_products(0)
        each(units[0])
        wqkv_load.wait()
        unit_first_grad(0)
        each(fc2[1], fc1[1], out, units[0])
        half_unit(1, 0)
        each(fc2[1], fc2[0], fc1[0], fc1[2])
        half_unit(1, 1)
        each(fc2[1], fc1[1], out)
        unit_products(1)
        each(units[1], fc1[0], units[0], fc2[0])
        unit_first_grad(1)
        each(fc1[0], fc1[2], units[1], fc2[0])
        half_unit(2, 0)
        each(fc1[0], fc1[2], fc1[1], out, units[0])
        half_unit(2, 1)
        hg_again = load(hgrad_hbm, ags.at[pl.ds(0, ROWS)], 8)
        each(fc1[2], fc1[1], out, units[1])
        unit_products(2)
        each(units[2], fc1[1], out, units[0])
        unit_first_grad(2)
        x_again = load(x_in, rows_b, 3)
        each(units[1], units[2], units[0])
        hg_again.wait()
        x_again.wait()
        for rows in halves:
            unit, inv = norm(rows_b[rows, :].astype(F32))
            grad = wide_a[rows, :]
            vec_ref[0:1] += col_sum(grad * unit)
            vec_ref[1:2] += col_sum(grad)
            rows_b[rows, :] = (ags[rows, :] + norm_back(unit, inv, grad, gain1_ref[...])).astype(BF)

    pl.run_scoped(
        attention,
        pltpu.VMEM((2, HALF, PADK, 3 * UNIT), BF),
        pltpu.VMEM((D, 3 * D), BF),
    )
    pgrad_store = load(rows_b, pgrad_out, 9)
    for i in range(4):
        vec_ref[8 + i : 9 + i] = b1_ref[:, i * D : (i + 1) * D]
    vec = VectorSum(net, vec_ref, vec_slots)
    each(vec, units[0])

    def decoder(inbox, stage):
        for make in slot_copies:
            make().wait()
        own_slots().wait()
        load(arrived, inbox, 0).wait()
        dev_blocks, most, _ = owner_blocks(seq_count)
        fill = jnp.where(
            lax.broadcasted_iota(jnp.int32, (16, DEC), 0) == 0, token_ref[...], 0.0
        ).astype(BF)

        full = dev_blocks // seq_count

        def store(t, slot):
            rows = dec_out.at[pl.ds(0, full * seq_count)].reshape(full, seq_count, IMG, DEC)
            return pltpu.make_async_copy(
                stage.at[slot, pl.ds(0, full)],
                rows.at[:, first_block(seq_count, t)],
                store_sem.at[slot],
            )

        def last_store(t, slot, act):
            if full < most:
                at = full * seq_count + first_block(seq_count, t)

                @pl.when(at < dev_blocks)
                def _():
                    act(
                        pltpu.make_async_copy(
                            stage.at[slot, full], dec_out.at[at], store_sem.at[2 + slot]
                        )
                    )

        def wait_store(t, slot):
            store(t, slot).wait()
            last_store(t, slot, lambda c: c.wait())

        def spread(t, carry):
            slot = lax.rem(t, 2)

            @pl.when(t >= 2)
            def _():
                wait_store(t - 2, slot)

            source = jnp.concatenate(
                [inbox[slot_rows(t)].reshape(slots * IMG, DEC), fill], axis=0
            )
            rows = dot(one_hot(slots * IMG + 16, code_ref[t]), source, TN).astype(BF)
            stage[slot] = rows[: most * IMG].reshape(most, IMG, DEC)
            store(t, slot).start()
            last_store(t, slot, lambda c: c.start())
            return carry

        per = seq_count // 4
        for part in range(4):
            lax.fori_loop(part * per, (part + 1) * per, spread, 0)
            each(vec, units[1], units[2])
        for t in (seq_count - 2, seq_count - 1):
            wait_store(t, t % 2)

    pl.run_scoped(
        decoder,
        pltpu.VMEM(arrived.shape, BF),
        pltpu.VMEM((2, owner_blocks(seq_count)[1], IMG, DEC), BF),
    )
    vec.end()
    for item in sums.values():
        item.end()
    pgrad_store.wait()


def backward_and_sums(
    egrad, block_in, hidden, act, slope, we, w2, w1, att, qkvp, x, wout, wqkv, send,
    gain1, shift1, gain2, shift2, mask_rows, code, token,
):
    dp_count, seq_count = lax.axis_size("dp"), lax.axis_size("seq")
    sizes = axis_sizes(dp_count, seq_count)
    table = chunk_table(dp_count, seq_count)
    nz, ny = sizes["z"], sizes["y"]
    scratch = [
        pltpu.VMEM((ROWS, D), F32),
        pltpu.VMEM((PROWS, D), F32),
        pltpu.VMEM((PROWS, D), F32),
        pltpu.VMEM((D, ROWS), BF),
        pltpu.VMEM((ROWS, D), BF),
        pltpu.VMEM((3, nz, ny, table["out"].padded, D), BF),
        pltpu.VMEM((1, FF), F32),
        pltpu.SemaphoreType.DMA((16,)),
        pltpu.SemaphoreType.DMA((8,)),
        pltpu.SemaphoreType.DMA((16,)),
    ]
    copies = sum(sizes["x"] * 3 + sizes["y"] + sizes["z"] for _ in table)
    copies += sum(sizes.values()) + seq_count
    scratch += [
        pltpu.SemaphoreType.DMA((copies,)),
        pltpu.SemaphoreType.DMA((copies,)),
        pltpu.SemaphoreType.DMA((len(table) * sizes["x"],)),
    ]
    scratch += [pltpu.VMEM((size, VROWS, D), F32) for size in sizes.values()]
    for chunk in table.values():
        scratch += chunk.scratch(sizes)
    anywhere = pl.BlockSpec(memory_space=pl.ANY)
    vmem = pl.BlockSpec(memory_space=pltpu.VMEM)
    outs = pl.pallas_call(
        functools.partial(back_kernel, sizes, table),
        in_specs=[anywhere] * 14 + [vmem] * 7,
        out_specs=[anywhere, vmem] + [anywhere] * (6 + len(table)),
        out_shape=[
            jax.ShapeDtypeStruct((ROWS, D), BF),
            jax.ShapeDtypeStruct((VROWS, D), F32),
            jax.ShapeDtypeStruct((PATCHES, IMG, DEC), BF),
            jax.ShapeDtypeStruct((ROWS, D), F32),
            jax.ShapeDtypeStruct((nz, ny, FF // seq_count, D), BF),
            jax.ShapeDtypeStruct((nz, ny, D // seq_count, FF), BF),
            jax.ShapeDtypeStruct((nz, ny, table["embed"].padded, DEC), BF),
            jax.ShapeDtypeStruct(send.shape, BF),
        ]
        + [jax.ShapeDtypeStruct((dp_count, c.rows, c.cols), BF) for c in table.values()],
        scratch_shapes=scratch,
        compiler_params=pltpu.CompilerParams(
            collective_id=0, has_side_effects=True, vmem_limit_bytes=64 * MIB - 65536
        ),
        name="backward_and_sums",
    )(
        egrad, block_in, hidden, act, slope, we, w2, w1, att, qkvp, x, wout, wqkv, send,
        gain1, shift1, gain2, shift2, mask_rows, code, token,
    )
    decoder_input = outs[2].reshape(PATCHES * IMG, DEC)
    return outs[0], outs[1], decoder_input, outs[8:]


def finish_kernel(seq_count, table, *refs):
    vec_ref, parts, refs = refs[0], refs[1 : 1 + len(table)], refs[1 + len(table) :]
    w2_ref, w1_ref, we_ref, wo_ref, wqkv_ref, rows_ref, b1_ref, dec_ref = refs
    def pieces(name):
        chunk, ref = table[name], parts[list(table).index(name)]
        for q in range(chunk.a * chunk.b):
            row, col = (q // chunk.b) * chunk.r + chunk.r0, chunk.c0 + (q % chunk.b) * chunk.cols
            yield row, col, ref[q].astype(F32)

    for name, ref in (("fc2", w2_ref), ("fc1", w1_ref), ("embed", we_ref), ("out", wo_ref)):
        for key in table:
            if key.split("_")[0] == name:
                for row, col, value in pieces(key):
                    rows = min(value.shape[0], ref.shape[0] - row)
                    if rows > 0:
                        ref[row : row + rows, col : col + value.shape[1]] = value[:rows]
    for u in range(UNITS):
        for row, col, value in pieces(f"unit_{u}"):
            rows = min(value.shape[0], wqkv_ref.shape[0] - row)
            if rows > 0:
                for i in range(value.shape[1] // 128):
                    c, within = (col + i * 128) // UNIT, (col + i * 128) % UNIT
                    to = c * D + u * UNIT + within
                    wqkv_ref[row : row + rows, to : to + 128] = value[
                        :rows, i * 128 : (i + 1) * 128
                    ]

    me = lax.axis_index("seq")

    def mine(row, size, first):
        shift = lax.rem(D - first, D)
        return pltpu.roll(vec_ref[row : row + 8], shift, 1)[:, :size]

    rows_ref[...] = mine(0, D // seq_count, me * (D // seq_count))
    per = seq_count // 4
    chosen = mine(8, FF // seq_count, lax.rem(me, per) * (FF // seq_count))
    at = lax.broadcasted_iota(jnp.int32, chosen.shape, 0)
    b1_ref[...] = jnp.sum(jnp.where(at == me // per, chosen, 0.0), axis=0, keepdims=True)
    dec_ref[...] = mine(8, DEC // seq_count, me * (DEC // seq_count))


def finish(seq_count, vec, parts, table):
    def share(rows, cols):
        return jax.ShapeDtypeStruct((rows // seq_count, cols), F32)

    out_shape = [
        share(FF, D),
        share(D, FF),
        share(D, DEC),
        share(D, D),
        share(D, 3 * D),
        jax.ShapeDtypeStruct((8, D // seq_count), F32),
        jax.ShapeDtypeStruct((1, FF // seq_count), F32),
        jax.ShapeDtypeStruct((8, DEC // seq_count), F32),
    ]
    return pl.pallas_call(
        functools.partial(finish_kernel, seq_count, table),
        out_shape=out_shape,
        compiler_params=params(),
        name="finish",
    )(vec, *parts)


def decoder_codes(keep_index, slots):
    seq_count = lax.axis_size("seq")
    dev_blocks, _, padded = owner_blocks(seq_count)
    t = jnp.arange(seq_count, dtype=jnp.int32)
    start = first_block(seq_count, t)
    lowest = (lax.axis_index("seq") * PATCHES + start) // seq_count
    m = jnp.arange(padded, dtype=jnp.int32)[:, None]
    image = jnp.arange(seq_count * IMG, dtype=jnp.int32)
    lowest_of, start_of = (jnp.repeat(v, IMG)[None, :] for v in (lowest, start))
    place_at = lowest_of + m
    kept = keep_index.T[:, None, :]
    below = (kept < place_at[None]) & (kept >= lowest_of[None])
    found = jnp.sum(jnp.where(kept == place_at[None], 64, below.astype(jnp.int32)), axis=0)
    code = jnp.where(found >= 64, (found - 64) * IMG + image[None, :] % IMG, slots * IMG)
    code = jnp.where(start_of + m * seq_count < dev_blocks, code, -1)
    return code.reshape(padded, seq_count, IMG).transpose(1, 0, 2).reshape(seq_count, 1, -1)


def image_codes(keep_index, slots):
    seq_count = lax.axis_size("seq")
    group_imgs = keep_index.shape[0]
    at = lax.axis_index("seq") * IMG
    own = lax.dynamic_slice_in_dim(keep_index, at, IMG, 0)
    image = jnp.arange(IMG, dtype=jnp.int32)[:, None]
    owner = (own * group_imgs + at + image) // (IMG * PATCHES)
    lower = jnp.sum((owner[:, None, :] < owner[:, :, None]).astype(jnp.int32), axis=2)
    rank = jnp.arange(KEEP, dtype=jnp.int32)[None, :] - lower
    code = (owner * slots + rank) * HALF + image % HALF
    return code.reshape(2, 1, HROWS)


def local(
    patches,
    keep_index,
    ln1_gain,
    ln1_shift,
    w_qkv,
    q_bias,
    v_bias,
    w_out,
    out_bias,
    ln2_gain,
    ln2_shift,
    w_fc1,
    fc1_bias,
    w_fc2,
    fc2_bias,
    w_embed,
    embed_bias,
    mask_token,
    decoder_grad,
):
    seq_count = lax.axis_size("seq")
    slots = 2 * KEEP // seq_count
    dec_code = decoder_codes(keep_index, slots)
    img_code = image_codes(keep_index, slots)
    grad_slots, mask_rows = pick(seq_count, slots, dec_code, decoder_grad)
    returned = lax.all_to_all(grad_slots, "seq", split_axis=0, concat_axis=0, tiled=True)

    qkv_bias = jnp.concatenate([q_bias, jnp.zeros_like(q_bias), v_bias])
    qkvp, attended, hidden = attn_fwd(
        patches, ln1_gain, ln1_shift, w_qkv, qkv_bias, w_out, out_bias
    )
    active, slope, block_in, embedded = mlp_fwd(
        hidden, ln2_gain, ln2_shift, w_fc1, fc1_bias, w_fc2, fc2_bias,
        w_embed, embed_bias,
    )
    send = pack(img_code, embedded, seq_count * slots)
    embed_grad = unpack(img_code, returned)
    patches_grad, vec, decoder_input, parts = backward_and_sums(
        embed_grad, block_in, hidden, active, slope, w_embed, w_fc2, w_fc1, attended, qkvp, patches, w_out, w_qkv, send,
        ln1_gain, ln1_shift, ln2_gain, ln2_shift, mask_rows, dec_code, mask_token,
    )
    table = chunk_table(lax.axis_size("dp"), seq_count)
    w2g, w1g, weg, woutg, wqkvg, rows, b1, dec_rows = finish(seq_count, vec, parts, table)
    ln1g, ln1s, qb, vb, obias, ln2g, ln2s, b2 = (rows[i] for i in range(8))
    b1, ebias, mask_grad = b1[0], dec_rows[4], dec_rows[5]
    return (
        decoder_input,
        patches_grad,
        ln1g,
        ln1s,
        wqkvg,
        qb,
        vb,
        woutg,
        obias,
        ln2g,
        ln2s,
        w1g,
        b1,
        w2g,
        b2,
        weg,
        ebias,
        mask_grad,
    )


def solution(mesh):
    rows = P(("dp", "seq"), None)
    placed = (rows, P("dp", None)) + (P(),) * 16 + (rows,)
    vec, mat = P("seq"), P("seq", None)
    return jax.shard_map(
        local,
        mesh=mesh,
        in_specs=placed,
        out_specs=(
            rows, rows, vec, vec, mat, vec, vec, mat, vec, vec, vec, mat, vec, mat, vec, mat, vec, vec,
        ),
        check_vma=False,
    )
```

```python
import functools
import math

import jax
import jax.numpy as jnp
from jax import lax
from jax.experimental import pallas as pl
from jax.experimental.pallas import tpu as pltpu
from jax.sharding import PartitionSpec as P

D = 768
HEADS = 12
HEAD = 64
FF = 3072
DEC = 512
PATCHES = 196
KEEP = 49
IMG = 32
HALF = 16
ROWS = IMG * KEEP
HROWS = HALF * KEEP
PADK = 64
UNITS = 3
EPSILON = 1e-06
BF = jnp.bfloat16
F32 = jnp.float32
MIB = 1 << 20

NN = (((1,), (0,)), ((), ()))
NT = (((1,), (1,)), ((), ()))
TN = (((0,), (0,)), ((), ()))


def dot(left, right, dims=NN):
    return lax.dot_general(left, right, dims, preferred_element_type=F32)


def params(mib=60):
    return pltpu.CompilerParams(vmem_limit_bytes=mib * MIB)


def whole(shape):
    return pl.BlockSpec(shape, lambda *_: (0,) * len(shape), pipeline_mode=pl.Buffered(1))


def norm(values):
    centered = values - jnp.mean(values, axis=-1, keepdims=True)
    inv = lax.rsqrt(jnp.mean(centered * centered, axis=-1, keepdims=True) + EPSILON)
    return centered * inv, inv


def norm_back(unit, inv, grad, gain):
    f = grad * gain
    return inv * (
        f
        - jnp.mean(f, axis=-1, keepdims=True)
        - unit * jnp.mean(f * unit, axis=-1, keepdims=True)
    )


def col_sum(values):
    return jnp.sum(values, axis=0, keepdims=True)


def gelu_pair(v):
    cdf = 0.5 + 0.5 * lax.erf(v * (1 / math.sqrt(2.0)))
    return v * cdf, cdf + v * (jnp.exp(-0.5 * v * v) * (1 / math.sqrt(2 * math.pi)))


def one_hot(rows, code):
    at = lax.broadcasted_iota(jnp.int32, (rows, code.shape[1]), 0)
    return jnp.where(at == code, 1.0, 0.0).astype(BF)


def owner_blocks(seq_count):
    dev_blocks = PATCHES
    most = -(-dev_blocks // seq_count)
    return dev_blocks, most, -(-most // 4) * 4


def first_block(seq_count, t):
    return lax.rem(
        t + seq_count - lax.rem(lax.axis_index("seq") * PATCHES, seq_count), seq_count
    )


UNIT = 4 * HEAD
PAIR = 2 * HEAD


def block_diag(rows):
    heads = rows.shape[1] // HEAD
    lane_head = lax.broadcasted_iota(jnp.int32, rows.shape, 1) // HEAD
    zero = jnp.zeros_like(rows)
    return jnp.concatenate([jnp.where(lane_head == h, rows, zero) for h in range(heads)], axis=0)


def fold_pair(rows):
    low = lax.broadcasted_iota(jnp.int32, (PADK, PAIR), 1) < HEAD
    return jnp.where(low, rows[:PADK], rows[PADK:])


def soft(scores, axis):
    valid = lax.broadcasted_iota(jnp.int32, scores.shape, axis) < KEEP
    scores = jnp.where(valid, scores, -1e30)
    e = jnp.exp(scores - jnp.max(scores, axis=axis, keepdims=True))
    return e * (1.0 / jnp.sum(e, axis=axis, keepdims=True))


def each_image(count, image, *refs):
    def group(g, carry):
        base = pl.multiple_of(g * 8 * KEEP, 8)
        views = [ref.at[pl.ds(base, 8 * KEEP + 16)] for ref in refs]
        for near in range(8):
            image(g * 8 + near, near, *views)
        return carry

    lax.fori_loop(0, count // 8, group, 0)


MESH = pl.DeviceIdType.MESH
ORDERS = (("x", "y", "z"), ("y", "x", "z"))
DIMS = {"x": 0, "z": 1, "y": 2}
VROWS = 16
FC1_PARTS = 3


def axis_sizes(dp_count, seq_count):
    z = 4 if seq_count % 4 == 0 else 1
    return {"core": 2, "x": dp_count // 2, "y": seq_count // z, "z": z}


def cut(dp_count, rows, cols):
    for padded in range(rows, rows + 256, 16):
        for a in range(1, dp_count + 1):
            b = dp_count // a
            if a * b == dp_count and padded % (16 * a) == 0 and cols % (128 * b) == 0:
                return a, b, padded
    raise ValueError("no cut")


class Chunk:
    def __init__(self, dp_count, rows, cols, order, half=0, halves=1, first_col=0):
        self.a, self.b, self.padded = cut(dp_count, rows, cols)
        self.r, self.cols = self.padded // self.a, cols // self.b
        self.rows = self.r // halves
        self.r0, self.c0 = half * self.rows, first_col
        self.order = ORDERS[order]

    def scratch(self, sizes):
        dims = [sizes[name] for name in ("x", "z", "y")]
        shapes = [(*dims, self.rows, self.cols)] * 2
        for stage in range(1, 4):
            left = [sizes[name] for name in ("x", "z", "y") if name not in self.order[:stage]]
            shapes.append((sizes[self.order[stage - 1]] - 1, *left, self.rows, self.cols))
        shapes.append((sizes["x"] * 2, self.rows, self.cols))
        return [pltpu.VMEM(shape, BF) for shape in shapes]


def halves_of(dp_count, rows, cols):
    a, _, padded = cut(dp_count, rows, cols)
    return 2 if (padded // a) % 32 == 0 else 1


def chunk_table(dp_count, seq_count):
    table = {}
    rows, span = D // seq_count, FF // FC1_PARTS
    for i in range(FC1_PARTS):
        table[f"fc1_{i}"] = Chunk(dp_count, rows, span, i % 2, first_col=i * span)
    halves = halves_of(dp_count, FF // seq_count, D)
    for h in range(halves):
        table[f"fc2_{h}"] = Chunk(dp_count, FF // seq_count, D, (h + 1) % 2, h, halves)
    table["embed"] = Chunk(dp_count, rows, DEC, 1)
    for i, name in enumerate(("out", "unit_0", "unit_1", "unit_2")):
        table[name] = Chunk(dp_count, rows, D, (i + 1) % 2)
    return table


class Net:
    def __init__(self, sizes, send_sem, recv_sem):
        self.sizes, self.send_sem, self.recv_sem = sizes, send_sem, recv_sem
        self.used = 0
        dp, sq = lax.axis_index("dp"), lax.axis_index("seq")
        ny = sizes["y"]
        self.me = {"core": lax.rem(dp, 2), "x": dp // 2, "y": lax.rem(sq, ny), "z": sq // ny}

    def device(self, axis, value):
        if axis == "seq":
            return {"dp": lax.axis_index("dp"), "seq": value}
        coord = dict(self.me)
        coord[axis] = value
        return {
            "dp": coord["x"] * 2 + coord["core"],
            "seq": coord["z"] * self.sizes["y"] + coord["y"],
        }

    def peer(self, axis, d):
        return lax.rem(self.me[axis] + d, self.sizes[axis])

    def barrier(self):
        sem, count = pltpu.get_barrier_semaphore(), 0
        for axis, size in self.sizes.items():
            if axis in ("core", "x"):
                for d in range(1, size):
                    pl.semaphore_signal(
                        sem, inc=1, device_id=self.device(axis, self.peer(axis, d)), device_id_type=MESH
                    )
                    count += 1
        seq_count = self.sizes["y"] * self.sizes["z"]
        for d in range(1, seq_count):
            to = lax.rem(lax.axis_index("seq") + d, seq_count)
            pl.semaphore_signal(sem, inc=1, device_id=self.device("seq", to), device_id_type=MESH)
            count += 1
        pl.semaphore_wait(sem, count)

    def copy(self, what):
        slot = self.used
        self.used += 1

        def make():
            src, dst, axis, value = what()
            return pltpu.make_async_remote_copy(
                src_ref=src,
                dst_ref=dst,
                send_sem=self.send_sem.at[slot],
                recv_sem=self.recv_sem.at[slot],
                device_id=self.device(axis, value),
                device_id_type=MESH,
            )

        make().start()
        return make


class Sum:
    def __init__(self, net, chunk, source, bufs, local_sems, out):
        self.net, self.chunk, self.source, self.out = net, chunk, source, out
        self.own, self.recv, self.gathered = bufs[0], bufs[1:5], bufs[5]
        self.local_sems = local_sems
        self.at = 0
        self.copies, self.loads = [], []

    def next(self):
        steps = (self.core, self.first, self.second, self.third, self.spread_x, self.spread_core, self.leave)
        if self.at < len(steps):
            steps[self.at]()
            self.at += 1

    def wait(self):
        for make in self.copies:
            make().wait()
        self.copies = []

    def piece(self, x, core):
        k = self.chunk
        q = x * 2 + core
        row = pl.multiple_of((q // k.b) * k.r + k.r0, 16)
        col = pl.multiple_of(k.c0 + lax.rem(q, k.b) * k.cols, 128)
        return self.source.at[:, :, pl.ds(row, k.rows), pl.ds(col, k.cols)]

    def core(self):
        net = self.net

        def send(x):
            other = net.peer("core", 1)
            return self.piece(x, other), self.recv[0].at[x], "core", other

        def load(x):
            return pltpu.make_async_copy(
                self.piece(x, net.me["core"]), self.own.at[x], self.local_sems[x]
            )

        for x in range(net.sizes["x"]):
            self.copies.append(net.copy(functools.partial(send, x)))
        for x in range(net.sizes["x"]):
            load(x).start()
            self.loads.append(functools.partial(load, x))

    def first(self):
        for load in self.loads:
            load().wait()
        self.wait()
        self.add(0)
        self.start(1)

    def second(self):
        self.wait()
        self.add(1)
        self.start(2)

    def third(self):
        self.wait()
        self.add(2)
        self.start(3)

    def start(self, stage):
        net, order = self.net, self.chunk.order
        axis, done = order[stage - 1], order[: stage - 1]

        def send(d):
            value = net.peer(axis, d)
            at = [slice(None)] * 3
            for name in done:
                at[DIMS[name]] = net.me[name]
            at[DIMS[axis]] = value
            return self.own.at[tuple(at)], self.recv[stage].at[d - 1], axis, value

        for d in range(1, net.sizes[axis]):
            self.copies.append(net.copy(functools.partial(send, d)))

    def add(self, stage):
        sizes, me = self.net.sizes, self.net.me
        done = self.chunk.order[:stage]
        left = [name for name in ("x", "z", "y") if name not in done]
        terms = 1 if stage == 0 else sizes[done[-1]] - 1

        def body(k, carry):
            at, rest = {name: me[name] for name in done}, k
            for name in reversed(left):
                at[name] = lax.rem(rest, sizes[name])
                rest = rest // sizes[name]
            here = (at["x"], at["z"], at["y"])
            there = tuple(at[name] for name in left)
            if terms == 1 and stage < 3:
                other = self.recv[stage][there if stage == 0 else (0,) + there]
                self.own[here] = self.own[here] + other
                return carry
            value = self.own[here].astype(F32)
            for d in range(terms):
                value = value + self.recv[stage][(d,) + there].astype(F32)
            if stage == 3:
                self.gathered[me["x"] * 2 + me["core"]] = value.astype(BF)
            else:
                self.own[here] = value.astype(BF)
            return carry

        total = math.prod(sizes[name] for name in left)
        if total == 1:
            body(0, 0)
        else:
            lax.fori_loop(0, total, body, 0)

    def spread_x(self):
        self.wait()
        self.add(3)
        net = self.net

        def send(d):
            mine = self.gathered.at[net.me["x"] * 2 + net.me["core"]]
            return mine, mine, "x", net.peer("x", d)

        for d in range(1, net.sizes["x"]):
            self.copies.append(net.copy(functools.partial(send, d)))

    def spread_core(self):
        self.wait()
        net = self.net

        def send(x):
            mine = self.gathered.at[x * 2 + net.me["core"]]
            return mine, mine, "core", net.peer("core", 1)

        for x in range(net.sizes["x"]):
            self.copies.append(net.copy(functools.partial(send, x)))

    def leave(self):
        self.wait()

        def store():
            return pltpu.make_async_copy(self.gathered, self.out, self.local_sems[0])

        store().start()
        self.loads = [store]

    def end(self):
        while self.at < 7:
            self.next()
        self.loads[0]().wait()


class VectorSum:
    def __init__(self, net, value, slots):
        self.net, self.value, self.slots = net, value, slots
        self.left = [name for name, size in net.sizes.items() if size > 1]
        self.copies = []

    def next(self):
        net = self.net
        if self.copies:
            for make in self.copies:
                make().wait()
            total = self.now[0]
            for i in range(1, net.sizes[self.axis]):
                total = total + self.now[i]
            self.value[...] = total
            self.copies = []
        if self.left:
            axis = self.axis = self.left.pop(0)
            now = self.now = self.slots[axis]
            now[net.me[axis]] = self.value[...]

            def send(d):
                mine = now.at[net.me[axis]]
                return mine, mine, axis, net.peer(axis, d)

            for d in range(1, net.sizes[axis]):
                self.copies.append(net.copy(functools.partial(send, d)))

    def end(self):
        while self.left or self.copies:
            self.next()


FTILE = 512
FSTEPS = FF // FTILE


def forward_kernel(sizes, *refs):
    (
        dec_in, x_in, wqkv_in, wout_in, w1_in, w2_in, we_in,
        code_ref, icode_ref, gain1_ref, shift1_ref, qb_ref, vb_ref, ob_ref, gain2_ref, shift2_ref, b1_ref, b2_ref, be_ref,
    ) = refs[:19]
    (
        mask_ref, returned, qkvp_out, att_out, hidden_out, act_out, slope_out, block_out, send_out, second_out,
        first_out, egrad_out,
    ) = refs[19:31]
    slot_buf, hid, xbuf, wqkv, wout, load_sem, tile_sem, store_sem, send_sem, recv_sem = refs[31:]
    net = Net(sizes, send_sem, recv_sem)
    net.barrier()
    seq_count = sizes["y"] * sizes["z"]
    slots = returned.shape[0] // seq_count
    me = lax.axis_index("seq")
    halves = [slice(0, HROWS), slice(HROWS, ROWS)]

    def load(src, dst, slot):
        c = pltpu.make_async_copy(src, dst, load_sem.at[slot])
        c.start()
        return c

    def slot_rows(owner):
        return pl.ds(owner * slots, slots)

    def slot_copy(d):
        return pltpu.make_async_remote_copy(
            src_ref=slot_buf.at[slot_rows(d)],
            dst_ref=returned.at[slot_rows(me)],
            send_sem=send_sem.at[d],
            recv_sem=recv_sem.at[d],
            device_id=net.device("seq", lax.rem(me + d, seq_count)),
            device_id_type=MESH,
        )

    def pick(dec):
        dec_load = load(dec_in, dec, 0)
        x_load = load(x_in, xbuf, 1)
        wqkv_load = load(wqkv_in, wqkv, 2)
        wout_load = load(wout_in, wout, 3)
        mask_ref[...] = jnp.zeros_like(mask_ref)
        dev_blocks, most, padded = owner_blocks(seq_count)
        dec_load.wait()

        def pick_for(d):
            t = lax.rem(me + d, seq_count)
            start = first_block(seq_count, t)
            pieces = []
            for m in range(most):
                at = jnp.minimum(start + m * seq_count, dev_blocks - 1)
                pieces.append(dec[pl.ds(pl.multiple_of(at * IMG, IMG), IMG), :])
            if padded > most:
                pieces.append(jnp.zeros(((padded - most) * IMG, DEC), BF))
            picked = dot(one_hot(slots * IMG + 16, code_ref[t]), jnp.concatenate(pieces, axis=0))
            slot_buf[slot_rows(d)] = picked[: slots * IMG].astype(BF).reshape(slots, IMG, DEC)
            mask_ref[...] += picked[slots * IMG : slots * IMG + 8]

        def far(k, carry):
            pick_for(k)
            slot_copy(k).start()
            return carry

        lax.fori_loop(seq_count // 2, seq_count, far, 0)
        lax.fori_loop(1, seq_count // 2, far, 0)
        pick_for(0)
        load(slot_buf.at[slot_rows(0)], returned.at[slot_rows(me)], 4)
        for c in (x_load, wqkv_load, wout_load):
            c.wait()

    pl.run_scoped(pick, pltpu.VMEM((PATCHES * IMG, DEC), BF))

    def attention(qs, ats, qstage, astage):
        def stores(g):
            rows = pl.ds(pl.multiple_of(g * HROWS, 16), HROWS)
            return [
                pltpu.make_async_copy(
                    qstage, qkvp_out.at[:, pl.ds(g * HALF, HALF)], store_sem.at[0]
                ),
                pltpu.make_async_copy(astage, att_out.at[rows], store_sem.at[1]),
            ]

        def half(g, carry):
            rows = pl.ds(pl.multiple_of(g * HROWS, 16), HROWS)
            unit, _ = norm(xbuf[rows, :].astype(F32))
            first = (unit * gain1_ref[...] + shift1_ref[...]).astype(BF)
            for c in range(3):
                cols = slice(c * D, (c + 1) * D)
                value = dot(first, wqkv[:, cols])
                if c != 1:
                    value = value + (qb_ref[...] if c == 0 else vb_ref[...])
                qs[:HROWS, cols] = value.astype(BF).astype(F32)
            qs[HROWS:, :] = jnp.zeros((16, 3 * D), F32)

            @pl.when(g == 1)
            def _():
                for c in stores(0):
                    c.wait()

            def image(i, near, qs, ats):
                r0 = near * KEEP
                for u in range(HEADS // 2):
                    part = []
                    for c in range(3):
                        cols = slice(c * D + u * PAIR, c * D + (u + 1) * PAIR)
                        value = qs[r0 : r0 + PADK, cols].astype(BF)
                        to = c * UNIT + (u % 2) * PAIR
                        qstage[u // 2, i, :, to : to + PAIR] = value
                        part.append(value)
                    q, k, v = part
                    probs = soft(dot(block_diag(q * BF(0.125)), k, NT), 1).astype(BF)
                    out = fold_pair(dot(probs, v))
                    ats[r0 : r0 + 56, u * PAIR : (u + 1) * PAIR] = out[:56]

            each_image(HALF, image, qs, ats)
            att = ats[:HROWS, :].astype(BF)
            astage[...] = att
            for c in stores(g):
                c.start()
            hid[rows, :] = xbuf[rows, :].astype(F32) + (dot(att, wout[...]) + ob_ref[...])
            return carry

        lax.fori_loop(0, 2, half, 0)
        for c in stores(1):
            c.wait()

    pl.run_scoped(
        attention,
        pltpu.VMEM((HROWS + 16, 3 * D), F32),
        pltpu.VMEM((HROWS + 16, D), F32),
        pltpu.VMEM((UNITS, HALF, PADK, 3 * UNIT), BF),
        pltpu.VMEM((HROWS, D), BF),
    )
    hid_store = load(hid, hidden_out, 5)

    def feed_forward(second, acc, turned, w1s, w2s, acts, slopes, we, emb, boxes):
        def columns(k):
            return pl.ds(pl.multiple_of(k * FTILE, FTILE), FTILE)

        def loads(k, slot):
            pairs = ((w1_in.at[:, columns(k)], w1s), (w2_in.at[columns(k), :], w2s))
            return [
                pltpu.make_async_copy(src, dst.at[slot], tile_sem.at[slot * 2 + i])
                for i, (src, dst) in enumerate(pairs)
            ]

        def stores(k, slot):
            pairs = ((acts, act_out), (slopes, slope_out))
            return [
                pltpu.make_async_copy(src.at[slot], dst.at[:, columns(k)], store_sem.at[slot * 2 + i])
                for i, (src, dst) in enumerate(pairs)
            ]

        for c in loads(0, 0):
            c.start()
        we_load = load(we_in, we, 6)
        for rows in halves:
            unit, _ = norm(hid[rows, :])
            second[rows, :] = (unit * gain2_ref[...] + shift2_ref[...]).astype(BF)
            acc[rows, :] = hid[rows, :] + b2_ref[...]

        def tile(k, carry):
            slot = lax.rem(k, 2)
            for c in loads(k, slot):
                c.wait()

            @pl.when(k + 1 < FSTEPS)
            def _():
                for c in loads(k + 1, 1 - slot):
                    c.start()

            @pl.when(k >= 2)
            def _():
                for c in stores(k - 2, slot):
                    c.wait()

            for rows in halves:
                inner = dot(second[rows, :], w1s[slot]) + b1_ref[:, columns(k)]
                active, slope = gelu_pair(inner)
                active = active.astype(BF)
                acts[slot, rows, :] = active
                slopes[slot, rows, :] = slope.astype(BF)
                acc[rows, :] += dot(active, w2s[slot])
            for c in stores(k, slot):
                c.start()
            return carry

        lax.fori_loop(0, FSTEPS, tile, 0)
        for rows in halves:
            turned[:, rows] = second[rows, :].T
        second_store = load(turned, second_out, 7)
        second[...] = acc[...].astype(BF)
        block_store = load(second, block_out, 8)
        we_load.wait()
        emb[...] = (dot(second[...], we[...]) + be_ref[...]).astype(BF)
        count = seq_count * slots

        def box_store(g):
            return pltpu.make_async_copy(
                boxes.at[g], send_out.at[:, pl.ds(g * HALF, HALF)], tile_sem.at[4 + g]
            )

        def pack(g, carry):
            rows = pl.ds(pl.multiple_of(g * HROWS, 16), HROWS)
            boxes[g] = (
                dot(one_hot(count * HALF, icode_ref[g]), emb[rows, :])
                .astype(BF)
                .reshape(count, HALF, DEC)
            )
            box_store(g).start()
            return carry

        lax.fori_loop(0, 2, pack, 0)
        for k in (FSTEPS - 2, FSTEPS - 1):
            for c in stores(k, k % 2):
                c.wait()
        second_store.wait()
        for rows in halves:
            unit, _ = norm(xbuf[rows, :].astype(F32))
            turned[:, rows] = (unit * gain1_ref[...] + shift1_ref[...]).astype(BF).T
        first_store = load(turned, first_out, 7)
        for g in range(2):
            box_store(g).wait()
        block_store.wait()
        first_store.wait()

    pl.run_scoped(
        feed_forward,
        pltpu.VMEM((ROWS, D), BF),
        pltpu.VMEM((ROWS, D), F32),
        pltpu.VMEM((D, ROWS), BF),
        pltpu.VMEM((2, D, FTILE), BF),
        pltpu.VMEM((2, FTILE, D), BF),
        pltpu.VMEM((2, ROWS, FTILE), BF),
        pltpu.VMEM((2, ROWS, FTILE), BF),
        pltpu.VMEM((D, DEC), BF),
        pltpu.VMEM((ROWS, DEC), BF),
        pltpu.VMEM((2, seq_count * slots, HALF, DEC), BF),
    )

    def unpack(egrad):
        pltpu.make_async_copy(
            slot_buf.at[slot_rows(0)], returned.at[slot_rows(me)], load_sem.at[4]
        ).wait()
        for d in range(1, seq_count):
            slot_copy(d).wait()
        load(returned, slot_buf, 4).wait()
        for g in range(2):
            source = slot_buf[:, g * HALF : (g + 1) * HALF].reshape(seq_count * slots * HALF, DEC)
            rows = slice(g * HROWS, (g + 1) * HROWS)
            egrad[rows, :] = dot(one_hot(seq_count * slots * HALF, icode_ref[g]), source, TN).astype(BF)
        load(egrad, egrad_out, 4).wait()

    pl.run_scoped(unpack, pltpu.VMEM((ROWS, DEC), BF))
    hid_store.wait()


def forward(
    dec_grad, x, wqkv, wout, w1, w2, we, code, icode, gain1, shift1, qb, vb, ob, gain2, shift2, b1, b2, be
):
    dp_count, seq_count = lax.axis_size("dp"), lax.axis_size("seq")
    sizes = axis_sizes(dp_count, seq_count)
    count = seq_count * (2 * KEEP // seq_count)
    anywhere = pl.BlockSpec(memory_space=pl.ANY)
    vmem = pl.BlockSpec(memory_space=pltpu.VMEM)
    out = jax.ShapeDtypeStruct
    return pl.pallas_call(
        functools.partial(forward_kernel, sizes),
        in_specs=[anywhere] * 7 + [vmem] * 12,
        out_specs=[vmem] + [anywhere] * 11,
        out_shape=[
            out((8, DEC), F32),
            out((count, IMG, DEC), BF),
            out((UNITS, IMG, PADK, 3 * UNIT), BF),
            out((ROWS, D), BF),
            out((ROWS, D), F32),
            out((ROWS, FF), BF),
            out((ROWS, FF), BF),
            out((ROWS, D), BF),
            out((count, IMG, DEC), BF),
            out((D, ROWS), BF),
            out((D, ROWS), BF),
            out((ROWS, DEC), BF),
        ],
        scratch_shapes=[
            pltpu.VMEM((count, IMG, DEC), BF),
            pltpu.VMEM((ROWS, D), F32),
            pltpu.VMEM((ROWS, D), BF),
            pltpu.VMEM((D, 3 * D), BF),
            pltpu.VMEM((D, D), BF),
            pltpu.SemaphoreType.DMA((9,)),
            pltpu.SemaphoreType.DMA((6,)),
            pltpu.SemaphoreType.DMA((4,)),
            pltpu.SemaphoreType.DMA((seq_count,)),
            pltpu.SemaphoreType.DMA((seq_count,)),
        ],
        compiler_params=pltpu.CompilerParams(
            collective_id=1, has_side_effects=True, vmem_limit_bytes=64 * MIB - 65536
        ),
        name="forward",
    )(
        dec_grad, x, wqkv, wout, w1, w2, we, code, icode, gain1, shift1, qb, vb, ob, gain2, shift2, b1, b2, be
    )


PROWS = ROWS + 16
SLOT = {"out": 0, "unit_0": 1, "unit_1": 2, "unit_2": 0}


def attn_unit_back(u, half, qbuf, slot, ags, dqs):
    def image(i, near, ags, dqs):
        r0 = near * KEEP
        valid = lax.broadcasted_iota(jnp.int32, (PADK, UNIT), 0) < KEEP
        q, k, v = (qbuf[slot, i, :, c * UNIT : (c + 1) * UNIT] for c in range(3))
        q_diag = block_diag(q * BF(0.125))
        probs = soft(dot(k, q_diag, NT), 0)
        probs_in = probs.astype(BF)
        agrad = jnp.where(valid, ags[r0 : r0 + PADK, u * UNIT : (u + 1) * UNIT], 0.0).astype(BF)
        a_diag = block_diag(agrad)
        pgrad = dot(v, a_diag, NT)
        inner = jnp.sum(probs * pgrad, axis=0, keepdims=True)
        sgrad = (probs * (pgrad - inner)).astype(BF)
        whole_q = dot(sgrad, k, TN)
        qgrad = 0.125 * jnp.concatenate(
            [
                fold_pair(whole_q[e * 2 * PADK : (e + 1) * 2 * PADK, e * PAIR : (e + 1) * PAIR])
                for e in range(2)
            ],
            axis=1,
        )
        for c, grad in enumerate((qgrad, dot(sgrad, q_diag), dot(probs_in, a_diag))):
            dqs[r0 : r0 + 56, c * UNIT : (c + 1) * UNIT] = grad[:56]

    rows = pl.ds(half * HROWS, HROWS + 16)
    each_image(HALF, image, ags.at[rows], dqs.at[rows])


BT = 512
TILES = FF // BT


def back_kernel(sizes, table, *refs):
    names = list(table)
    (
        egrad_in, block_in, hidden_in, act_in, slope_in, we_in, w2_in, w1_in, att_in, qkvp_in, x_in, wout_in, wqkv_in, second_in, first_in,
        send_in, gain1_ref, gain2_ref, mask_ref, code_ref, token_ref,
    ) = refs[:21]
    pgrad_out, vec_ref, dec_out, hgrad_hbm, w2g_hbm, w1g_hbm, weg_hbm, arrived = refs[21:29]
    outs, refs = refs[29 : 29 + len(names)], refs[29 + len(names) :]
    (
        wide_a, ags, dqs, tall, rows_b, wgs, b1_ref, load_sem, tile_sem, store_sem, send_sem, recv_sem, local_sem,
    ) = refs[:13]
    refs = refs[13:]
    vec_slots = {name: refs[i] for i, name in enumerate(sizes)}
    refs = refs[len(sizes) :]

    net = Net(sizes, send_sem, recv_sem)
    net.barrier()
    seq_count = sizes["y"] * sizes["z"]
    slots = arrived.shape[0] // seq_count
    seq_me = lax.axis_index("seq")

    def slot_rows(owner):
        return pl.ds(owner * slots, slots)

    def slot_send(d):
        to = lax.rem(seq_me + d, seq_count)
        return send_in.at[slot_rows(to)], arrived.at[slot_rows(seq_me)], "seq", to

    slot_copies = [net.copy(functools.partial(slot_send, d)) for d in range(1, seq_count)]

    def own_slots():
        return pltpu.make_async_copy(
            send_in.at[slot_rows(seq_me)], arrived.at[slot_rows(seq_me)], load_sem.at[2]
        )

    own_slots().start()
    sources = {"fc2": w2g_hbm, "fc1": w1g_hbm, "embed": weg_hbm}
    sums = {}
    for i, name in enumerate(names):
        sums[name] = Sum(
            net,
            table[name],
            wgs.at[SLOT[name]] if name in SLOT else sources[name.split("_")[0]],
            refs[6 * i : 6 * (i + 1)],
            [local_sem.at[i * sizes["x"] + x] for x in range(sizes["x"])],
            outs[i],
        )
    fc2 = [sums.get(f"fc2_{h}") for h in range(2)]
    fc1 = [sums[n] for n in names if n.startswith("fc1")]
    embed, out = sums["embed"], sums["out"]
    units = [sums[f"unit_{u}"] for u in range(UNITS)]

    def each(*items):
        for item in items:
            if item is not None:
                item.next()

    def load(src, dst, slot):
        c = pltpu.make_async_copy(src, dst, load_sem.at[slot])
        c.start()
        return c

    ny, blocks = sizes["y"], sizes["y"] * sizes["z"]
    block_rows = D // blocks
    halves = [slice(0, HROWS), slice(HROWS, ROWS)]

    def put_blocks(ref, cols, value):
        for t in range(blocks):
            ref[t // ny, t % ny, :block_rows, cols] = value[
                t * block_rows : (t + 1) * block_rows
            ].astype(BF)

    def clear_padding(ref):
        pad = ref.shape[-2] - block_rows
        if pad:
            ref[..., block_rows:, :] = jnp.zeros((*ref.shape[:-2], pad, ref.shape[-1]), BF)

    clear_padding(wgs)
    vec_ref[...] = jnp.zeros_like(vec_ref)
    vec_ref[13:14, :DEC] = mask_ref[:1]

    third = FF // blocks // 3

    def columns(k):
        return pl.ds(pl.multiple_of(k * BT, BT), BT)

    hidden_load = load(hidden_in, ags.at[pl.ds(0, ROWS)], 3)
    second_load = load(second_in, tall, 8)

    def embedding(egrad, block, we, weg):
        clear_padding(weg)
        eg_load = load(egrad_in, egrad, 0)
        we_load = load(we_in, we, 1)
        block_load = load(block_in, block, 4)
        eg_load.wait()
        we_load.wait()
        for rows in halves:
            out_grad = dot(egrad[rows, :], we[...], NT)
            wide_a[rows, :] = out_grad
            two = out_grad.astype(BF)
            rows_b[rows, :] = two
            vec_ref[7:8] += col_sum(two.astype(F32))
            vec_ref[12:13, :DEC] += col_sum(egrad[rows, :].astype(F32))
        block_load.wait()
        put_blocks(weg, slice(None), dot(block[...], egrad[...], TN))
        load(weg, weg_hbm, 5).wait()
        each(embed)

    pl.run_scoped(
        embedding,
        pltpu.VMEM((ROWS, DEC), BF),
        pltpu.VMEM((ROWS, D), BF),
        pltpu.VMEM((D, DEC), BF),
        pltpu.VMEM(weg_hbm.shape, BF),
    )

    def second_weight(acts, stage):
        def act_load(k, slot):
            return pltpu.make_async_copy(act_in.at[:, columns(k)], acts.at[slot], tile_sem.at[slot])

        def stores(k, slot):
            copies = []
            for i in range(BT // third):
                block = k * (BT // third) + i
                owner = block // 3
                rows = pl.ds(pl.multiple_of(lax.rem(block, 3) * third, third), third)
                copies.append(
                    pltpu.make_async_copy(
                        stage.at[slot, pl.ds(i * third, third)],
                        w2g_hbm.at[owner // ny, lax.rem(owner, ny), rows],
                        store_sem.at[slot * (BT // third) + i],
                    )
                )
            return copies

        act_load(0, 0).start()

        def tile(k, carry):
            slot = lax.rem(k, 2)
            act_load(k, slot).wait()

            @pl.when(k + 1 < TILES)
            def _():
                act_load(k + 1, 1 - slot).start()

            @pl.when(k >= 2)
            def _():
                for c in stores(k - 2, slot):
                    c.wait()

            stage[slot] = dot(acts[slot], rows_b[...], TN).astype(BF)
            for c in stores(k, slot):
                c.start()
            return carry

        lax.fori_loop(0, TILES, tile, 0)
        for k in (TILES - 2, TILES - 1):
            for c in stores(k, k % 2):
                c.wait()

    pl.run_scoped(second_weight, pltpu.VMEM((2, ROWS, BT), BF), pltpu.VMEM((2, BT, D), BF))
    each(*fc2, embed)

    def first_weight(slopes, w2s, w1s, stage):
        def loads(k, slot):
            pairs = (
                (slope_in.at[:, columns(k)], slopes),
                (w2_in.at[columns(k), :], w2s),
                (w1_in.at[:, columns(k)], w1s),
            )
            return [
                pltpu.make_async_copy(src, dst.at[slot], tile_sem.at[slot * 3 + i])
                for i, (src, dst) in enumerate(pairs)
            ]

        def store(k):
            return pltpu.make_async_copy(stage, w1g_hbm.at[:, :, :, columns(k)], store_sem.at[0])

        per = TILES // FC1_PARTS
        for c in loads(0, 0):
            c.start()
        hidden_load.wait()
        second_load.wait()
        dqs[...] = jnp.zeros_like(dqs)

        def tile(k, carry):
            slot = lax.rem(k, 2)
            for c in loads(k, slot):
                c.wait()

            @pl.when(k + 1 < TILES)
            def _():
                for c in loads(k + 1, 1 - slot):
                    c.start()

            inner = (dot(rows_b[...], w2s[slot], NT) * slopes[slot].astype(F32)).astype(BF)
            b1_ref[:, columns(k)] = col_sum(inner.astype(F32))
            grad = dot(tall[...], inner)

            @pl.when(lax.rem(k, per) > 0)
            def _():
                store(k - 1).wait()

            put_blocks(stage, slice(None), grad)
            store(k).start()
            dqs[:ROWS, :] += dot(inner, w1s[slot], NT)
            return carry

        for part in range(FC1_PARTS):
            lax.fori_loop(part * per, (part + 1) * per, tile, 0)
            store((part + 1) * per - 1).wait()
            if part == 0:
                each(fc1[0], embed, *fc2)
            if part == 1:
                each(fc1[1], embed, fc1[0])
            if part == 2:
                each(fc1[2], fc2[1], fc1[1])

    pl.run_scoped(
        first_weight,
        pltpu.VMEM((2, ROWS, BT), BF),
        pltpu.VMEM((2, BT, D), BF),
        pltpu.VMEM((2, D, BT), BF),
        pltpu.VMEM((sizes["z"], ny, block_rows, BT), BF),
    )

    def attention_out(wout, att):
        wout_load = load(wout_in, wout, 4)
        att_load = load(att_in, att, 5)
        for rows in halves:
            unit, inv = norm(ags[rows, :])
            grad = dqs[rows, :]
            vec_ref[5:6] += col_sum(grad * unit)
            vec_ref[6:7] += col_sum(grad)
            hgrad = wide_a[rows, :] + norm_back(unit, inv, grad, gain2_ref[...])
            wide_a[rows, :] = hgrad
            branch = hgrad.astype(BF)
            rows_b[rows, :] = branch
            vec_ref[4:5] += col_sum(branch.astype(F32))
        hg_store = load(wide_a, hgrad_hbm, 7)
        each(fc1[0], fc1[2])
        wout_load.wait()
        for rows in halves:
            ags[rows, :] = dot(rows_b[rows, :], wout[...], NT)
        ags[ROWS:, :] = jnp.zeros((PROWS - ROWS, D), F32)
        each(embed, fc2[0])
        att_load.wait()
        put_blocks(wgs.at[0], slice(None), dot(att[...], rows_b[...], TN))
        each(out)
        hg_store.wait()

    pl.run_scoped(attention_out, pltpu.VMEM((D, D), BF), pltpu.VMEM((ROWS, D), BF))

    def attention(qbuf, wqkv):
        q_loads = []

        def load_next():
            k = len(q_loads)
            if k < 2 * UNITS:
                part = qkvp_in.at[k // 2, pl.ds((k % 2) * HALF, HALF)]
                q_loads.append(load(part, qbuf.at[k % 2], 10 + k))

        load_next()
        first_load = load(first_in, tall, 3)
        wqkv_load = load(wqkv_in, wqkv, 6)

        def unit_products(u):
            rows_b[...] = dqs[:ROWS, :].astype(BF)
            put_blocks(wgs.at[SLOT[f"unit_{u}"]], slice(None), dot(tall[...], rows_b[...]))
            for c, row in ((0, 2), (2, 3)):
                vec_ref[row : row + 1, u * UNIT : (u + 1) * UNIT] = col_sum(
                    rows_b[:, c * UNIT : (c + 1) * UNIT].astype(F32)
                )

        def unit_first_grad(u):
            weight = jnp.concatenate(
                [wqkv[:, c * D + u * UNIT : c * D + (u + 1) * UNIT] for c in range(3)], axis=1
            )
            for rows in halves:
                total = dot(rows_b[rows, :], weight, NT)
                wide_a[rows, :] = total if u == 0 else wide_a[rows, :] + total

        def half_unit(u, half):
            q_loads[2 * u + half].wait()
            load_next()
            attn_unit_back(u, half, qbuf, half, ags, dqs)

        half_unit(0, 0)
        each(embed, fc2[1], fc1[2], out)
        half_unit(0, 1)
        each(embed, fc2[0])
        first_load.wait()
        unit_products(0)
        each(units[0])
        wqkv_load.wait()
        unit_first_grad(0)
        each(fc2[1], fc1[1], out, units[0])
        half_unit(1, 0)
        each(fc2[1], fc2[0], fc1[0], fc1[2])
        half_unit(1, 1)
        each(fc2[1], fc1[1], out)
        unit_products(1)
        each(units[1], fc1[0], units[0], fc2[0])
        unit_first_grad(1)
        each(fc1[0], fc1[2], units[1], fc2[0])
        half_unit(2, 0)
        each(fc1[0], fc1[2], fc1[1], out, units[0])
        half_unit(2, 1)
        hg_again = load(hgrad_hbm, ags.at[pl.ds(0, ROWS)], 8)
        each(fc1[2], fc1[1], out, units[1])
        unit_products(2)
        each(units[2], fc1[1], out, units[0])
        unit_first_grad(2)
        x_again = load(x_in, rows_b, 3)
        each(units[1], units[2], units[0])
        hg_again.wait()
        x_again.wait()
        for rows in halves:
            unit, inv = norm(rows_b[rows, :].astype(F32))
            grad = wide_a[rows, :]
            vec_ref[0:1] += col_sum(grad * unit)
            vec_ref[1:2] += col_sum(grad)
            rows_b[rows, :] = (ags[rows, :] + norm_back(unit, inv, grad, gain1_ref[...])).astype(BF)

    pl.run_scoped(
        attention,
        pltpu.VMEM((2, HALF, PADK, 3 * UNIT), BF),
        pltpu.VMEM((D, 3 * D), BF),
    )
    pgrad_store = load(rows_b, pgrad_out, 9)
    for i in range(4):
        vec_ref[8 + i : 9 + i] = b1_ref[:, i * D : (i + 1) * D]
    vec = VectorSum(net, vec_ref, vec_slots)
    each(vec, units[0])

    def decoder(inbox, stage):
        for make in slot_copies:
            make().wait()
        own_slots().wait()
        load(arrived, inbox, 0).wait()
        dev_blocks, most, _ = owner_blocks(seq_count)
        fill = jnp.where(
            lax.broadcasted_iota(jnp.int32, (16, DEC), 0) == 0, token_ref[...], 0.0
        ).astype(BF)

        full = dev_blocks // seq_count

        def store(t, slot):
            rows = dec_out.at[pl.ds(0, full * seq_count)].reshape(full, seq_count, IMG, DEC)
            return pltpu.make_async_copy(
                stage.at[slot, pl.ds(0, full)],
                rows.at[:, first_block(seq_count, t)],
                store_sem.at[slot],
            )

        def last_store(t, slot, act):
            if full < most:
                at = full * seq_count + first_block(seq_count, t)

                @pl.when(at < dev_blocks)
                def _():
                    act(
                        pltpu.make_async_copy(
                            stage.at[slot, full], dec_out.at[at], store_sem.at[2 + slot]
                        )
                    )

        def wait_store(t, slot):
            store(t, slot).wait()
            last_store(t, slot, lambda c: c.wait())

        def spread(t, carry):
            slot = lax.rem(t, 2)

            @pl.when(t >= 2)
            def _():
                wait_store(t - 2, slot)

            source = jnp.concatenate(
                [inbox[slot_rows(t)].reshape(slots * IMG, DEC), fill], axis=0
            )
            rows = dot(one_hot(slots * IMG + 16, code_ref[t]), source, TN).astype(BF)
            stage[slot] = rows[: most * IMG].reshape(most, IMG, DEC)
            store(t, slot).start()
            last_store(t, slot, lambda c: c.start())
            return carry

        per = seq_count // 4
        for part in range(4):
            lax.fori_loop(part * per, (part + 1) * per, spread, 0)
            each(vec, units[1], units[2])
        for t in (seq_count - 2, seq_count - 1):
            wait_store(t, t % 2)

    pl.run_scoped(
        decoder,
        pltpu.VMEM(arrived.shape, BF),
        pltpu.VMEM((2, owner_blocks(seq_count)[1], IMG, DEC), BF),
    )
    vec.end()
    for item in sums.values():
        item.end()
    pgrad_store.wait()


def backward_and_sums(
    egrad, block_in, hidden, act, slope, we, w2, w1, att, qkvp, x, wout, wqkv, second, first, send,
    gain1, gain2, mask_rows, code, token,
):
    dp_count, seq_count = lax.axis_size("dp"), lax.axis_size("seq")
    sizes = axis_sizes(dp_count, seq_count)
    table = chunk_table(dp_count, seq_count)
    nz, ny = sizes["z"], sizes["y"]
    scratch = [
        pltpu.VMEM((ROWS, D), F32),
        pltpu.VMEM((PROWS, D), F32),
        pltpu.VMEM((PROWS, D), F32),
        pltpu.VMEM((D, ROWS), BF),
        pltpu.VMEM((ROWS, D), BF),
        pltpu.VMEM((3, nz, ny, table["out"].padded, D), BF),
        pltpu.VMEM((1, FF), F32),
        pltpu.SemaphoreType.DMA((16,)),
        pltpu.SemaphoreType.DMA((8,)),
        pltpu.SemaphoreType.DMA((16,)),
    ]
    copies = sum(sizes["x"] * 3 + sizes["y"] + sizes["z"] for _ in table)
    copies += sum(sizes.values()) + seq_count
    scratch += [
        pltpu.SemaphoreType.DMA((copies,)),
        pltpu.SemaphoreType.DMA((copies,)),
        pltpu.SemaphoreType.DMA((len(table) * sizes["x"],)),
    ]
    scratch += [pltpu.VMEM((size, VROWS, D), F32) for size in sizes.values()]
    for chunk in table.values():
        scratch += chunk.scratch(sizes)
    anywhere = pl.BlockSpec(memory_space=pl.ANY)
    vmem = pl.BlockSpec(memory_space=pltpu.VMEM)
    outs = pl.pallas_call(
        functools.partial(back_kernel, sizes, table),
        in_specs=[anywhere] * 16 + [vmem] * 5,
        out_specs=[anywhere, vmem] + [anywhere] * (6 + len(table)),
        out_shape=[
            jax.ShapeDtypeStruct((ROWS, D), BF),
            jax.ShapeDtypeStruct((VROWS, D), F32),
            jax.ShapeDtypeStruct((PATCHES, IMG, DEC), BF),
            jax.ShapeDtypeStruct((ROWS, D), F32),
            jax.ShapeDtypeStruct((nz, ny, FF // seq_count, D), BF),
            jax.ShapeDtypeStruct((nz, ny, D // seq_count, FF), BF),
            jax.ShapeDtypeStruct((nz, ny, table["embed"].padded, DEC), BF),
            jax.ShapeDtypeStruct(send.shape, BF),
        ]
        + [jax.ShapeDtypeStruct((dp_count, c.rows, c.cols), BF) for c in table.values()],
        scratch_shapes=scratch,
        compiler_params=pltpu.CompilerParams(
            collective_id=0, has_side_effects=True, vmem_limit_bytes=64 * MIB - 65536
        ),
        name="backward_and_sums",
    )(
        egrad, block_in, hidden, act, slope, we, w2, w1, att, qkvp, x, wout, wqkv, second, first, send,
        gain1, gain2, mask_rows, code, token,
    )
    decoder_input = outs[2].reshape(PATCHES * IMG, DEC)
    return outs[0], outs[1], decoder_input, outs[8:]


def finish_kernel(seq_count, table, vec_ref, dec_in, pgrad_in, *refs):
    parts, refs = refs[: len(table)], refs[len(table) :]
    vecs, (dec_out, pgrad_out) = refs[5:16], refs[16:]
    dec_out[...] = dec_in[...]
    pgrad_out[...] = pgrad_in[...]

    @pl.when(pl.program_id(0) == 0)
    def _():
        finish_sums(seq_count, table, vec_ref, parts, refs[:5], vecs)


def finish_sums(seq_count, table, vec_ref, parts, weights, vecs):
    w2_ref, w1_ref, we_ref, wo_ref, wqkv_ref = weights

    def pieces(name):
        chunk, ref = table[name], parts[list(table).index(name)]
        for q in range(chunk.a * chunk.b):
            row, col = (q // chunk.b) * chunk.r + chunk.r0, chunk.c0 + (q % chunk.b) * chunk.cols
            yield row, col, ref[q].astype(F32)

    for name, ref in (("fc2", w2_ref), ("fc1", w1_ref), ("embed", we_ref), ("out", wo_ref)):
        for key in table:
            if key.split("_")[0] == name:
                for row, col, value in pieces(key):
                    rows = min(value.shape[0], ref.shape[0] - row)
                    if rows > 0:
                        ref[row : row + rows, col : col + value.shape[1]] = value[:rows]
    for u in range(UNITS):
        for row, col, value in pieces(f"unit_{u}"):
            rows = min(value.shape[0], wqkv_ref.shape[0] - row)
            if rows > 0:
                for i in range(value.shape[1] // 128):
                    c, within = (col + i * 128) // UNIT, (col + i * 128) % UNIT
                    to = c * D + u * UNIT + within
                    wqkv_ref[row : row + rows, to : to + 128] = value[
                        :rows, i * 128 : (i + 1) * 128
                    ]

    me = lax.axis_index("seq")

    def mine(row, size, first):
        shift = lax.rem(D - first, D)
        return pltpu.roll(vec_ref[row : row + 8], shift, 1)[:, :size]

    size = D // seq_count
    rows = mine(0, size, me * size)
    for i in range(8):
        vecs[i][...] = rows[i]
    per = seq_count // 4
    chosen = mine(8, FF // seq_count, lax.rem(me, per) * (FF // seq_count))
    at = lax.broadcasted_iota(jnp.int32, chosen.shape, 0)
    vecs[8][...] = jnp.sum(jnp.where(at == me // per, chosen, 0.0), axis=0)
    dec_rows = mine(8, DEC // seq_count, me * (DEC // seq_count))
    vecs[9][...] = dec_rows[4]
    vecs[10][...] = dec_rows[5]


def finish(seq_count, vec, dec, pgrad, parts, table):
    def share(*dims):
        return jax.ShapeDtypeStruct((dims[0] // seq_count, *dims[1:]), F32)

    out_shape = [share(FF, D), share(D, FF), share(D, DEC), share(D, D), share(D, 3 * D)]
    out_shape += [share(D)] * 8 + [share(FF), share(DEC), share(DEC)]
    out_shape += [jax.ShapeDtypeStruct(v.shape, v.dtype) for v in (dec, pgrad)]
    steps = 7
    blocks = [pl.BlockSpec((v.shape[0] // steps, v.shape[1]), lambda i: (i, 0)) for v in (dec, pgrad)]
    return pl.pallas_call(
        functools.partial(finish_kernel, seq_count, table),
        grid=(steps,),
        in_specs=[whole(vec.shape)] + blocks + [whole(v.shape) for v in parts],
        out_specs=[whole(v.shape) for v in out_shape[:16]] + blocks,
        out_shape=out_shape,
        compiler_params=params(),
        name="finish",
    )(vec, dec, pgrad, *parts)


def decoder_codes(keep_index, slots):
    seq_count = lax.axis_size("seq")
    dev_blocks, _, padded = owner_blocks(seq_count)
    t = jnp.arange(seq_count, dtype=jnp.int32)
    start = first_block(seq_count, t)
    lowest = (lax.axis_index("seq") * PATCHES + start) // seq_count
    m = jnp.arange(padded, dtype=jnp.int32)[:, None]
    image = jnp.arange(seq_count * IMG, dtype=jnp.int32)
    lowest_of, start_of = (jnp.repeat(v, IMG)[None, :] for v in (lowest, start))
    place_at = lowest_of + m
    kept = keep_index.T[:, None, :]
    below = (kept < place_at[None]) & (kept >= lowest_of[None])
    found = jnp.sum(jnp.where(kept == place_at[None], 64, below.astype(jnp.int32)), axis=0)
    code = jnp.where(found >= 64, (found - 64) * IMG + image[None, :] % IMG, slots * IMG)
    code = jnp.where(start_of + m * seq_count < dev_blocks, code, -1)
    return code.reshape(padded, seq_count, IMG).transpose(1, 0, 2).reshape(seq_count, 1, -1)


def image_codes(keep_index, slots):
    seq_count = lax.axis_size("seq")
    group_imgs = keep_index.shape[0]
    at = lax.axis_index("seq") * IMG
    own = lax.dynamic_slice_in_dim(keep_index, at, IMG, 0)
    image = jnp.arange(IMG, dtype=jnp.int32)[:, None]
    owner = (own * group_imgs + at + image) // (IMG * PATCHES)
    lower = jnp.sum((owner[:, None, :] < owner[:, :, None]).astype(jnp.int32), axis=2)
    rank = jnp.arange(KEEP, dtype=jnp.int32)[None, :] - lower
    code = (owner * slots + rank) * HALF + image % HALF
    return code.reshape(2, 1, HROWS)


def local(
    patches,
    keep_index,
    ln1_gain,
    ln1_shift,
    w_qkv,
    q_bias,
    v_bias,
    w_out,
    out_bias,
    ln2_gain,
    ln2_shift,
    w_fc1,
    fc1_bias,
    w_fc2,
    fc2_bias,
    w_embed,
    embed_bias,
    mask_token,
    decoder_grad,
):
    seq_count = lax.axis_size("seq")
    slots = 2 * KEEP // seq_count
    dec_code = decoder_codes(keep_index, slots)
    img_code = image_codes(keep_index, slots)
    (
        mask_rows, _, qkvp, attended, hidden, active, slope, block_in, send, second, first, embed_grad,
    ) = forward(
        decoder_grad, patches, w_qkv, w_out, w_fc1, w_fc2, w_embed, dec_code, img_code, ln1_gain, ln1_shift,
        q_bias, v_bias, out_bias, ln2_gain, ln2_shift, fc1_bias.reshape(1, FF), fc2_bias, embed_bias,
    )
    patches_grad, vec, decoder_input, parts = backward_and_sums(
        embed_grad, block_in, hidden, active, slope, w_embed, w_fc2, w_fc1, attended, qkvp, patches, w_out, w_qkv,
        second, first, send, ln1_gain, ln2_gain, mask_rows, dec_code, mask_token,
    )
    table = chunk_table(lax.axis_size("dp"), seq_count)
    (
        w2g, w1g, weg, woutg, wqkvg, ln1g, ln1s, qb, vb, obias, ln2g, ln2s, b2, b1, ebias, mask_grad,
        decoder_input, patches_grad,
    ) = finish(seq_count, vec, decoder_input, patches_grad, parts, table)
    return (
        decoder_input,
        patches_grad,
        ln1g,
        ln1s,
        wqkvg,
        qb,
        vb,
        woutg,
        obias,
        ln2g,
        ln2s,
        w1g,
        b1,
        w2g,
        b2,
        weg,
        ebias,
        mask_grad,
    )


def solution(mesh):
    rows = P(("dp", "seq"), None)
    placed = (rows, P("dp", None)) + (P(),) * 16 + (rows,)
    vec, mat = P("seq"), P("seq", None)
    return jax.shard_map(
        local,
        mesh=mesh,
        in_specs=placed,
        out_specs=(
            rows, rows, vec, vec, mat, vec, vec, mat, vec, vec, vec, mat, vec, mat, vec, mat, vec, vec,
        ),
        check_vma=False,
    )
```

```python
import functools
import math

import jax
import jax.numpy as jnp
from jax import lax
from jax.experimental import pallas as pl
from jax.experimental.pallas import tpu as pltpu
from jax.sharding import PartitionSpec as P

D = 768
HEADS = 12
HEAD = 64
FF = 3072
DEC = 512
PATCHES = 196
KEEP = 49
IMG = 32
HALF = 16
ROWS = IMG * KEEP
HROWS = HALF * KEEP
PADK = 64
UNITS = 3
EPSILON = 1e-06
BF = jnp.bfloat16
F32 = jnp.float32
MIB = 1 << 20

NN = (((1,), (0,)), ((), ()))
NT = (((1,), (1,)), ((), ()))
TN = (((0,), (0,)), ((), ()))


def dot(left, right, dims=NN):
    return lax.dot_general(left, right, dims, preferred_element_type=F32)


def params(mib=60):
    return pltpu.CompilerParams(vmem_limit_bytes=mib * MIB)


def whole(shape):
    return pl.BlockSpec(shape, lambda *_: (0,) * len(shape), pipeline_mode=pl.Buffered(1))


def norm(values):
    centered = values - jnp.mean(values, axis=-1, keepdims=True)
    inv = lax.rsqrt(jnp.mean(centered * centered, axis=-1, keepdims=True) + EPSILON)
    return centered * inv, inv


def norm_back(unit, inv, grad, gain):
    f = grad * gain
    return inv * (
        f
        - jnp.mean(f, axis=-1, keepdims=True)
        - unit * jnp.mean(f * unit, axis=-1, keepdims=True)
    )


def col_sum(values):
    return jnp.sum(values, axis=0, keepdims=True)


def gelu_pair(v):
    cdf = 0.5 + 0.5 * lax.erf(v * (1 / math.sqrt(2.0)))
    return v * cdf, cdf + v * (jnp.exp(-0.5 * v * v) * (1 / math.sqrt(2 * math.pi)))


def one_hot(rows, code):
    at = lax.broadcasted_iota(jnp.int32, (rows, code.shape[1]), 0)
    return jnp.where(at == code, 1.0, 0.0).astype(BF)


def owner_blocks(seq_count):
    dev_blocks = PATCHES
    most = -(-dev_blocks // seq_count)
    return dev_blocks, most, -(-most // 4) * 4


def first_block(seq_count, t):
    return lax.rem(
        t + seq_count - lax.rem(lax.axis_index("seq") * PATCHES, seq_count), seq_count
    )


UNIT = 4 * HEAD
PAIR = 2 * HEAD


def block_diag(rows):
    heads = rows.shape[1] // HEAD
    lane_head = lax.broadcasted_iota(jnp.int32, rows.shape, 1) // HEAD
    zero = jnp.zeros_like(rows)
    return jnp.concatenate([jnp.where(lane_head == h, rows, zero) for h in range(heads)], axis=0)


def fold_pair(rows):
    low = lax.broadcasted_iota(jnp.int32, (PADK, PAIR), 1) < HEAD
    return jnp.where(low, rows[:PADK], rows[PADK:])


def soft(scores, axis):
    valid = lax.broadcasted_iota(jnp.int32, scores.shape, axis) < KEEP
    scores = jnp.where(valid, scores, -1e30)
    e = jnp.exp(scores - jnp.max(scores, axis=axis, keepdims=True))
    return e * (1.0 / jnp.sum(e, axis=axis, keepdims=True))


def each_image(count, image, *refs):
    def group(g, carry):
        base = pl.multiple_of(g * 8 * KEEP, 8)
        views = [ref.at[pl.ds(base, 8 * KEEP + 16)] for ref in refs]
        for near in range(8):
            image(g * 8 + near, near, *views)
        return carry

    lax.fori_loop(0, count // 8, group, 0)


MESH = pl.DeviceIdType.MESH
ORDERS = (("x", "y", "z"), ("y", "x", "z"))
DIMS = {"x": 0, "z": 1, "y": 2}
VROWS = 16
FC1_PARTS = 3


def axis_sizes(dp_count, seq_count):
    z = 4 if seq_count % 4 == 0 else 1
    return {"core": 2, "x": dp_count // 2, "y": seq_count // z, "z": z}


def cut(dp_count, rows, cols):
    for padded in range(rows, rows + 256, 16):
        for a in range(1, dp_count + 1):
            b = dp_count // a
            if a * b == dp_count and padded % (16 * a) == 0 and cols % (128 * b) == 0:
                return a, b, padded
    raise ValueError("no cut")


class Chunk:
    def __init__(self, dp_count, rows, cols, order, half=0, halves=1, first_col=0):
        self.a, self.b, self.padded = cut(dp_count, rows, cols)
        self.r, self.cols = self.padded // self.a, cols // self.b
        self.rows = self.r // halves
        self.r0, self.c0 = half * self.rows, first_col
        self.order = ORDERS[order]

    def scratch(self, sizes):
        dims = [sizes[name] for name in ("x", "z", "y")]
        shapes = [(*dims, self.rows, self.cols)] * 2
        for stage in range(1, 4):
            left = [sizes[name] for name in ("x", "z", "y") if name not in self.order[:stage]]
            shapes.append((sizes[self.order[stage - 1]] - 1, *left, self.rows, self.cols))
        shapes.append((sizes["x"] * 2, self.rows, self.cols))
        return [pltpu.VMEM(shape, BF) for shape in shapes]


def halves_of(dp_count, rows, cols):
    a, _, padded = cut(dp_count, rows, cols)
    return 2 if (padded // a) % 32 == 0 else 1


def chunk_table(dp_count, seq_count):
    table = {}
    rows, span = D // seq_count, FF // FC1_PARTS
    for i in range(FC1_PARTS):
        table[f"fc1_{i}"] = Chunk(dp_count, rows, span, i % 2, first_col=i * span)
    halves = halves_of(dp_count, FF // seq_count, D)
    for h in range(halves):
        table[f"fc2_{h}"] = Chunk(dp_count, FF // seq_count, D, (h + 1) % 2, h, halves)
    table["embed"] = Chunk(dp_count, rows, DEC, 1)
    for i, name in enumerate(("out", "unit_0", "unit_1", "unit_2")):
        table[name] = Chunk(dp_count, rows, D, (i + 1) % 2)
    return table


class Net:
    def __init__(self, sizes, send_sem, recv_sem):
        self.sizes, self.send_sem, self.recv_sem = sizes, send_sem, recv_sem
        self.used = 0
        dp, sq = lax.axis_index("dp"), lax.axis_index("seq")
        ny = sizes["y"]
        self.me = {"core": lax.rem(dp, 2), "x": dp // 2, "y": lax.rem(sq, ny), "z": sq // ny}

    def device(self, axis, value):
        if axis == "seq":
            return {"dp": lax.axis_index("dp"), "seq": value}
        coord = dict(self.me)
        coord[axis] = value
        return {
            "dp": coord["x"] * 2 + coord["core"],
            "seq": coord["z"] * self.sizes["y"] + coord["y"],
        }

    def peer(self, axis, d):
        return lax.rem(self.me[axis] + d, self.sizes[axis])

    def barrier(self):
        sem, count = pltpu.get_barrier_semaphore(), 0
        for axis, size in self.sizes.items():
            if axis in ("core", "x"):
                for d in range(1, size):
                    pl.semaphore_signal(
                        sem, inc=1, device_id=self.device(axis, self.peer(axis, d)), device_id_type=MESH
                    )
                    count += 1
        seq_count = self.sizes["y"] * self.sizes["z"]
        for d in range(1, seq_count):
            to = lax.rem(lax.axis_index("seq") + d, seq_count)
            pl.semaphore_signal(sem, inc=1, device_id=self.device("seq", to), device_id_type=MESH)
            count += 1
        pl.semaphore_wait(sem, count)

    def copy(self, what):
        slot = self.used
        self.used += 1

        def make():
            src, dst, axis, value = what()
            return pltpu.make_async_remote_copy(
                src_ref=src,
                dst_ref=dst,
                send_sem=self.send_sem.at[slot],
                recv_sem=self.recv_sem.at[slot],
                device_id=self.device(axis, value),
                device_id_type=MESH,
            )

        make().start()
        return make


class Sum:
    def __init__(self, net, chunk, source, bufs, local_sems, out):
        self.net, self.chunk, self.source, self.out = net, chunk, source, out
        self.own, self.recv, self.gathered = bufs[0], bufs[1:5], bufs[5]
        self.local_sems = local_sems
        self.at = 0
        self.copies, self.loads = [], []

    def next(self):
        steps = (self.core, self.first, self.second, self.third, self.spread_x, self.spread_core, self.leave)
        if self.at < len(steps):
            steps[self.at]()
            self.at += 1

    def wait(self):
        for make in self.copies:
            make().wait()
        self.copies = []

    def piece(self, x, core):
        k = self.chunk
        q = x * 2 + core
        row = pl.multiple_of((q // k.b) * k.r + k.r0, 16)
        col = pl.multiple_of(k.c0 + lax.rem(q, k.b) * k.cols, 128)
        return self.source.at[:, :, pl.ds(row, k.rows), pl.ds(col, k.cols)]

    def core(self):
        net = self.net

        def send(x):
            other = net.peer("core", 1)
            return self.piece(x, other), self.recv[0].at[x], "core", other

        def load(x):
            return pltpu.make_async_copy(
                self.piece(x, net.me["core"]), self.own.at[x], self.local_sems[x]
            )

        for x in range(net.sizes["x"]):
            self.copies.append(net.copy(functools.partial(send, x)))
        for x in range(net.sizes["x"]):
            load(x).start()
            self.loads.append(functools.partial(load, x))

    def first(self):
        for load in self.loads:
            load().wait()
        self.wait()
        self.add(0)
        self.start(1)

    def second(self):
        self.wait()
        self.add(1)
        self.start(2)

    def third(self):
        self.wait()
        self.add(2)
        self.start(3)

    def start(self, stage):
        net, order = self.net, self.chunk.order
        axis, done = order[stage - 1], order[: stage - 1]

        def send(d):
            value = net.peer(axis, d)
            at = [slice(None)] * 3
            for name in done:
                at[DIMS[name]] = net.me[name]
            at[DIMS[axis]] = value
            return self.own.at[tuple(at)], self.recv[stage].at[d - 1], axis, value

        for d in range(1, net.sizes[axis]):
            self.copies.append(net.copy(functools.partial(send, d)))

    def add(self, stage):
        sizes, me = self.net.sizes, self.net.me
        done = self.chunk.order[:stage]
        left = [name for name in ("x", "z", "y") if name not in done]
        terms = 1 if stage == 0 else sizes[done[-1]] - 1

        def body(k, carry):
            at, rest = {name: me[name] for name in done}, k
            for name in reversed(left):
                at[name] = lax.rem(rest, sizes[name])
                rest = rest // sizes[name]
            here = (at["x"], at["z"], at["y"])
            there = tuple(at[name] for name in left)
            if terms == 1 and stage < 3:
                other = self.recv[stage][there if stage == 0 else (0,) + there]
                self.own[here] = self.own[here] + other
                return carry
            value = self.own[here].astype(F32)
            for d in range(terms):
                value = value + self.recv[stage][(d,) + there].astype(F32)
            if stage == 3:
                self.gathered[me["x"] * 2 + me["core"]] = value.astype(BF)
            else:
                self.own[here] = value.astype(BF)
            return carry

        total = math.prod(sizes[name] for name in left)
        if total == 1:
            body(0, 0)
        else:
            lax.fori_loop(0, total, body, 0)

    def spread_x(self):
        self.wait()
        self.add(3)
        net = self.net

        def send(d):
            mine = self.gathered.at[net.me["x"] * 2 + net.me["core"]]
            return mine, mine, "x", net.peer("x", d)

        for d in range(1, net.sizes["x"]):
            self.copies.append(net.copy(functools.partial(send, d)))

    def spread_core(self):
        self.wait()
        net = self.net

        def send(x):
            mine = self.gathered.at[x * 2 + net.me["core"]]
            return mine, mine, "core", net.peer("core", 1)

        for x in range(net.sizes["x"]):
            self.copies.append(net.copy(functools.partial(send, x)))

    def leave(self):
        self.wait()

        def store():
            return pltpu.make_async_copy(self.gathered, self.out, self.local_sems[0])

        store().start()
        self.loads = [store]

    def end(self):
        while self.at < 7:
            self.next()
        self.loads[0]().wait()


class VectorSum:
    def __init__(self, net, value, slots):
        self.net, self.value, self.slots = net, value, slots
        self.left = [name for name, size in net.sizes.items() if size > 1]
        self.copies = []

    def next(self):
        net = self.net
        if self.copies:
            for make in self.copies:
                make().wait()
            total = self.now[0]
            for i in range(1, net.sizes[self.axis]):
                total = total + self.now[i]
            self.value[...] = total
            self.copies = []
        if self.left:
            axis = self.axis = self.left.pop(0)
            now = self.now = self.slots[axis]
            now[net.me[axis]] = self.value[...]

            def send(d):
                mine = now.at[net.me[axis]]
                return mine, mine, axis, net.peer(axis, d)

            for d in range(1, net.sizes[axis]):
                self.copies.append(net.copy(functools.partial(send, d)))

    def end(self):
        while self.left or self.copies:
            self.next()


FTILE = 512
FSTEPS = FF // FTILE


def forward_kernel(sizes, *refs):
    (
        dec_in, x_in, wqkv_in, wout_in, w1_in, w2_in, we_in,
        code_ref, icode_ref, gain1_ref, shift1_ref, qb_ref, vb_ref, ob_ref, gain2_ref, shift2_ref, b1_ref, b2_ref, be_ref,
    ) = refs[:19]
    (
        mask_ref, returned, qkvp_out, att_out, hidden_out, act_out, slope_out, block_out, send_out, second_out,
        first_out, egrad_out,
    ) = refs[19:31]
    slot_buf, hid, xbuf, wqkv, wout, load_sem, tile_sem, store_sem, send_sem, recv_sem = refs[31:]
    net = Net(sizes, send_sem, recv_sem)
    net.barrier()
    seq_count = sizes["y"] * sizes["z"]
    slots = returned.shape[0] // seq_count
    me = lax.axis_index("seq")
    halves = [slice(0, HROWS), slice(HROWS, ROWS)]

    def load(src, dst, slot):
        c = pltpu.make_async_copy(src, dst, load_sem.at[slot])
        c.start()
        return c

    def slot_rows(owner):
        return pl.ds(owner * slots, slots)

    def slot_copy(d):
        return pltpu.make_async_remote_copy(
            src_ref=slot_buf.at[slot_rows(d)],
            dst_ref=returned.at[slot_rows(me)],
            send_sem=send_sem.at[d],
            recv_sem=recv_sem.at[d],
            device_id=net.device("seq", lax.rem(me + d, seq_count)),
            device_id_type=MESH,
        )

    def pick(dec):
        dec_load = load(dec_in, dec, 0)
        x_load = load(x_in, xbuf, 1)
        wqkv_load = load(wqkv_in, wqkv, 2)
        wout_load = load(wout_in, wout, 3)
        mask_ref[...] = jnp.zeros_like(mask_ref)
        dev_blocks, most, padded = owner_blocks(seq_count)
        dec_load.wait()

        def pick_for(d):
            t = lax.rem(me + d, seq_count)
            start = first_block(seq_count, t)
            pieces = []
            for m in range(most):
                at = jnp.minimum(start + m * seq_count, dev_blocks - 1)
                pieces.append(dec[pl.ds(pl.multiple_of(at * IMG, IMG), IMG), :])
            if padded > most:
                pieces.append(jnp.zeros(((padded - most) * IMG, DEC), BF))
            picked = dot(one_hot(slots * IMG + 16, code_ref[t]), jnp.concatenate(pieces, axis=0))
            slot_buf[slot_rows(d)] = picked[: slots * IMG].astype(BF).reshape(slots, IMG, DEC)
            mask_ref[...] += picked[slots * IMG : slots * IMG + 8]

        def far(k, carry):
            pick_for(k)
            slot_copy(k).start()
            return carry

        lax.fori_loop(seq_count // 2, seq_count, far, 0)
        lax.fori_loop(1, seq_count // 2, far, 0)
        pick_for(0)
        load(slot_buf.at[slot_rows(0)], returned.at[slot_rows(me)], 4)
        for c in (x_load, wqkv_load, wout_load):
            c.wait()

    pl.run_scoped(pick, pltpu.VMEM((PATCHES * IMG, DEC), BF))

    def attention(qs, ats, qstage, astage):
        def stores(g):
            rows = pl.ds(pl.multiple_of(g * HROWS, 16), HROWS)
            return [
                pltpu.make_async_copy(
                    qstage, qkvp_out.at[:, pl.ds(g * HALF, HALF)], store_sem.at[0]
                ),
                pltpu.make_async_copy(astage, att_out.at[rows], store_sem.at[1]),
            ]

        def half(g, carry):
            rows = pl.ds(pl.multiple_of(g * HROWS, 16), HROWS)
            unit, _ = norm(xbuf[rows, :].astype(F32))
            first = (unit * gain1_ref[...] + shift1_ref[...]).astype(BF)
            for c in range(3):
                cols = slice(c * D, (c + 1) * D)
                value = dot(first, wqkv[:, cols])
                if c != 1:
                    value = value + (qb_ref[...] if c == 0 else vb_ref[...])
                qs[:HROWS, cols] = value.astype(BF).astype(F32)
            qs[HROWS:, :] = jnp.zeros((16, 3 * D), F32)

            @pl.when(g == 1)
            def _():
                for c in stores(0):
                    c.wait()

            def image(i, near, qs, ats):
                r0 = near * KEEP
                for u in range(HEADS // 2):
                    part = []
                    for c in range(3):
                        cols = slice(c * D + u * PAIR, c * D + (u + 1) * PAIR)
                        value = qs[r0 : r0 + PADK, cols].astype(BF)
                        to = c * UNIT + (u % 2) * PAIR
                        qstage[u // 2, i, :, to : to + PAIR] = value
                        part.append(value)
                    q, k, v = part
                    probs = soft(dot(block_diag(q * BF(0.125)), k, NT).T, 0).astype(BF)
                    to = 3 * UNIT + (u % 2) * PAIR
                    qstage[u // 2, i, :, to : to + PAIR] = probs
                    out = fold_pair(dot(probs, v, TN))
                    ats[r0 : r0 + 56, u * PAIR : (u + 1) * PAIR] = out[:56]

            each_image(HALF, image, qs, ats)
            att = ats[:HROWS, :].astype(BF)
            astage[...] = att
            for c in stores(g):
                c.start()
            hid[rows, :] = xbuf[rows, :].astype(F32) + (dot(att, wout[...]) + ob_ref[...])
            return carry

        lax.fori_loop(0, 2, half, 0)
        for c in stores(1):
            c.wait()

    pl.run_scoped(
        attention,
        pltpu.VMEM((HROWS + 16, 3 * D), F32),
        pltpu.VMEM((HROWS + 16, D), F32),
        pltpu.VMEM((UNITS, HALF, PADK, 4 * UNIT), BF),
        pltpu.VMEM((HROWS, D), BF),
    )
    hid_store = load(hid, hidden_out, 5)

    def feed_forward(second, acc, turned, w1s, w2s, acts, slopes, we, emb, boxes):
        def columns(k):
            return pl.ds(pl.multiple_of(k * FTILE, FTILE), FTILE)

        def loads(k, slot):
            pairs = ((w1_in.at[:, columns(k)], w1s), (w2_in.at[columns(k), :], w2s))
            return [
                pltpu.make_async_copy(src, dst.at[slot], tile_sem.at[slot * 2 + i])
                for i, (src, dst) in enumerate(pairs)
            ]

        def stores(k, slot):
            pairs = ((acts, act_out), (slopes, slope_out))
            return [
                pltpu.make_async_copy(src.at[slot], dst.at[:, columns(k)], store_sem.at[slot * 2 + i])
                for i, (src, dst) in enumerate(pairs)
            ]

        for c in loads(0, 0):
            c.start()
        we_load = load(we_in, we, 6)
        for rows in halves:
            unit, _ = norm(hid[rows, :])
            second[rows, :] = (unit * gain2_ref[...] + shift2_ref[...]).astype(BF)
            acc[rows, :] = hid[rows, :] + b2_ref[...]

        def tile(k, carry):
            slot = lax.rem(k, 2)
            for c in loads(k, slot):
                c.wait()

            @pl.when(k + 1 < FSTEPS)
            def _():
                for c in loads(k + 1, 1 - slot):
                    c.start()

            @pl.when(k >= 2)
            def _():
                for c in stores(k - 2, slot):
                    c.wait()

            for rows in halves:
                inner = dot(second[rows, :], w1s[slot]) + b1_ref[:, columns(k)]
                active, slope = gelu_pair(inner)
                active = active.astype(BF)
                acts[slot, rows, :] = active
                slopes[slot, rows, :] = slope.astype(BF)
                acc[rows, :] += dot(active, w2s[slot])
            for c in stores(k, slot):
                c.start()
            return carry

        lax.fori_loop(0, FSTEPS, tile, 0)
        for rows in halves:
            turned[:, rows] = second[rows, :].T
        second_store = load(turned, second_out, 7)
        second[...] = acc[...].astype(BF)
        block_store = load(second, block_out, 8)
        we_load.wait()
        emb[...] = (dot(second[...], we[...]) + be_ref[...]).astype(BF)
        count = seq_count * slots

        def box_store(g):
            return pltpu.make_async_copy(
                boxes.at[g], send_out.at[:, pl.ds(g * HALF, HALF)], tile_sem.at[4 + g]
            )

        def pack(g, carry):
            rows = pl.ds(pl.multiple_of(g * HROWS, 16), HROWS)
            boxes[g] = (
                dot(one_hot(count * HALF, icode_ref[g]), emb[rows, :])
                .astype(BF)
                .reshape(count, HALF, DEC)
            )
            box_store(g).start()
            return carry

        lax.fori_loop(0, 2, pack, 0)
        for k in (FSTEPS - 2, FSTEPS - 1):
            for c in stores(k, k % 2):
                c.wait()
        second_store.wait()
        for rows in halves:
            unit, _ = norm(xbuf[rows, :].astype(F32))
            turned[:, rows] = (unit * gain1_ref[...] + shift1_ref[...]).astype(BF).T
        first_store = load(turned, first_out, 7)
        for g in range(2):
            box_store(g).wait()
        block_store.wait()
        first_store.wait()

    pl.run_scoped(
        feed_forward,
        pltpu.VMEM((ROWS, D), BF),
        pltpu.VMEM((ROWS, D), F32),
        pltpu.VMEM((D, ROWS), BF),
        pltpu.VMEM((2, D, FTILE), BF),
        pltpu.VMEM((2, FTILE, D), BF),
        pltpu.VMEM((2, ROWS, FTILE), BF),
        pltpu.VMEM((2, ROWS, FTILE), BF),
        pltpu.VMEM((D, DEC), BF),
        pltpu.VMEM((ROWS, DEC), BF),
        pltpu.VMEM((2, seq_count * slots, HALF, DEC), BF),
    )

    def unpack(egrad):
        pltpu.make_async_copy(
            slot_buf.at[slot_rows(0)], returned.at[slot_rows(me)], load_sem.at[4]
        ).wait()
        for d in range(1, seq_count):
            slot_copy(d).wait()
        load(returned, slot_buf, 4).wait()
        for g in range(2):
            source = slot_buf[:, g * HALF : (g + 1) * HALF].reshape(seq_count * slots * HALF, DEC)
            rows = slice(g * HROWS, (g + 1) * HROWS)
            egrad[rows, :] = dot(one_hot(seq_count * slots * HALF, icode_ref[g]), source, TN).astype(BF)
        load(egrad, egrad_out, 4).wait()

    pl.run_scoped(unpack, pltpu.VMEM((ROWS, DEC), BF))
    hid_store.wait()


def forward(
    dec_grad, x, wqkv, wout, w1, w2, we, code, icode, gain1, shift1, qb, vb, ob, gain2, shift2, b1, b2, be
):
    dp_count, seq_count = lax.axis_size("dp"), lax.axis_size("seq")
    sizes = axis_sizes(dp_count, seq_count)
    count = seq_count * (2 * KEEP // seq_count)
    anywhere = pl.BlockSpec(memory_space=pl.ANY)
    vmem = pl.BlockSpec(memory_space=pltpu.VMEM)
    out = jax.ShapeDtypeStruct
    return pl.pallas_call(
        functools.partial(forward_kernel, sizes),
        in_specs=[anywhere] * 7 + [vmem] * 12,
        out_specs=[vmem] + [anywhere] * 11,
        out_shape=[
            out((8, DEC), F32),
            out((count, IMG, DEC), BF),
            out((UNITS, IMG, PADK, 4 * UNIT), BF),
            out((ROWS, D), BF),
            out((ROWS, D), F32),
            out((ROWS, FF), BF),
            out((ROWS, FF), BF),
            out((ROWS, D), BF),
            out((count, IMG, DEC), BF),
            out((D, ROWS), BF),
            out((D, ROWS), BF),
            out((ROWS, DEC), BF),
        ],
        scratch_shapes=[
            pltpu.VMEM((count, IMG, DEC), BF),
            pltpu.VMEM((ROWS, D), F32),
            pltpu.VMEM((ROWS, D), BF),
            pltpu.VMEM((D, 3 * D), BF),
            pltpu.VMEM((D, D), BF),
            pltpu.SemaphoreType.DMA((9,)),
            pltpu.SemaphoreType.DMA((6,)),
            pltpu.SemaphoreType.DMA((4,)),
            pltpu.SemaphoreType.DMA((seq_count,)),
            pltpu.SemaphoreType.DMA((seq_count,)),
        ],
        compiler_params=pltpu.CompilerParams(
            collective_id=1, has_side_effects=True, vmem_limit_bytes=64 * MIB - 65536
        ),
        name="forward",
    )(
        dec_grad, x, wqkv, wout, w1, w2, we, code, icode, gain1, shift1, qb, vb, ob, gain2, shift2, b1, b2, be
    )


PROWS = ROWS + 16
SLOT = {"out": 0, "unit_0": 1, "unit_1": 2, "unit_2": 0}


def attn_unit_back(u, half, qbuf, slot, ags, dqs):
    def image(i, near, ags, dqs):
        r0 = near * KEEP
        valid = lax.broadcasted_iota(jnp.int32, (PADK, UNIT), 0) < KEEP
        q, k, v, probs_in = (qbuf[slot, i, :, c * UNIT : (c + 1) * UNIT] for c in range(4))
        q_diag = block_diag(q * BF(0.125))
        probs = probs_in.astype(F32)
        agrad = jnp.where(valid, ags[r0 : r0 + PADK, u * UNIT : (u + 1) * UNIT], 0.0).astype(BF)
        a_diag = block_diag(agrad)
        pgrad = dot(v, a_diag, NT)
        inner = jnp.sum(probs * pgrad, axis=0, keepdims=True)
        sgrad = (probs * (pgrad - inner)).astype(BF)
        whole_q = dot(sgrad, k, TN)
        qgrad = 0.125 * jnp.concatenate(
            [
                fold_pair(whole_q[e * 2 * PADK : (e + 1) * 2 * PADK, e * PAIR : (e + 1) * PAIR])
                for e in range(2)
            ],
            axis=1,
        )
        for c, grad in enumerate((qgrad, dot(sgrad, q_diag), dot(probs_in, a_diag))):
            dqs[r0 : r0 + 56, c * UNIT : (c + 1) * UNIT] = grad[:56]

    rows = pl.ds(half * HROWS, HROWS + 16)
    each_image(HALF, image, ags.at[rows], dqs.at[rows])


SCHEDULE = {
    "P": ("embed",),
    "F2": ("fc2_0", "fc2_1", "embed",),
    "F1a": ("fc1_0", "embed", "fc2_0", "fc2_1",),
    "F1b": ("fc1_1", "embed", "fc1_0",),
    "F1c": ("fc1_2", "fc2_1", "fc1_1",),
    "LN2b": ("fc1_0", "fc1_2",),
    "ags": ("embed", "fc2_0",),
    "wout": ("out",),
    "h00": ("embed", "fc2_1", "fc1_2", "out",),
    "h01": ("embed", "fc2_0",),
    "p0": ("unit_0",),
    "f0": ("fc2_1", "fc1_1", "out", "unit_0",),
    "h10": ("fc2_1", "fc2_0", "fc1_0", "fc1_2",),
    "h11": ("fc2_1", "fc1_1", "out",),
    "p1": ("unit_1", "fc1_0", "unit_0", "fc2_0",),
    "f1": ("fc1_0", "fc1_2", "unit_1", "fc2_0",),
    "h20": ("fc1_0", "fc1_2", "fc1_1", "out", "unit_0",),
    "h21": ("fc1_2", "fc1_1", "out", "unit_1",),
    "p2": ("unit_2", "fc1_1", "out", "unit_0",),
    "f2": ("unit_1", "unit_2", "unit_0",),
    "LN1b": ("unit_0",),
    "D0": ("unit_1", "unit_2",),
    "D1": ("unit_1", "unit_2",),
    "D2": ("unit_1", "unit_2",),
    "D3": ("unit_1", "unit_2",),
}


BT = 512
TILES = FF // BT


def back_kernel(sizes, table, *refs):
    names = list(table)
    (
        egrad_in, block_in, hidden_in, act_in, slope_in, we_in, w2_in, w1_in, att_in, qkvp_in, x_in, wout_in, wqkv_in, second_in, first_in,
        send_in, gain1_ref, gain2_ref, mask_ref, code_ref, token_ref,
    ) = refs[:21]
    pgrad_out, vec_ref, dec_out, hgrad_hbm, w2g_hbm, w1g_hbm, weg_hbm, arrived = refs[21:29]
    outs, refs = refs[29 : 29 + len(names)], refs[29 + len(names) :]
    (
        wide_a, ags, dqs, tall, rows_b, wgs, b1_ref, load_sem, tile_sem, store_sem, send_sem, recv_sem, local_sem,
    ) = refs[:13]
    refs = refs[13:]
    vec_slots = {name: refs[i] for i, name in enumerate(sizes)}
    refs = refs[len(sizes) :]

    net = Net(sizes, send_sem, recv_sem)
    net.barrier()
    seq_count = sizes["y"] * sizes["z"]
    slots = arrived.shape[0] // seq_count
    seq_me = lax.axis_index("seq")

    def slot_rows(owner):
        return pl.ds(owner * slots, slots)

    def slot_send(d):
        to = lax.rem(seq_me + d, seq_count)
        return send_in.at[slot_rows(to)], arrived.at[slot_rows(seq_me)], "seq", to

    slot_copies = [net.copy(functools.partial(slot_send, d)) for d in range(1, seq_count)]

    def own_slots():
        return pltpu.make_async_copy(
            send_in.at[slot_rows(seq_me)], arrived.at[slot_rows(seq_me)], load_sem.at[2]
        )

    own_slots().start()
    sources = {"fc2": w2g_hbm, "fc1": w1g_hbm, "embed": weg_hbm}
    sums = {}
    for i, name in enumerate(names):
        sums[name] = Sum(
            net,
            table[name],
            wgs.at[SLOT[name]] if name in SLOT else sources[name.split("_")[0]],
            refs[6 * i : 6 * (i + 1)],
            [local_sem.at[i * sizes["x"] + x] for x in range(sizes["x"])],
            outs[i],
        )

    def step(place):
        for name in SCHEDULE.get(place, ()):
            if name in sums:
                sums[name].next()

    def load(src, dst, slot):
        c = pltpu.make_async_copy(src, dst, load_sem.at[slot])
        c.start()
        return c

    ny, blocks = sizes["y"], sizes["y"] * sizes["z"]
    block_rows = D // blocks
    halves = [slice(0, HROWS), slice(HROWS, ROWS)]

    def put_blocks(ref, cols, value):
        for t in range(blocks):
            ref[t // ny, t % ny, :block_rows, cols] = value[
                t * block_rows : (t + 1) * block_rows
            ].astype(BF)

    def clear_padding(ref):
        pad = ref.shape[-2] - block_rows
        if pad:
            ref[..., block_rows:, :] = jnp.zeros((*ref.shape[:-2], pad, ref.shape[-1]), BF)

    clear_padding(wgs)
    vec_ref[...] = jnp.zeros_like(vec_ref)
    vec_ref[13:14, :DEC] = mask_ref[:1]

    third = FF // blocks // 3

    def columns(k):
        return pl.ds(pl.multiple_of(k * BT, BT), BT)

    hidden_load = load(hidden_in, ags.at[pl.ds(0, ROWS)], 3)
    second_load = load(second_in, tall, 8)

    def embedding(egrad, block, we, weg):
        clear_padding(weg)
        eg_load = load(egrad_in, egrad, 0)
        we_load = load(we_in, we, 1)
        block_load = load(block_in, block, 4)
        eg_load.wait()
        we_load.wait()
        for rows in halves:
            out_grad = dot(egrad[rows, :], we[...], NT)
            wide_a[rows, :] = out_grad
            two = out_grad.astype(BF)
            rows_b[rows, :] = two
            vec_ref[7:8] += col_sum(two.astype(F32))
            vec_ref[12:13, :DEC] += col_sum(egrad[rows, :].astype(F32))
        block_load.wait()
        put_blocks(weg, slice(None), dot(block[...], egrad[...], TN))
        load(weg, weg_hbm, 5).wait()
        step("P")

    pl.run_scoped(
        embedding,
        pltpu.VMEM((ROWS, DEC), BF),
        pltpu.VMEM((ROWS, D), BF),
        pltpu.VMEM((D, DEC), BF),
        pltpu.VMEM(weg_hbm.shape, BF),
    )

    def second_weight(acts, stage):
        def act_load(k, slot):
            return pltpu.make_async_copy(act_in.at[:, columns(k)], acts.at[slot], tile_sem.at[slot])

        def stores(k, slot):
            copies = []
            for i in range(BT // third):
                block = k * (BT // third) + i
                owner = block // 3
                rows = pl.ds(pl.multiple_of(lax.rem(block, 3) * third, third), third)
                copies.append(
                    pltpu.make_async_copy(
                        stage.at[slot, pl.ds(i * third, third)],
                        w2g_hbm.at[owner // ny, lax.rem(owner, ny), rows],
                        store_sem.at[slot * (BT // third) + i],
                    )
                )
            return copies

        act_load(0, 0).start()

        def tile(k, carry):
            slot = lax.rem(k, 2)
            act_load(k, slot).wait()

            @pl.when(k + 1 < TILES)
            def _():
                act_load(k + 1, 1 - slot).start()

            @pl.when(k >= 2)
            def _():
                for c in stores(k - 2, slot):
                    c.wait()

            stage[slot] = dot(acts[slot], rows_b[...], TN).astype(BF)
            for c in stores(k, slot):
                c.start()
            return carry

        lax.fori_loop(0, TILES, tile, 0)
        for k in (TILES - 2, TILES - 1):
            for c in stores(k, k % 2):
                c.wait()

    pl.run_scoped(second_weight, pltpu.VMEM((2, ROWS, BT), BF), pltpu.VMEM((2, BT, D), BF))
    step("F2")

    def first_weight(slopes, w2s, w1s, stage):
        def loads(k, slot):
            pairs = (
                (slope_in.at[:, columns(k)], slopes),
                (w2_in.at[columns(k), :], w2s),
                (w1_in.at[:, columns(k)], w1s),
            )
            return [
                pltpu.make_async_copy(src, dst.at[slot], tile_sem.at[slot * 3 + i])
                for i, (src, dst) in enumerate(pairs)
            ]

        def store(k):
            return pltpu.make_async_copy(stage, w1g_hbm.at[:, :, :, columns(k)], store_sem.at[0])

        per = TILES // FC1_PARTS
        for c in loads(0, 0):
            c.start()
        hidden_load.wait()
        second_load.wait()
        dqs[...] = jnp.zeros_like(dqs)
        step("LN2")

        def tile(k, carry):
            slot = lax.rem(k, 2)
            for c in loads(k, slot):
                c.wait()

            @pl.when(k + 1 < TILES)
            def _():
                for c in loads(k + 1, 1 - slot):
                    c.start()

            inner = (dot(rows_b[...], w2s[slot], NT) * slopes[slot].astype(F32)).astype(BF)
            b1_ref[:, columns(k)] = col_sum(inner.astype(F32))
            grad = dot(tall[...], inner)

            @pl.when(lax.rem(k, per) > 0)
            def _():
                store(k - 1).wait()

            put_blocks(stage, slice(None), grad)
            store(k).start()
            dqs[:ROWS, :] += dot(inner, w1s[slot], NT)
            return carry

        for part in range(FC1_PARTS):
            lax.fori_loop(part * per, (part + 1) * per, tile, 0)
            store((part + 1) * per - 1).wait()
            step(("F1a", "F1b", "F1c")[part])

    pl.run_scoped(
        first_weight,
        pltpu.VMEM((2, ROWS, BT), BF),
        pltpu.VMEM((2, BT, D), BF),
        pltpu.VMEM((2, D, BT), BF),
        pltpu.VMEM((sizes["z"], ny, block_rows, BT), BF),
    )

    def attention_out(wout, att):
        wout_load = load(wout_in, wout, 4)
        att_load = load(att_in, att, 5)
        for rows in halves:
            unit, inv = norm(ags[rows, :])
            grad = dqs[rows, :]
            vec_ref[5:6] += col_sum(grad * unit)
            vec_ref[6:7] += col_sum(grad)
            hgrad = wide_a[rows, :] + norm_back(unit, inv, grad, gain2_ref[...])
            wide_a[rows, :] = hgrad
            branch = hgrad.astype(BF)
            rows_b[rows, :] = branch
            vec_ref[4:5] += col_sum(branch.astype(F32))
        hg_store = load(wide_a, hgrad_hbm, 7)
        step("LN2b")
        wout_load.wait()
        for rows in halves:
            ags[rows, :] = dot(rows_b[rows, :], wout[...], NT)
        ags[ROWS:, :] = jnp.zeros((PROWS - ROWS, D), F32)
        step("ags")
        att_load.wait()
        put_blocks(wgs.at[0], slice(None), dot(att[...], rows_b[...], TN))
        step("wout")
        hg_store.wait()

    pl.run_scoped(attention_out, pltpu.VMEM((D, D), BF), pltpu.VMEM((ROWS, D), BF))

    def attention(qbuf, wqkv):
        q_loads = []

        def load_next():
            k = len(q_loads)
            if k < 2 * UNITS:
                part = qkvp_in.at[k // 2, pl.ds((k % 2) * HALF, HALF)]
                q_loads.append(load(part, qbuf.at[k % 2], 10 + k))

        load_next()
        first_load = load(first_in, tall, 3)
        wqkv_load = load(wqkv_in, wqkv, 6)

        def unit_products(u):
            rows_b[...] = dqs[:ROWS, :].astype(BF)
            put_blocks(wgs.at[SLOT[f"unit_{u}"]], slice(None), dot(tall[...], rows_b[...]))
            for c, row in ((0, 2), (2, 3)):
                vec_ref[row : row + 1, u * UNIT : (u + 1) * UNIT] = col_sum(
                    rows_b[:, c * UNIT : (c + 1) * UNIT].astype(F32)
                )

        def unit_first_grad(u):
            weight = jnp.concatenate(
                [wqkv[:, c * D + u * UNIT : c * D + (u + 1) * UNIT] for c in range(3)], axis=1
            )
            for rows in halves:
                total = dot(rows_b[rows, :], weight, NT)
                wide_a[rows, :] = total if u == 0 else wide_a[rows, :] + total

        def half_unit(u, half):
            q_loads[2 * u + half].wait()
            load_next()
            attn_unit_back(u, half, qbuf, half, ags, dqs)

        for u in range(UNITS):
            for half in range(2):
                half_unit(u, half)
                if (u, half) == (UNITS - 1, 1):
                    hg_again = load(hgrad_hbm, ags.at[pl.ds(0, ROWS)], 8)
                step(f"h{u}{half}")
            if u == 0:
                first_load.wait()
            unit_products(u)
            step(f"p{u}")
            if u == 0:
                wqkv_load.wait()
            unit_first_grad(u)
            if u == UNITS - 1:
                x_again = load(x_in, rows_b, 3)
            step(f"f{u}")
        hg_again.wait()
        x_again.wait()
        for rows in halves:
            unit, inv = norm(rows_b[rows, :].astype(F32))
            grad = wide_a[rows, :]
            vec_ref[0:1] += col_sum(grad * unit)
            vec_ref[1:2] += col_sum(grad)
            rows_b[rows, :] = (ags[rows, :] + norm_back(unit, inv, grad, gain1_ref[...])).astype(BF)

    pl.run_scoped(
        attention,
        pltpu.VMEM((2, HALF, PADK, 4 * UNIT), BF),
        pltpu.VMEM((D, 3 * D), BF),
    )
    pgrad_store = load(rows_b, pgrad_out, 9)
    for i in range(4):
        vec_ref[8 + i : 9 + i] = b1_ref[:, i * D : (i + 1) * D]
    vec = VectorSum(net, vec_ref, vec_slots)
    vec.next()
    step("LN1b")

    def decoder(inbox, stage):
        for make in slot_copies:
            make().wait()
        own_slots().wait()
        load(arrived, inbox, 0).wait()
        dev_blocks, most, _ = owner_blocks(seq_count)
        fill = jnp.where(
            lax.broadcasted_iota(jnp.int32, (16, DEC), 0) == 0, token_ref[...], 0.0
        ).astype(BF)

        full = dev_blocks // seq_count

        def store(t, slot):
            rows = dec_out.at[pl.ds(0, full * seq_count)].reshape(full, seq_count, IMG, DEC)
            return pltpu.make_async_copy(
                stage.at[slot, pl.ds(0, full)],
                rows.at[:, first_block(seq_count, t)],
                store_sem.at[slot],
            )

        def last_store(t, slot, act):
            if full < most:
                at = full * seq_count + first_block(seq_count, t)

                @pl.when(at < dev_blocks)
                def _():
                    act(
                        pltpu.make_async_copy(
                            stage.at[slot, full], dec_out.at[at], store_sem.at[2 + slot]
                        )
                    )

        def wait_store(t, slot):
            store(t, slot).wait()
            last_store(t, slot, lambda c: c.wait())

        def spread(t, carry):
            slot = lax.rem(t, 2)

            @pl.when(t >= 2)
            def _():
                wait_store(t - 2, slot)

            source = jnp.concatenate(
                [inbox[slot_rows(t)].reshape(slots * IMG, DEC), fill], axis=0
            )
            rows = dot(one_hot(slots * IMG + 16, code_ref[t]), source, TN).astype(BF)
            stage[slot] = rows[: most * IMG].reshape(most, IMG, DEC)
            store(t, slot).start()
            last_store(t, slot, lambda c: c.start())
            return carry

        per = seq_count // 4
        for part in range(4):
            lax.fori_loop(part * per, (part + 1) * per, spread, 0)
            vec.next()
            step(f"D{part}")
        for t in (seq_count - 2, seq_count - 1):
            wait_store(t, t % 2)

    pl.run_scoped(
        decoder,
        pltpu.VMEM(arrived.shape, BF),
        pltpu.VMEM((2, owner_blocks(seq_count)[1], IMG, DEC), BF),
    )
    vec.end()
    for item in sums.values():
        item.end()
    pgrad_store.wait()


def backward_and_sums(
    egrad, block_in, hidden, act, slope, we, w2, w1, att, qkvp, x, wout, wqkv, second, first, send,
    gain1, gain2, mask_rows, code, token,
):
    dp_count, seq_count = lax.axis_size("dp"), lax.axis_size("seq")
    sizes = axis_sizes(dp_count, seq_count)
    table = chunk_table(dp_count, seq_count)
    nz, ny = sizes["z"], sizes["y"]
    scratch = [
        pltpu.VMEM((ROWS, D), F32),
        pltpu.VMEM((PROWS, D), F32),
        pltpu.VMEM((PROWS, D), F32),
        pltpu.VMEM((D, ROWS), BF),
        pltpu.VMEM((ROWS, D), BF),
        pltpu.VMEM((3, nz, ny, table["out"].padded, D), BF),
        pltpu.VMEM((1, FF), F32),
        pltpu.SemaphoreType.DMA((16,)),
        pltpu.SemaphoreType.DMA((8,)),
        pltpu.SemaphoreType.DMA((16,)),
    ]
    copies = sum(sizes["x"] * 3 + sizes["y"] + sizes["z"] for _ in table)
    copies += sum(sizes.values()) + seq_count
    scratch += [
        pltpu.SemaphoreType.DMA((copies,)),
        pltpu.SemaphoreType.DMA((copies,)),
        pltpu.SemaphoreType.DMA((len(table) * sizes["x"],)),
    ]
    scratch += [pltpu.VMEM((size, VROWS, D), F32) for size in sizes.values()]
    for chunk in table.values():
        scratch += chunk.scratch(sizes)
    anywhere = pl.BlockSpec(memory_space=pl.ANY)
    vmem = pl.BlockSpec(memory_space=pltpu.VMEM)
    outs = pl.pallas_call(
        functools.partial(back_kernel, sizes, table),
        in_specs=[anywhere] * 16 + [vmem] * 5,
        out_specs=[anywhere, vmem] + [anywhere] * (6 + len(table)),
        out_shape=[
            jax.ShapeDtypeStruct((ROWS, D), BF),
            jax.ShapeDtypeStruct((VROWS, D), F32),
            jax.ShapeDtypeStruct((PATCHES, IMG, DEC), BF),
            jax.ShapeDtypeStruct((ROWS, D), F32),
            jax.ShapeDtypeStruct((nz, ny, FF // seq_count, D), BF),
            jax.ShapeDtypeStruct((nz, ny, D // seq_count, FF), BF),
            jax.ShapeDtypeStruct((nz, ny, table["embed"].padded, DEC), BF),
            jax.ShapeDtypeStruct(send.shape, BF),
        ]
        + [jax.ShapeDtypeStruct((dp_count, c.rows, c.cols), BF) for c in table.values()],
        scratch_shapes=scratch,
        compiler_params=pltpu.CompilerParams(
            collective_id=0, has_side_effects=True, vmem_limit_bytes=64 * MIB - 65536
        ),
        name="backward_and_sums",
    )(
        egrad, block_in, hidden, act, slope, we, w2, w1, att, qkvp, x, wout, wqkv, second, first, send,
        gain1, gain2, mask_rows, code, token,
    )
    decoder_input = outs[2].reshape(PATCHES * IMG, DEC)
    return outs[0], outs[1], decoder_input, outs[8:]


def finish_kernel(seq_count, table, vec_ref, dec_in, pgrad_in, *refs):
    parts, refs = refs[: len(table)], refs[len(table) :]
    w2_ref, w1_ref, we_ref, wo_ref, wqkv_ref = refs[:5]
    vecs, (dec_out, pgrad_out, dec, pgrad, in_sem, out_sem) = refs[5:16], refs[16:]
    loads, stores = [], []
    for src, dst, buf, n in ((dec_in, dec_out, dec, 7), (pgrad_in, pgrad_out, pgrad, 2)):
        per = src.shape[0] // n
        for i in range(n):
            rows, at = pl.ds(i * per, per), len(loads)
            loads.append(pltpu.make_async_copy(src.at[rows], buf.at[rows], in_sem.at[at]))
            stores.append(pltpu.make_async_copy(buf.at[rows], dst.at[rows], out_sem.at[at]))
            loads[-1].start()

    def pass_on(count):
        for _ in range(count):
            at = len(stores) - len(loads)
            loads.pop(0).wait()
            stores[at].start()

    def pieces(name):
        chunk, ref = table[name], parts[list(table).index(name)]
        for q in range(chunk.a * chunk.b):
            row, col = (q // chunk.b) * chunk.r + chunk.r0, chunk.c0 + (q % chunk.b) * chunk.cols
            yield row, col, ref[q].astype(F32)

    for name, ref in (("fc2", w2_ref), ("fc1", w1_ref), ("embed", we_ref), ("out", wo_ref)):
        for key in table:
            if key.split("_")[0] == name:
                for row, col, value in pieces(key):
                    rows = min(value.shape[0], ref.shape[0] - row)
                    if rows > 0:
                        ref[row : row + rows, col : col + value.shape[1]] = value[:rows]
    pass_on(7)
    for u in range(UNITS):
        for row, col, value in pieces(f"unit_{u}"):
            rows = min(value.shape[0], wqkv_ref.shape[0] - row)
            if rows > 0:
                for i in range(value.shape[1] // 128):
                    c, within = (col + i * 128) // UNIT, (col + i * 128) % UNIT
                    to = c * D + u * UNIT + within
                    wqkv_ref[row : row + rows, to : to + 128] = value[
                        :rows, i * 128 : (i + 1) * 128
                    ]

    pass_on(2)

    me = lax.axis_index("seq")

    def mine(row, size, first):
        shift = lax.rem(D - first, D)
        return pltpu.roll(vec_ref[row : row + 8], shift, 1)[:, :size]

    size = D // seq_count
    rows = mine(0, size, me * size)
    for i in range(8):
        vecs[i][...] = rows[i]
    per = seq_count // 4
    chosen = mine(8, FF // seq_count, lax.rem(me, per) * (FF // seq_count))
    at = lax.broadcasted_iota(jnp.int32, chosen.shape, 0)
    vecs[8][...] = jnp.sum(jnp.where(at == me // per, chosen, 0.0), axis=0)
    dec_rows = mine(8, DEC // seq_count, me * (DEC // seq_count))
    vecs[9][...] = dec_rows[4]
    vecs[10][...] = dec_rows[5]
    for store in stores:
        store.wait()


def finish(seq_count, vec, dec, pgrad, parts, table):
    def share(*dims):
        return jax.ShapeDtypeStruct((dims[0] // seq_count, *dims[1:]), F32)

    out_shape = [share(FF, D), share(D, FF), share(D, DEC), share(D, D), share(D, 3 * D)]
    out_shape += [share(D)] * 8 + [share(FF), share(DEC), share(DEC)]
    out_shape += [jax.ShapeDtypeStruct(v.shape, v.dtype) for v in (dec, pgrad)]
    anywhere = pl.BlockSpec(memory_space=pl.ANY)
    vmem = pl.BlockSpec(memory_space=pltpu.VMEM)
    return pl.pallas_call(
        functools.partial(finish_kernel, seq_count, table),
        in_specs=[vmem, anywhere, anywhere] + [vmem] * len(parts),
        out_specs=[vmem] * 16 + [anywhere] * 2,
        out_shape=out_shape,
        scratch_shapes=[
            pltpu.VMEM(dec.shape, BF),
            pltpu.VMEM(pgrad.shape, BF),
            pltpu.SemaphoreType.DMA((9,)),
            pltpu.SemaphoreType.DMA((9,)),
        ],
        compiler_params=params(),
        name="finish",
    )(vec, dec, pgrad, *parts)


def decoder_codes(keep_index, slots):
    seq_count = lax.axis_size("seq")
    dev_blocks, _, padded = owner_blocks(seq_count)
    t = jnp.arange(seq_count, dtype=jnp.int32)
    start = first_block(seq_count, t)
    lowest = (lax.axis_index("seq") * PATCHES + start) // seq_count
    m = jnp.arange(padded, dtype=jnp.int32)[:, None]
    image = jnp.arange(seq_count * IMG, dtype=jnp.int32)
    lowest_of, start_of = (jnp.repeat(v, IMG)[None, :] for v in (lowest, start))
    place_at = lowest_of + m
    kept = keep_index.T[:, None, :]
    below = (kept < place_at[None]) & (kept >= lowest_of[None])
    found = jnp.sum(jnp.where(kept == place_at[None], 64, below.astype(jnp.int32)), axis=0)
    code = jnp.where(found >= 64, (found - 64) * IMG + image[None, :] % IMG, slots * IMG)
    code = jnp.where(start_of + m * seq_count < dev_blocks, code, -1)
    return code.reshape(padded, seq_count, IMG).transpose(1, 0, 2).reshape(seq_count, 1, -1)


def image_codes(keep_index, slots):
    seq_count = lax.axis_size("seq")
    group_imgs = keep_index.shape[0]
    at = lax.axis_index("seq") * IMG
    own = lax.dynamic_slice_in_dim(keep_index, at, IMG, 0)
    image = jnp.arange(IMG, dtype=jnp.int32)[:, None]
    owner = (own * group_imgs + at + image) // (IMG * PATCHES)
    lower = jnp.sum((owner[:, None, :] < owner[:, :, None]).astype(jnp.int32), axis=2)
    rank = jnp.arange(KEEP, dtype=jnp.int32)[None, :] - lower
    code = (owner * slots + rank) * HALF + image % HALF
    return code.reshape(2, 1, HROWS)


def local(
    patches,
    keep_index,
    ln1_gain,
    ln1_shift,
    w_qkv,
    q_bias,
    v_bias,
    w_out,
    out_bias,
    ln2_gain,
    ln2_shift,
    w_fc1,
    fc1_bias,
    w_fc2,
    fc2_bias,
    w_embed,
    embed_bias,
    mask_token,
    decoder_grad,
):
    seq_count = lax.axis_size("seq")
    slots = 2 * KEEP // seq_count
    dec_code = decoder_codes(keep_index, slots)
    img_code = image_codes(keep_index, slots)
    (
        mask_rows, _, qkvp, attended, hidden, active, slope, block_in, send, second, first, embed_grad,
    ) = forward(
        decoder_grad, patches, w_qkv, w_out, w_fc1, w_fc2, w_embed, dec_code, img_code, ln1_gain, ln1_shift,
        q_bias, v_bias, out_bias, ln2_gain, ln2_shift, fc1_bias.reshape(1, FF), fc2_bias, embed_bias,
    )
    patches_grad, vec, decoder_input, parts = backward_and_sums(
        embed_grad, block_in, hidden, active, slope, w_embed, w_fc2, w_fc1, attended, qkvp, patches, w_out, w_qkv,
        second, first, send, ln1_gain, ln2_gain, mask_rows, dec_code, mask_token,
    )
    table = chunk_table(lax.axis_size("dp"), seq_count)
    (
        w2g, w1g, weg, woutg, wqkvg, ln1g, ln1s, qb, vb, obias, ln2g, ln2s, b2, b1, ebias, mask_grad,
        decoder_input, patches_grad,
    ) = finish(seq_count, vec, decoder_input, patches_grad, parts, table)
    return (
        decoder_input,
        patches_grad,
        ln1g,
        ln1s,
        wqkvg,
        qb,
        vb,
        woutg,
        obias,
        ln2g,
        ln2s,
        w1g,
        b1,
        w2g,
        b2,
        weg,
        ebias,
        mask_grad,
    )


def solution(mesh):
    rows = P(("dp", "seq"), None)
    placed = (rows, P("dp", None)) + (P(),) * 16 + (rows,)
    vec, mat = P("seq"), P("seq", None)
    return jax.shard_map(
        local,
        mesh=mesh,
        in_specs=placed,
        out_specs=(
            rows, rows, vec, vec, mat, vec, vec, mat, vec, vec, vec, mat, vec, mat, vec, mat, vec, vec,
        ),
        check_vma=False,
    )
```
